32 devices in a mesh: row: 8 (over z, x), col: 1, seq: 4 (over y, core).
Axes of the slice: x: 2, y: 2, z: 4, core: 2. Of those that a mesh axis runs over, the one named last changes fastest.
Arguments:
- pair: bfloat16 [256, 256, 128], P(('row', 'seq'), 'col'), may hold values from -6 to 6
- alignment: bfloat16 [128, 256, 256], P(('row', 'seq'), 'col'), may hold values from -6 to 6
- opm_left: bfloat16 [256, 32], replicated, may hold values from -0.375 to 0.375
- opm_right: bfloat16 [256, 32], replicated, may hold values from -0.375 to 0.375
- opm_out: bfloat16 [1024, 128], replicated, may hold values from -2 to 2
- tri_left: bfloat16 [128, 128], replicated, may hold values from -0.5 to 0.5
- tri_left_gate: bfloat16 [128, 128], replicated, may hold values from -0.5 to 0.5
- tri_right: bfloat16 [128, 128], replicated, may hold values from -0.5 to 0.5
- tri_right_gate: bfloat16 [128, 128], replicated, may hold values from -0.5 to 0.5
- tri_gate: bfloat16 [128, 128], replicated, may hold values from -0.5 to 0.5
- tri_out: bfloat16 [128, 128], replicated, may hold values from -0.5 to 0.5
Outputs:
- pair_out: bfloat16 [256, 256, 128], P(('row', 'seq'), 'col')
The draws below stay inside these ranges and needn't reach their ends.
All inputs are finite; a program needn't handle non-finite values.
Results may differ from the reference program's by a relative error of at most 0.0075.
Values may be sent and summed in bfloat16 or wider, within the bound.
No kernel may reach another device: no remote copies, remote signals or barrier semaphores. Data moves between devices by JAX's collectives and lax.ppermute only.
A program may use at most 64 MiB of HBM per device.

```python
import jax
import jax.numpy as jnp
from jax import lax

CZ = 128
CM = 256
CO = 32
CH = 128
SEQS = 128
NRES = 256


def level_of(stream_key, dims, split, least, high):
    factor_of = 1.0
    for dim, blocks in split:
        steps = jax.random.uniform(jax.random.fold_in(jax.random.fold_in(stream_key, 6), dim), (blocks,), jnp.float32, least / len(split), high / len(split))
        factor_of = factor_of * jnp.repeat(jnp.exp(steps), dims[dim] // blocks).reshape((-1,) + (1,) * (len(dims) - 1 - dim))
    return factor_of


def bell_draw(rng, dims, width, limit, shards=(), held_as=jnp.bfloat16):
    loudness = level_of(rng, dims, shards, -0.22, 0.18) if shards else 1.0
    drawn = jax.random.normal(rng, dims, jnp.float32) * width * loudness
    return jnp.minimum(jnp.maximum(drawn, -limit), limit).astype(held_as)


def setup_inputs(seed: int = 0) -> dict:
    key_list = jax.random.split(jax.random.key(seed), 12)
    pair = bell_draw(key_list[0], (NRES, NRES, CZ), 1.0, 6.0, ((0, 32),))
    alignment = bell_draw(key_list[1], (SEQS, NRES, CM), 1.0, 6.0, ((0, 32),))
    opm_left = bell_draw(key_list[2], (CM, CO), CM ** -0.5, 0.375)
    opm_right = bell_draw(key_list[3], (CM, CO), CM ** -0.5, 0.375)
    opm_out = bell_draw(key_list[4], (CO * CO, CZ), 0.35, 2.0)
    tri_left = bell_draw(key_list[5], (CZ, CH), CZ ** -0.5, 0.5)
    tri_left_gate = bell_draw(key_list[6], (CZ, CH), CZ ** -0.5, 0.5)
    tri_right = bell_draw(key_list[7], (CZ, CH), CZ ** -0.5, 0.5)
    tri_right_gate = bell_draw(key_list[8], (CZ, CH), CZ ** -0.5, 0.5)
    tri_gate = bell_draw(key_list[9], (CZ, CZ), CZ ** -0.5, 0.5)
    tri_out = bell_draw(key_list[10], (CH, CZ), CH ** -0.5, 0.5)
    return dict(pair=pair, alignment=alignment, opm_left=opm_left, opm_right=opm_right, opm_out=opm_out, tri_left=tri_left, tri_left_gate=tri_left_gate, tri_right=tri_right, tri_right_gate=tri_right_gate, tri_gate=tri_gate, tri_out=tri_out)


EPS = 1e-05

def layer_norm(values, axis):
    values = values.astype(jnp.float32)
    center = values - lax.optimization_barrier(jnp.mean(values, axis=axis, keepdims=True))
    spread = lax.optimization_barrier(jnp.mean(center * center, axis=axis, keepdims=True))
    return center * lax.rsqrt(spread + EPS)

def reference(pair, alignment, opm_left, opm_right, opm_out, tri_left, tri_left_gate, tri_right, tri_right_gate, tri_gate, tri_out):
    seq_normed = layer_norm(alignment, 2).astype(jnp.bfloat16).reshape(SEQS * NRES, CM)
    left_factor = jnp.dot(seq_normed, opm_left, preferred_element_type=jnp.float32).astype(jnp.bfloat16).reshape(SEQS, NRES, CO)
    right_factor = jnp.dot(seq_normed, opm_right, preferred_element_type=jnp.float32).astype(jnp.bfloat16).reshape(SEQS, NRES, CO)
    right_wide = right_factor.astype(jnp.float32)

    def outer_row(packed):
        row_vals, pair_row = packed
        outer_sum = jnp.einsum('np,njq->jpq', row_vals.astype(jnp.float32), right_wide)
        mean_outer = (outer_sum * (1.0 / SEQS)).astype(jnp.bfloat16).reshape(NRES, CO * CO)
        return (pair_row.astype(jnp.float32) + jnp.dot(mean_outer, opm_out, preferred_element_type=jnp.float32)).astype(jnp.bfloat16)
    pair_mid = lax.map(outer_row, (jnp.swapaxes(left_factor, 0, 1), pair))
    normed_pair = layer_norm(pair_mid, 2).astype(jnp.bfloat16)
    flat_pair = normed_pair.reshape(NRES * NRES, CZ)

    def gated(weight_gate, weight_value):
        gate_part = jax.nn.sigmoid(jnp.dot(flat_pair, weight_gate, preferred_element_type=jnp.float32))
        value_part = jnp.dot(flat_pair, weight_value, preferred_element_type=jnp.float32)
        return (gate_part * value_part).astype(jnp.bfloat16).reshape(NRES, NRES, CH)
    left_tri = jnp.transpose(gated(tri_left_gate, tri_left), (2, 0, 1))
    right_tri = jnp.transpose(gated(tri_right_gate, tri_right), (2, 0, 1))

    def channel(packed):
        left_chan, right_chan = packed
        return jnp.dot(left_chan, right_chan.T, preferred_element_type=jnp.float32).astype(jnp.bfloat16)
    product = lax.map(channel, (left_tri, right_tri))
    product_last = jnp.transpose(product, (1, 2, 0))

    def finish(packed):
        product_row, normed_row, pair_row = packed
        normed_product = layer_norm(product_row, 1).astype(jnp.bfloat16)
        update = jnp.dot(normed_product, tri_out, preferred_element_type=jnp.float32)
        gate_part = jax.nn.sigmoid(jnp.dot(normed_row, tri_gate, preferred_element_type=jnp.float32))
        return (pair_row.astype(jnp.float32) + gate_part * update).astype(jnp.bfloat16)
    return lax.map(finish, (product_last, normed_pair, pair_mid))
```

```python
import functools

import jax
import jax.numpy as jnp
from jax import lax
from jax.experimental import pallas as pl
from jax.experimental.pallas import tpu as pltpu
from jax.sharding import PartitionSpec as P

EPS = 1e-05
BOTH = ("row", "seq")
BF16 = jnp.bfloat16
F32 = jnp.float32


def spread_2(shard, axis, root):
    mine = lax.axis_index(axis) == root
    return lax.psum(jnp.where(mine, shard, jnp.zeros_like(shard)), axis)


def layer_norm(values, axis):
    values = values.astype(jnp.float32)
    center = values - jnp.mean(values, axis=axis, keepdims=True)
    spread = jnp.mean(center * center, axis=axis, keepdims=True)
    return center * lax.rsqrt(spread + EPS)


def contract(local_rows, piece):
    return jnp.einsum("cik,cjk->cij", local_rows, piece, preferred_element_type=jnp.float32)


def by_groups(
    pair,
    alignment,
    opm_left,
    opm_right,
    opm_out,
    tri_left,
    tri_left_gate,
    tri_right,
    tri_right_gate,
    tri_gate,
    tri_out,
):
    rows_here, cols_here, pair_width = pair.shape
    seq_here = alignment.shape[0]
    model_width = alignment.shape[2]
    factor_width = opm_left.shape[1]
    hidden = tri_left.shape[1]
    n_row = lax.axis_size("row")
    n_col = lax.axis_size("col")
    n_seq = lax.axis_size("seq")
    seq_normed = (
        layer_norm(alignment, 2).astype(jnp.bfloat16).reshape(seq_here * cols_here, model_width)
    )
    left_proj = (
        jnp.dot(seq_normed, opm_left, preferred_element_type=jnp.float32)
        .astype(jnp.bfloat16)
        .reshape(seq_here, cols_here * factor_width)
    )
    right_proj = (
        jnp.dot(seq_normed, opm_right, preferred_element_type=jnp.float32)
        .astype(jnp.bfloat16)
        .reshape(seq_here, cols_here * factor_width)
    )
    per_col = n_row // n_col
    index_row = lax.axis_index("row")
    root_col = index_row // per_col
    right_all = lax.all_gather(right_proj, ("row", "seq"), axis=0, tiled=True)
    left_blocks = left_proj.reshape(seq_here, per_col * n_seq, rows_here * factor_width)
    left_send = jnp.tile(left_blocks, (1, n_col, 1))
    left_recv = lax.all_to_all(left_send, ("row", "seq"), split_axis=1, concat_axis=0, tiled=True)
    row_slice = left_recv.reshape(seq_here * n_row * n_seq, rows_here * factor_width)
    seqs_all = right_all.shape[0]
    row_factors = spread_2(row_slice, "col", root_col)
    right_wide = right_all.reshape(seqs_all, cols_here, factor_width)
    row_stack = jnp.swapaxes(row_factors.reshape(seqs_all, rows_here, factor_width), 0, 1)

    def outer_row(packed):
        row_vals, pair_row = packed
        outer_sum = jnp.einsum(
            "np,njq->jpq", row_vals, right_wide, preferred_element_type=jnp.float32
        )
        mean_outer = (
            (outer_sum * (1.0 / seqs_all))
            .astype(jnp.bfloat16)
            .reshape(cols_here, factor_width * factor_width)
        )
        return (
            pair_row.astype(jnp.float32)
            + jnp.dot(mean_outer, opm_out, preferred_element_type=jnp.float32)
        ).astype(jnp.bfloat16)

    pair_mid = lax.map(outer_row, (row_stack, pair))
    normed_pair = layer_norm(pair_mid, 2).astype(jnp.bfloat16)
    flat_pair = normed_pair.reshape(rows_here * cols_here, pair_width)

    def project(weight):
        return lax.dot_general(
            weight, flat_pair, (((0,), (1,)), ((), ())), preferred_element_type=jnp.float32
        )

    def gated(weight_gate, weight_value):
        gate_part = jax.nn.sigmoid(project(weight_gate))
        return (
            (gate_part * project(weight_value))
            .astype(jnp.bfloat16)
            .reshape(hidden, rows_here, cols_here)
        )

    left_first = gated(tri_left_gate, tri_left)
    right_first = gated(tri_right_gate, tri_right)
    left_local, right_local = (
        lax.all_to_all(
            lax.all_to_all(left_first, "col", split_axis=0, concat_axis=2, tiled=True),
            "seq",
            split_axis=0,
            concat_axis=1,
            tiled=True,
        ),
        lax.all_to_all(
            lax.all_to_all(right_first, "col", split_axis=0, concat_axis=2, tiled=True),
            "seq",
            split_axis=0,
            concat_axis=1,
            tiled=True,
        ),
    )
    product = contract(left_local, lax.all_gather(right_local, "row", axis=1, tiled=True))
    product = product.astype(jnp.bfloat16)
    returned = lax.all_to_all(
        lax.all_to_all(product, "col", split_axis=2, concat_axis=0, tiled=True),
        "seq",
        split_axis=1,
        concat_axis=0,
        tiled=True,
    )
    per_group = hidden // (n_col * n_seq)
    weights_order = (
        tri_out.reshape(n_col, n_seq, per_group, pair_width)
        .transpose(1, 0, 2, 3)
        .reshape(hidden, pair_width)
    )
    normed_product = layer_norm(returned, 0).astype(jnp.bfloat16)
    update = jnp.einsum(
        "cij,cd->ijd", normed_product, weights_order, preferred_element_type=jnp.float32
    )
    gate_part = jax.nn.sigmoid(
        jnp.dot(flat_pair, tri_gate, preferred_element_type=jnp.float32)
    ).reshape(rows_here, cols_here, pair_width)
    return (pair_mid.astype(jnp.float32) + gate_part * update).astype(jnp.bfloat16)


def mul(a, b):
    return jnp.dot(a, b, preferred_element_type=F32)


def mul_t(a, b):
    return lax.dot_general(a, b, (((1,), (1,)), ((), ())), preferred_element_type=F32)


def ones_where(mask):
    return jnp.where(mask, 1.0, 0.0).astype(BF16)


def iotas(rows, cols):
    shape = (rows, cols)
    return lax.broadcasted_iota(jnp.int32, shape, 0), lax.broadcasted_iota(jnp.int32, shape, 1)


def identity(size):
    row, col = iotas(size, size)
    return ones_where(row == col)


def swap_rows(outer, inner):
    row, col = iotas(outer * inner, outer * inner)
    return ones_where(col == (row % outer) * inner + row // outer)


def normalize(values, axis):
    center = values - jnp.mean(values, axis=axis, keepdims=True)
    spread = jnp.mean(center * center, axis=axis, keepdims=True)
    return center * lax.rsqrt(spread + EPS)


def factors_kernel(sizes, align_ref, left_ref, right_ref, *refs):
    n_far, n_near, n_core, rows, _ = sizes
    out_refs, parts = refs[:n_far], refs[n_far]
    seqs, cols, width = align_ref.shape
    factor = left_ref.shape[1]
    chip_rows = n_core * rows
    chips = n_far * n_near
    row, col = iotas(factor, chip_rows * factor)
    left_wide = mul(left_ref[...], ones_where(row == col % factor)).astype(BF16)
    right_t = right_ref[...].astype(F32).T.astype(BF16)
    row, col = iotas(cols, chip_rows * factor)
    own_lane = (row % chip_rows) == (col // factor)
    row, col = iotas(n_far * seqs * n_near, cols)
    chip_of_row = (row // (seqs * n_near)) * n_near + row % n_near
    seq_of_row = (row // n_near) % seqs
    chip_match = chip_of_row == col // chip_rows
    right_rows, left_rows = [], None
    for n in range(seqs):
        normed = normalize(align_ref[n].astype(F32), 1).astype(BF16)
        right_rows.append(mul_t(right_t, normed))
        spread = jnp.where(own_lane, mul(normed, left_wide), 0.0).astype(BF16)
        part = mul(ones_where(chip_match & (seq_of_row == n)), spread)
        left_rows = part if left_rows is None else left_rows + part
    right_block = jnp.concatenate(right_rows, 0).astype(BF16)
    part_rows = seqs * n_near
    pieces = n_core
    for far in range(n_far):
        for piece in range(pieces):
            parts[far, piece * part_rows : (piece + 1) * part_rows, :] = left_rows[
                far * part_rows : (far + 1) * part_rows, piece * cols : (piece + 1) * cols
            ].astype(BF16)
    here = lax.axis_index("row") // 2
    for k in range(n_far):
        out_refs[k][: seqs * factor, :] = right_block
        out_refs[k][seqs * factor :, :] = parts[here ^ k]


def regroup_kernel(sizes, factor, seqs, *refs):
    n_far, n_near, n_core, _, _ = sizes
    in_refs, out_refs, parts = refs[:n_far], refs[n_far : n_far + n_near], refs[-1]
    held = n_far * seqs
    half = 256 // held
    shuffle = swap_rows(held, half)
    for h in range(factor // half):
        block = jnp.concatenate(
            [
                ref[n * factor + h * half : n * factor + (h + 1) * half, :]
                for ref in in_refs
                for n in range(seqs)
            ],
            0,
        )
        block = mul(shuffle, block).astype(BF16)
        for ref in out_refs:
            ref[h * half * held : (h + 1) * half * held, :] = block
    part_rows = seqs * n_near
    base = seqs * factor
    pick = swap_rows(held, n_near)
    for piece in range(n_core):
        block = jnp.concatenate(
            [ref[base + piece * part_rows : base + (piece + 1) * part_rows, :] for ref in in_refs], 0
        )
        block = mul(pick, block).astype(BF16)
        for near in range(n_near):
            parts[near, piece * held : (piece + 1) * held, :] = block[
                near * held : (near + 1) * held
            ]
    n_y = n_near // 2
    here = (lax.axis_index("row") % 2) * n_y + lax.axis_index("seq") // n_core
    for k in range(n_near):
        out_refs[k][factor * held :, :] = parts[here ^ k]


def pair_kernel(sizes, held, scale, *refs):
    n_core, rows, n_dev = sizes[2], sizes[3], sizes[4]
    groups = refs[:-8]
    pair_ref, out_w, tri_w, send_ref, mid_ref, norm_ref, outer, both = refs[-8:]
    _, cols, width = pair_ref.shape
    factor_sq = out_w.shape[1]
    factor = groups[0].shape[0] // held - n_core
    hidden = tri_w.shape[0] // 4
    core = lax.axis_index("seq") % n_core
    at = pl.multiple_of((factor + core) * held, held)
    left = jnp.concatenate([ref[pl.ds(at, held), :] for ref in groups], 0)
    left_t = mul_t(identity(rows * factor), left).astype(BF16)
    for q in range(factor):
        right = jnp.concatenate([ref[q * held : (q + 1) * held, :] for ref in groups], 0)
        block = mul(left_t, right).astype(BF16)
        for i in range(rows):
            outer[i, q * factor : (q + 1) * factor, :] = block[i * factor : (i + 1) * factor]
    eye = identity(width)
    for i in range(rows):
        update = mul(out_w[...], outer[i])
        mid = (mul_t(eye, pair_ref[i]) + update * scale).astype(BF16)
        mid_ref[i] = mid
        normed = normalize(mid.astype(F32), 0).astype(BF16)
        norm_ref[i] = normed
        for side in range(2):
            at = 2 * side * hidden
            gate = jax.nn.sigmoid(mul(tri_w[at : at + hidden, :], normed))
            value = mul(tri_w[at + hidden : at + 2 * hidden, :], normed)
            both[side, i] = (gate * value).astype(BF16)
    per = hidden // n_dev
    some = 256 // rows
    shuffle = swap_rows(rows, some)
    chunk = per * rows
    for side in range(2):
        for b in range(hidden // some):
            block = jnp.concatenate(
                [both[side, i, b * some : (b + 1) * some, :] for i in range(rows)], 0
            )
            block = mul(shuffle, block).astype(BF16)
            for d in range(some // per):
                to = ((b * some // per + d) * 2 + side) * chunk
                send_ref[to : to + chunk, :] = block[d * chunk : (d + 1) * chunk]


def product_kernel(sizes, per, recv_ref, send_ref, factors, total):
    rows, n_dev = sizes[3], sizes[4]
    chunk = per * rows
    for src in range(n_dev):
        for side in range(2):
            at = (src * 2 + side) * chunk
            block = recv_ref[at : at + chunk, :].astype(F32)
            for c in range(per):
                factors[side, c, src * rows : (src + 1) * rows, :] = block[c * rows : (c + 1) * rows]
    for c in range(per):
        prod = mul_t(factors[0, c].astype(BF16), factors[1, c].astype(BF16))
        for dst in range(n_dev):
            total[dst, c * rows : (c + 1) * rows, :] = prod[dst * rows : (dst + 1) * rows]
    for dst in range(n_dev):
        send_ref[dst * chunk : (dst + 1) * chunk, :] = total[dst].astype(BF16)


def finish_kernel(sizes, recv_ref, mid_ref, norm_ref, gate_w, out_w, out_ref, apart):
    rows = sizes[3]
    _, width, cols = mid_ref.shape
    hidden = out_w.shape[1]
    some = 256 // rows
    blocks = hidden // some
    count = some * rows

    def piece(b):
        return recv_ref[b * count : (b + 1) * count, :].astype(F32).reshape(some, rows, cols)

    mean = sum(jnp.sum(piece(b), 0) for b in range(blocks)) * (1.0 / hidden)
    spread = sum(jnp.sum((piece(b) - mean) ** 2, 0) for b in range(blocks)) * (1.0 / hidden)
    factor = lax.rsqrt(spread + EPS)
    shuffle = swap_rows(some, rows)
    for b in range(blocks):
        normed = ((piece(b) - mean) * factor).reshape(count, cols).astype(BF16)
        normed = mul(shuffle, normed).astype(BF16)
        for i in range(rows):
            apart[i, b * some : (b + 1) * some, :] = normed[i * some : (i + 1) * some]
    eye = identity(cols)
    for i in range(rows):
        update = mul(out_w[...], apart[i])
        gate = jax.nn.sigmoid(mul(gate_w[...], norm_ref[i]))
        done = (mid_ref[i].astype(F32) + gate * update).astype(BF16)
        out_ref[i] = mul_t(eye, done).astype(BF16)


def call(kernel, out_shape, scratch, flops, *args):
    out_shape = [jax.ShapeDtypeStruct(s, BF16) for s in out_shape]
    moved = sum(a.size * 2 for a in (*args, *out_shape))
    return pl.pallas_call(
        kernel,
        out_shape=out_shape,
        in_specs=[pl.BlockSpec(memory_space=pltpu.VMEM)] * len(args),
        out_specs=[pl.BlockSpec(memory_space=pltpu.VMEM)] * len(out_shape),
        scratch_shapes=scratch,
        compiler_params=pltpu.CompilerParams(vmem_limit_bytes=40 * 2**20),
        cost_estimate=pl.CostEstimate(flops=flops, bytes_accessed=moved, transcendentals=0),
    )(*args)


def whole_channels(
    pair,
    alignment,
    opm_left,
    opm_right,
    opm_out,
    tri_left,
    tri_left_gate,
    tri_right,
    tri_right_gate,
    tri_gate,
    tri_out,
):
    rows, cols, width = pair.shape
    seqs = alignment.shape[0]
    factor = opm_left.shape[1]
    hidden = tri_left.shape[1]
    n_row, n_seq = lax.axis_size("row"), lax.axis_size("seq")
    n_dev = n_row * n_seq
    n_core = 2
    n_far, n_near = n_row // 2, 2 * (n_seq // n_core)
    n_y = n_near // 2
    sizes = (n_far, n_near, n_core, rows, n_dev)
    held = n_far * seqs
    per = hidden // n_dev

    def exchange(value, row_bits, seq_bits):
        pairs = [
            (r * n_seq + s, (r ^ row_bits) * n_seq + (s ^ seq_bits))
            for r in range(n_row)
            for s in range(n_seq)
        ]
        return lax.ppermute(value, BOTH, pairs)

    out_wt = jnp.transpose(opm_out.reshape(factor, factor, width), (2, 1, 0))
    out_wt = out_wt.reshape(width, factor * factor)
    tri_wt = jnp.concatenate([w.T for w in (tri_left_gate, tri_left, tri_right_gate, tri_right)], 0)

    message = (seqs * factor + n_core * seqs * n_near, cols)
    mine = call(
        functools.partial(factors_kernel, sizes),
        [message] * n_far,
        [pltpu.VMEM((n_far, n_core * seqs * n_near, cols), BF16)],
        4 * seqs * cols * alignment.shape[2] * factor,
        alignment,
        opm_left,
        opm_right,
    )
    far = [mine[0]] + [exchange(mine[k], 2 * k, 0) for k in range(1, n_far)]
    message = ((factor + n_core) * held, cols)
    mine = call(
        functools.partial(regroup_kernel, sizes, factor, seqs),
        [message] * n_near,
        [pltpu.VMEM((n_near, n_core * held, cols), BF16)],
        2 * 256 * factor * held * cols,
        *far,
    )
    near = [mine[0]] + [
        exchange(mine[k], k // n_y, (k % n_y) * n_core) for k in range(1, n_near)
    ]
    groups = near + [exchange(block, 0, 1) for block in near]
    scale = 1.0 / (held * n_near * n_core)
    send, mid, normed = call(
        functools.partial(pair_kernel, sizes, held, scale),
        [(2 * hidden * rows, cols), (rows, width, cols), (rows, width, cols)],
        [
            pltpu.VMEM((rows, factor * factor, cols), BF16),
            pltpu.VMEM((2, rows, hidden, cols), BF16),
        ],
        4 * rows * cols * width * (factor * factor + hidden * 2),
        *groups,
        pair,
        out_wt,
        tri_wt,
    )
    recv = lax.all_to_all(send, BOTH, split_axis=0, concat_axis=0, tiled=True)
    (send,) = call(
        functools.partial(product_kernel, sizes, per),
        [(hidden * rows, cols)],
        [
            pltpu.VMEM((2, per, rows * n_dev, cols), F32),
            pltpu.VMEM((n_dev, per * rows, cols), F32),
        ],
        2 * per * cols * cols * cols,
        recv,
    )
    recv = lax.all_to_all(send, BOTH, split_axis=0, concat_axis=0, tiled=True)
    (out,) = call(
        functools.partial(finish_kernel, sizes),
        [(rows, cols, width)],
        [pltpu.VMEM((rows, hidden, cols), BF16)],
        4 * rows * cols * width * hidden,
        recv,
        mid,
        normed,
        tri_gate.T,
        tri_out.T,
    )
    return out


def power_of_two(n):
    return n & (n - 1) == 0


def on_device(pair, alignment, opm_left, *rest):
    rows, cols, _ = pair.shape
    factor, hidden = opm_left.shape[1], rest[2].shape[1]
    n_row, n_col, n_seq = (lax.axis_size(a) for a in ("row", "col", "seq"))
    n_dev = n_row * n_seq
    held = n_row // 2 * alignment.shape[0]
    fits = (
        n_col == 1
        and power_of_two(n_row)
        and power_of_two(n_seq)
        and power_of_two(rows)
        and n_row >= 4
        and n_seq >= 4
        and hidden % n_dev == 0
        and rows % 8 == 0
        and (hidden // n_dev * rows) % 16 == 0
        and cols % 256 == 0
        and rows * factor == cols
        and rows * n_dev == cols
        and held % 16 == 0
        and 256 % held == 0
        and factor % (256 // held) == 0
        and hidden % (256 // rows) == 0
        and power_of_two(held * n_seq * 2)
    )
    plan = whole_channels if fits else by_groups
    return plan(pair, alignment, opm_left, *rest)


def solution(mesh):
    return jax.shard_map(
        on_device,
        mesh=mesh,
        in_specs=(
            P(("row", "seq"), "col", None),
            P(("row", "seq"), "col", None),
            P(),
            P(),
            P(),
            P(),
            P(),
            P(),
            P(),
            P(),
            P(),
        ),
        out_specs=P(("row", "seq"), "col", None),
        check_vma=False,
    )
```

```python
import functools
import math

import jax
import jax.numpy as jnp
from jax import lax
from jax.experimental import pallas as pl
from jax.experimental.pallas import tpu as pltpu
from jax.sharding import PartitionSpec as P

EPS = 1e-05
BOTH = ("row", "seq")
BF16 = jnp.bfloat16
F32 = jnp.float32


def spread_2(shard, axis, root):
    mine = lax.axis_index(axis) == root
    return lax.psum(jnp.where(mine, shard, jnp.zeros_like(shard)), axis)


def layer_norm(values, axis):
    values = values.astype(jnp.float32)
    center = values - jnp.mean(values, axis=axis, keepdims=True)
    spread = jnp.mean(center * center, axis=axis, keepdims=True)
    return center * lax.rsqrt(spread + EPS)


def contract(local_rows, piece):
    return jnp.einsum("cik,cjk->cij", local_rows, piece, preferred_element_type=jnp.float32)


def by_groups(
    pair,
    alignment,
    opm_left,
    opm_right,
    opm_out,
    tri_left,
    tri_left_gate,
    tri_right,
    tri_right_gate,
    tri_gate,
    tri_out,
):
    rows_here, cols_here, pair_width = pair.shape
    seq_here = alignment.shape[0]
    model_width = alignment.shape[2]
    factor_width = opm_left.shape[1]
    hidden = tri_left.shape[1]
    n_row = lax.axis_size("row")
    n_col = lax.axis_size("col")
    n_seq = lax.axis_size("seq")
    seq_normed = (
        layer_norm(alignment, 2).astype(jnp.bfloat16).reshape(seq_here * cols_here, model_width)
    )
    left_proj = (
        jnp.dot(seq_normed, opm_left, preferred_element_type=jnp.float32)
        .astype(jnp.bfloat16)
        .reshape(seq_here, cols_here * factor_width)
    )
    right_proj = (
        jnp.dot(seq_normed, opm_right, preferred_element_type=jnp.float32)
        .astype(jnp.bfloat16)
        .reshape(seq_here, cols_here * factor_width)
    )
    per_col = n_row // n_col
    index_row = lax.axis_index("row")
    root_col = index_row // per_col
    right_all = lax.all_gather(right_proj, ("row", "seq"), axis=0, tiled=True)
    left_blocks = left_proj.reshape(seq_here, per_col * n_seq, rows_here * factor_width)
    left_send = jnp.tile(left_blocks, (1, n_col, 1))
    left_recv = lax.all_to_all(left_send, ("row", "seq"), split_axis=1, concat_axis=0, tiled=True)
    row_slice = left_recv.reshape(seq_here * n_row * n_seq, rows_here * factor_width)
    seqs_all = right_all.shape[0]
    row_factors = spread_2(row_slice, "col", root_col)
    right_wide = right_all.reshape(seqs_all, cols_here, factor_width)
    row_stack = jnp.swapaxes(row_factors.reshape(seqs_all, rows_here, factor_width), 0, 1)

    def outer_row(packed):
        row_vals, pair_row = packed
        outer_sum = jnp.einsum(
            "np,njq->jpq", row_vals, right_wide, preferred_element_type=jnp.float32
        )
        mean_outer = (
            (outer_sum * (1.0 / seqs_all))
            .astype(jnp.bfloat16)
            .reshape(cols_here, factor_width * factor_width)
        )
        return (
            pair_row.astype(jnp.float32)
            + jnp.dot(mean_outer, opm_out, preferred_element_type=jnp.float32)
        ).astype(jnp.bfloat16)

    pair_mid = lax.map(outer_row, (row_stack, pair))
    normed_pair = layer_norm(pair_mid, 2).astype(jnp.bfloat16)
    flat_pair = normed_pair.reshape(rows_here * cols_here, pair_width)

    def project(weight):
        return lax.dot_general(
            weight, flat_pair, (((0,), (1,)), ((), ())), preferred_element_type=jnp.float32
        )

    def gated(weight_gate, weight_value):
        gate_part = jax.nn.sigmoid(project(weight_gate))
        return (
            (gate_part * project(weight_value))
            .astype(jnp.bfloat16)
            .reshape(hidden, rows_here, cols_here)
        )

    left_first = gated(tri_left_gate, tri_left)
    right_first = gated(tri_right_gate, tri_right)
    left_local, right_local = (
        lax.all_to_all(
            lax.all_to_all(left_first, "col", split_axis=0, concat_axis=2, tiled=True),
            "seq",
            split_axis=0,
            concat_axis=1,
            tiled=True,
        ),
        lax.all_to_all(
            lax.all_to_all(right_first, "col", split_axis=0, concat_axis=2, tiled=True),
            "seq",
            split_axis=0,
            concat_axis=1,
            tiled=True,
        ),
    )
    product = contract(left_local, lax.all_gather(right_local, "row", axis=1, tiled=True))
    product = product.astype(jnp.bfloat16)
    returned = lax.all_to_all(
        lax.all_to_all(product, "col", split_axis=2, concat_axis=0, tiled=True),
        "seq",
        split_axis=1,
        concat_axis=0,
        tiled=True,
    )
    per_group = hidden // (n_col * n_seq)
    weights_order = (
        tri_out.reshape(n_col, n_seq, per_group, pair_width)
        .transpose(1, 0, 2, 3)
        .reshape(hidden, pair_width)
    )
    normed_product = layer_norm(returned, 0).astype(jnp.bfloat16)
    update = jnp.einsum(
        "cij,cd->ijd", normed_product, weights_order, preferred_element_type=jnp.float32
    )
    gate_part = jax.nn.sigmoid(
        jnp.dot(flat_pair, tri_gate, preferred_element_type=jnp.float32)
    ).reshape(rows_here, cols_here, pair_width)
    return (pair_mid.astype(jnp.float32) + gate_part * update).astype(jnp.bfloat16)


def mul(a, b):
    return jnp.dot(a, b, preferred_element_type=F32)


def mul_t(a, b):
    return lax.dot_general(a, b, (((1,), (1,)), ((), ())), preferred_element_type=F32)


def ones_where(mask):
    return jnp.where(mask, 1.0, 0.0).astype(BF16)


def iotas(rows, cols):
    shape = (rows, cols)
    return lax.broadcasted_iota(jnp.int32, shape, 0), lax.broadcasted_iota(jnp.int32, shape, 1)


def identity(size):
    row, col = iotas(size, size)
    return ones_where(row == col)


def swap_rows(outer, inner):
    row, col = iotas(outer * inner, outer * inner)
    return ones_where(col == (row % outer) * inner + row // outer)


def normalize(values, axis):
    center = values - jnp.mean(values, axis=axis, keepdims=True)
    spread = jnp.mean(center * center, axis=axis, keepdims=True)
    return center * lax.rsqrt(spread + EPS)


def fetch(sems, pairs):
    copies = [
        pltpu.make_async_copy(source, target, sems.at[k]) for k, (source, target) in enumerate(pairs)
    ]
    for copy in copies:
        copy.start()
    return copies


def factors_kernel(sizes, align_in, left_in, right_in, *refs):
    n_far, n_near, n_core, rows, _ = sizes
    out_refs, (parts, align_ref, left_ref, right_ref, sems) = refs[:n_far], refs[n_far:]
    pairs = [(left_in, left_ref), (right_in, right_ref)]
    pairs += [(align_in.at[n], align_ref.at[n]) for n in range(align_in.shape[0])]
    copies = fetch(sems, pairs)
    copies[0].wait()
    copies[1].wait()
    seqs, cols, width = align_ref.shape
    factor = left_ref.shape[0]
    chip_rows = n_core * rows
    chips = n_far * n_near
    row, col = iotas(chip_rows * factor, factor)
    left_wide = mul(ones_where(row % factor == col), left_ref[...]).astype(BF16)
    row, col = iotas(cols, chip_rows * factor)
    own_lane = (row % chip_rows) == (col // factor)
    row, col = iotas(n_far * seqs * n_near, cols)
    chip_of_row = (row // (seqs * n_near)) * n_near + row % n_near
    seq_of_row = (row // n_near) % seqs
    chip_match = chip_of_row == col // chip_rows
    right_rows, left_rows = [], None
    for n in range(seqs):
        copies[2 + n].wait()
        normed = normalize(align_ref[n].astype(F32), 1).astype(BF16)
        right_rows.append(mul_t(right_ref[...], normed))
        spread = jnp.where(own_lane, mul_t(normed, left_wide), 0.0).astype(BF16)
        part = mul(ones_where(chip_match & (seq_of_row == n)), spread)
        left_rows = part if left_rows is None else left_rows + part
    right_block = jnp.concatenate(right_rows, 0).astype(BF16)
    part_rows = seqs * n_near
    pieces = n_core
    for far in range(n_far):
        for piece in range(pieces):
            parts[far, piece * part_rows : (piece + 1) * part_rows, :] = left_rows[
                far * part_rows : (far + 1) * part_rows, piece * cols : (piece + 1) * cols
            ].astype(BF16)
    here = lax.axis_index("row") // 2
    for k in range(n_far):
        out_refs[k][: seqs * factor, :] = right_block
        out_refs[k][seqs * factor :, :] = parts[here ^ k]


def regroup_kernel(sizes, factor, seqs, *refs):
    n_far, n_near, n_core, _, _ = sizes
    in_refs, out_refs, parts = refs[:n_far], refs[n_far : n_far + n_near], refs[-1]
    held = n_far * seqs
    half = 256 // held
    shuffle = swap_rows(held, half)
    for h in range(factor // half):
        block = jnp.concatenate(
            [
                ref[n * factor + h * half : n * factor + (h + 1) * half, :]
                for ref in in_refs
                for n in range(seqs)
            ],
            0,
        )
        block = mul(shuffle, block).astype(BF16)
        for ref in out_refs:
            ref[h * half * held : (h + 1) * half * held, :] = block
    part_rows = seqs * n_near
    base = seqs * factor
    pick = swap_rows(held, n_near)
    for piece in range(n_core):
        block = jnp.concatenate(
            [ref[base + piece * part_rows : base + (piece + 1) * part_rows, :] for ref in in_refs], 0
        )
        block = mul(pick, block).astype(BF16)
        for near in range(n_near):
            parts[near, piece * held : (piece + 1) * held, :] = block[
                near * held : (near + 1) * held
            ]
    n_y = n_near // 2
    here = (lax.axis_index("row") % 2) * n_y + lax.axis_index("seq") // n_core
    for k in range(n_near):
        out_refs[k][factor * held :, :] = parts[here ^ k]


def prepare_kernel(factor, *refs):
    n = (len(refs) - 6) // 2
    sources, (pair_t, out_t, tri_t, gate_t, final_t), targets = refs[:n], refs[n : n + 5], refs[n + 5 : -1]
    copies = fetch(refs[-1], list(zip(sources, targets, strict=True)))
    pair_ref, out_w, *tri, gate_w, final_w = targets
    eye = identity(pair_ref.shape[2])
    for copy in copies:
        copy.wait()
    for i in range(pair_ref.shape[0]):
        pair_t[i] = mul_t(eye, pair_ref[i]).astype(BF16)
    shuffle = swap_rows(256 // 16, 16)
    for q in range(0, factor, 16):
        for p in range(0, factor, 256 // 16):
            block = jnp.concatenate(
                [
                    out_w[(p + k) * factor + q : (p + k) * factor + q + 16, :]
                    for k in range(256 // 16)
                ],
                0,
            )
            block = mul(shuffle, block).astype(BF16)
            block = mul_t(eye, block).astype(BF16)
            at = (q // 16 * (factor // 16) + p // 16) * 256
            out_t[:, at : at + 256] = block
    for k, ref in enumerate(tri):
        width = ref.shape[1]
        tri_t[k * width : (k + 1) * width, :] = mul_t(eye, ref[...]).astype(BF16)
    gate_t[...] = mul_t(eye, gate_w[...]).astype(BF16)
    final_t[...] = mul_t(eye, final_w[...]).astype(BF16)


def gate_kernel(norm_ref, gate_w, gate_ref):
    for i in range(norm_ref.shape[0]):
        gate_ref[i] = jax.nn.sigmoid(mul(gate_w[...], norm_ref[i]))


def pair_kernel(sizes, held, scale, *refs):
    n_core, rows, n_dev = sizes[2], sizes[3], sizes[4]
    groups = refs[:-8]
    pair_ref, out_w, tri_w, send_ref, mid_ref, norm_ref, outer, both = refs[-8:]
    factor = groups[0].shape[0] // held - n_core
    hidden = tri_w.shape[0] // 4
    core = lax.axis_index("seq") % n_core
    at = pl.multiple_of((factor + core) * held, held)
    left = jnp.concatenate([ref[pl.ds(at, held), :] for ref in groups], 0)
    left_t = mul_t(identity(rows * factor), left).astype(BF16)
    for q in range(factor):
        right = jnp.concatenate([ref[q * held : (q + 1) * held, :] for ref in groups], 0)
        block = mul(left_t, right).astype(BF16)
        for i in range(rows):
            for p in range(0, factor, 16):
                at = (q // 16 * (factor // 16) + p // 16) * 256 + q % 16 * 16
                outer[i, at : at + 16, :] = block[i * factor + p : i * factor + p + 16]
    for i in range(rows):
        update = mul(out_w[...], outer[i])
        mid = (pair_ref[i].astype(F32) + update * scale).astype(BF16)
        mid_ref[i] = mid
        normed = normalize(mid.astype(F32), 0).astype(BF16)
        norm_ref[i] = normed
        for side in range(2):
            at = 2 * side * hidden
            gate = jax.nn.sigmoid(mul(tri_w[at : at + hidden, :], normed))
            value = mul(tri_w[at + hidden : at + 2 * hidden, :], normed)
            both[side, i] = (gate * value).astype(BF16)
    per = hidden // n_dev
    some = 256 // rows
    shuffle = swap_rows(rows, some)
    chunk = per * rows
    for side in range(2):
        for b in range(hidden // some):
            block = jnp.concatenate(
                [both[side, i, b * some : (b + 1) * some, :] for i in range(rows)], 0
            )
            block = mul(shuffle, block).astype(BF16)
            for d in range(some // per):
                to = ((b * some // per + d) * 2 + side) * chunk
                send_ref[to : to + chunk, :] = block[d * chunk : (d + 1) * chunk]


def product_kernel(sizes, per, recv_ref, send_ref, factors, total):
    rows, n_dev = sizes[3], sizes[4]
    chunk = per * rows
    for src in range(n_dev):
        for side in range(2):
            at = (src * 2 + side) * chunk
            block = recv_ref[at : at + chunk, :].astype(F32)
            for c in range(per):
                factors[side, c, src * rows : (src + 1) * rows, :] = block[c * rows : (c + 1) * rows]
    for c in range(per):
        prod = mul_t(factors[0, c].astype(BF16), factors[1, c].astype(BF16))
        for dst in range(n_dev):
            total[dst, c * rows : (c + 1) * rows, :] = prod[dst * rows : (dst + 1) * rows]
    for dst in range(n_dev):
        send_ref[dst * chunk : (dst + 1) * chunk, :] = total[dst].astype(BF16)


def finish_kernel(sizes, recv_ref, mid_ref, gate_ref, out_w, out_ref, apart, done_ref, sems):
    rows = sizes[3]
    _, width, cols = mid_ref.shape
    hidden = out_w.shape[1]
    some = 256 // rows
    blocks = hidden // some
    count = some * rows

    def piece(b):
        return recv_ref[b * count : (b + 1) * count, :].astype(F32).reshape(some, rows, cols)

    mean = sum(jnp.sum(piece(b), 0) for b in range(blocks)) * (1.0 / hidden)
    spread = sum(jnp.sum((piece(b) - mean) ** 2, 0) for b in range(blocks)) * (1.0 / hidden)
    factor = lax.rsqrt(spread + EPS)
    shuffle = swap_rows(some, rows)
    for b in range(blocks):
        normed = ((piece(b) - mean) * factor).reshape(count, cols).astype(BF16)
        normed = mul(shuffle, normed).astype(BF16)
        for i in range(rows):
            apart[i, b * some : (b + 1) * some, :] = normed[i * some : (i + 1) * some]
    eye = identity(cols)
    copies = []
    for i in range(rows):
        update = mul(out_w[...], apart[i])
        done = (mid_ref[i].astype(F32) + gate_ref[i] * update).astype(BF16)
        done_ref[i] = mul_t(eye, done).astype(BF16)
        copies.append(pltpu.make_async_copy(done_ref.at[i], out_ref.at[i], sems.at[i]))
        copies[i].start()
    for copy in copies:
        copy.wait()


def call(kernel, out_shape, scratch, grant, flops, *args, far_in=False, far_out=False):
    spaces = [pltpu.HBM if far else pltpu.VMEM for far in (far_in, far_out)]
    place = jax.ShapeDtypeStruct if far_out else pltpu.VMEM
    out_shape = [place(*s) if isinstance(s[0], tuple) else place(s, BF16) for s in out_shape]
    if far_in:
        args = [pltpu.with_memory_space_constraint(a, pltpu.HBM) for a in args]
    moved = sum(math.prod(a.shape) * jnp.dtype(a.dtype).itemsize for a in (*args, *out_shape))
    return pl.pallas_call(
        kernel,
        out_shape=out_shape,
        in_specs=[pl.BlockSpec(memory_space=spaces[0])] * len(args),
        out_specs=[pl.BlockSpec(memory_space=spaces[1])] * len(out_shape),
        scratch_shapes=scratch,
        compiler_params=pltpu.CompilerParams(vmem_limit_bytes=grant * 2**20),
        cost_estimate=pl.CostEstimate(flops=flops, bytes_accessed=moved, transcendentals=0),
    )(*args)


def whole_channels(
    pair,
    alignment,
    opm_left,
    opm_right,
    opm_out,
    tri_left,
    tri_left_gate,
    tri_right,
    tri_right_gate,
    tri_gate,
    tri_out,
):
    rows, cols, width = pair.shape
    seqs = alignment.shape[0]
    factor = opm_left.shape[1]
    hidden = tri_left.shape[1]
    n_row, n_seq = lax.axis_size("row"), lax.axis_size("seq")
    n_dev = n_row * n_seq
    n_core = 2
    n_far, n_near = n_row // 2, 2 * (n_seq // n_core)
    n_y = n_near // 2
    sizes = (n_far, n_near, n_core, rows, n_dev)
    held = n_far * seqs
    per = hidden // n_dev

    def exchange(value, row_bits, seq_bits):
        pairs = [
            (r * n_seq + s, (r ^ row_bits) * n_seq + (s ^ seq_bits))
            for r in range(n_row)
            for s in range(n_seq)
        ]
        return lax.ppermute(value, BOTH, pairs)

    message = (seqs * factor + n_core * seqs * n_near, cols)
    mine = call(
        functools.partial(factors_kernel, sizes),
        [message] * n_far,
        [
            pltpu.VMEM((n_far, n_core * seqs * n_near, cols), BF16),
            pltpu.VMEM(alignment.shape, BF16),
            pltpu.VMEM(opm_left.shape[::-1], BF16),
            pltpu.VMEM(opm_right.shape[::-1], BF16),
            pltpu.SemaphoreType.DMA((2 + seqs,)),
        ],
        8,
        4 * seqs * cols * alignment.shape[2] * factor,
        alignment,
        opm_left.T,
        opm_right.T,
        far_in=True,
    )
    weights = (
        pair,
        opm_out,
        tri_left_gate,
        tri_left,
        tri_right_gate,
        tri_right,
        tri_gate,
        tri_out,
    )
    mine, weights = lax.optimization_barrier((mine, weights))
    far = [mine[0]] + [exchange(mine[k], 2 * k, 0) for k in range(1, n_far)]
    prepared = call(
        functools.partial(prepare_kernel, factor),
        [
            (rows, width, cols),
            (width, factor * factor),
            (4 * hidden, width),
            (width, width),
            (width, hidden),
        ],
        [pltpu.VMEM(w.shape, BF16) for w in weights] + [pltpu.SemaphoreType.DMA((len(weights),))],
        8,
        4 * rows * cols * width * width,
        *weights,
        far_in=True,
    )
    far, prepared = lax.optimization_barrier((far, prepared))
    pair_t, out_t, tri_t, gate_t, final_t = prepared
    message = ((factor + n_core) * held, cols)
    mine = call(
        functools.partial(regroup_kernel, sizes, factor, seqs),
        [message] * n_near,
        [pltpu.VMEM((n_near, n_core * held, cols), BF16)],
        8,
        2 * 256 * factor * held * cols,
        *far,
    )
    near = [mine[0]] + [
        exchange(mine[k], k // n_y, (k % n_y) * n_core) for k in range(1, n_near)
    ]
    groups = near + [exchange(block, 0, 1) for block in near]
    scale = 1.0 / (held * n_near * n_core)
    send, mid, normed = call(
        functools.partial(pair_kernel, sizes, held, scale),
        [(2 * hidden * rows, cols), (rows, width, cols), (rows, width, cols)],
        [
            pltpu.VMEM((rows, factor * factor, cols), BF16),
            pltpu.VMEM((2, rows, hidden, cols), BF16),
        ],
        16,
        4 * rows * cols * width * (factor * factor + hidden * 2),
        *groups,
        pair_t,
        out_t,
        tri_t,
    )
    (gate,) = call(
        gate_kernel,
        [((rows, width, cols), F32)],
        [],
        8,
        2 * rows * cols * width * width,
        normed,
        gate_t,
    )
    recv = lax.all_to_all(send, BOTH, split_axis=0, concat_axis=0, tiled=True)
    (send,) = call(
        functools.partial(product_kernel, sizes, per),
        [(hidden * rows, cols)],
        [
            pltpu.VMEM((2, per, rows * n_dev, cols), F32),
            pltpu.VMEM((n_dev, per * rows, cols), F32),
        ],
        16,
        2 * per * cols * cols * cols,
        recv,
    )
    recv = lax.all_to_all(send, BOTH, split_axis=0, concat_axis=0, tiled=True)
    (out,) = call(
        functools.partial(finish_kernel, sizes),
        [(rows, cols, width)],
        [
            pltpu.VMEM((rows, hidden, cols), BF16),
            pltpu.VMEM((rows, cols, width), BF16),
            pltpu.SemaphoreType.DMA((rows,)),
        ],
        16,
        4 * rows * cols * width * hidden,
        recv,
        mid,
        gate,
        final_t,
        far_out=True,
    )
    return out


def power_of_two(n):
    return n & (n - 1) == 0


def on_device(pair, alignment, opm_left, *rest):
    rows, cols, width = pair.shape
    factor, hidden = opm_left.shape[1], rest[2].shape[1]
    n_row, n_col, n_seq = (lax.axis_size(a) for a in ("row", "col", "seq"))
    n_dev = n_row * n_seq
    held = n_row // 2 * alignment.shape[0]
    fits = (
        n_col == 1
        and power_of_two(n_row)
        and power_of_two(n_seq)
        and power_of_two(rows)
        and n_row >= 4
        and n_seq >= 4
        and hidden % n_dev == 0
        and hidden == width
        and factor % 16 == 0
        and rows % 8 == 0
        and (hidden // n_dev * rows) % 16 == 0
        and cols % 256 == 0
        and rows * factor == cols
        and rows * n_dev == cols
        and held % 16 == 0
        and 256 % held == 0
        and factor % (256 // held) == 0
        and hidden % (256 // rows) == 0
        and power_of_two(held * n_seq * 2)
    )
    plan = whole_channels if fits else by_groups
    return plan(pair, alignment, opm_left, *rest)


def solution(mesh):
    return jax.shard_map(
        on_device,
        mesh=mesh,
        in_specs=(
            P(("row", "seq"), "col", None),
            P(("row", "seq"), "col", None),
            P(),
            P(),
            P(),
            P(),
            P(),
            P(),
            P(),
            P(),
            P(),
        ),
        out_specs=P(("row", "seq"), "col", None),
        check_vma=False,
    )
```

```python
import functools
import math

import jax
import jax.numpy as jnp
from jax import lax
from jax.experimental import pallas as pl
from jax.experimental.pallas import tpu as pltpu
from jax.sharding import PartitionSpec as P

EPS = 1e-05
BOTH = ("row", "seq")
BF16 = jnp.bfloat16
F32 = jnp.float32


def spread_2(shard, axis, root):
    mine = lax.axis_index(axis) == root
    return lax.psum(jnp.where(mine, shard, jnp.zeros_like(shard)), axis)


def layer_norm(values, axis):
    values = values.astype(jnp.float32)
    center = values - jnp.mean(values, axis=axis, keepdims=True)
    spread = jnp.mean(center * center, axis=axis, keepdims=True)
    return center * lax.rsqrt(spread + EPS)


def contract(local_rows, piece):
    return jnp.einsum("cik,cjk->cij", local_rows, piece, preferred_element_type=jnp.float32)


def by_groups(
    pair,
    alignment,
    opm_left,
    opm_right,
    opm_out,
    tri_left,
    tri_left_gate,
    tri_right,
    tri_right_gate,
    tri_gate,
    tri_out,
):
    rows_here, cols_here, pair_width = pair.shape
    seq_here = alignment.shape[0]
    model_width = alignment.shape[2]
    factor_width = opm_left.shape[1]
    hidden = tri_left.shape[1]
    n_row = lax.axis_size("row")
    n_col = lax.axis_size("col")
    n_seq = lax.axis_size("seq")
    seq_normed = (
        layer_norm(alignment, 2).astype(jnp.bfloat16).reshape(seq_here * cols_here, model_width)
    )
    left_proj = (
        jnp.dot(seq_normed, opm_left, preferred_element_type=jnp.float32)
        .astype(jnp.bfloat16)
        .reshape(seq_here, cols_here * factor_width)
    )
    right_proj = (
        jnp.dot(seq_normed, opm_right, preferred_element_type=jnp.float32)
        .astype(jnp.bfloat16)
        .reshape(seq_here, cols_here * factor_width)
    )
    per_col = n_row // n_col
    index_row = lax.axis_index("row")
    root_col = index_row // per_col
    right_all = lax.all_gather(right_proj, ("row", "seq"), axis=0, tiled=True)
    left_blocks = left_proj.reshape(seq_here, per_col * n_seq, rows_here * factor_width)
    left_send = jnp.tile(left_blocks, (1, n_col, 1))
    left_recv = lax.all_to_all(left_send, ("row", "seq"), split_axis=1, concat_axis=0, tiled=True)
    row_slice = left_recv.reshape(seq_here * n_row * n_seq, rows_here * factor_width)
    seqs_all = right_all.shape[0]
    row_factors = spread_2(row_slice, "col", root_col)
    right_wide = right_all.reshape(seqs_all, cols_here, factor_width)
    row_stack = jnp.swapaxes(row_factors.reshape(seqs_all, rows_here, factor_width), 0, 1)

    def outer_row(packed):
        row_vals, pair_row = packed
        outer_sum = jnp.einsum(
            "np,njq->jpq", row_vals, right_wide, preferred_element_type=jnp.float32
        )
        mean_outer = (
            (outer_sum * (1.0 / seqs_all))
            .astype(jnp.bfloat16)
            .reshape(cols_here, factor_width * factor_width)
        )
        return (
            pair_row.astype(jnp.float32)
            + jnp.dot(mean_outer, opm_out, preferred_element_type=jnp.float32)
        ).astype(jnp.bfloat16)

    pair_mid = lax.map(outer_row, (row_stack, pair))
    normed_pair = layer_norm(pair_mid, 2).astype(jnp.bfloat16)
    flat_pair = normed_pair.reshape(rows_here * cols_here, pair_width)

    def project(weight):
        return lax.dot_general(
            weight, flat_pair, (((0,), (1,)), ((), ())), preferred_element_type=jnp.float32
        )

    def gated(weight_gate, weight_value):
        gate_part = jax.nn.sigmoid(project(weight_gate))
        return (
            (gate_part * project(weight_value))
            .astype(jnp.bfloat16)
            .reshape(hidden, rows_here, cols_here)
        )

    left_first = gated(tri_left_gate, tri_left)
    right_first = gated(tri_right_gate, tri_right)
    left_local, right_local = (
        lax.all_to_all(
            lax.all_to_all(left_first, "col", split_axis=0, concat_axis=2, tiled=True),
            "seq",
            split_axis=0,
            concat_axis=1,
            tiled=True,
        ),
        lax.all_to_all(
            lax.all_to_all(right_first, "col", split_axis=0, concat_axis=2, tiled=True),
            "seq",
            split_axis=0,
            concat_axis=1,
            tiled=True,
        ),
    )
    product = contract(left_local, lax.all_gather(right_local, "row", axis=1, tiled=True))
    product = product.astype(jnp.bfloat16)
    returned = lax.all_to_all(
        lax.all_to_all(product, "col", split_axis=2, concat_axis=0, tiled=True),
        "seq",
        split_axis=1,
        concat_axis=0,
        tiled=True,
    )
    per_group = hidden // (n_col * n_seq)
    weights_order = (
        tri_out.reshape(n_col, n_seq, per_group, pair_width)
        .transpose(1, 0, 2, 3)
        .reshape(hidden, pair_width)
    )
    normed_product = layer_norm(returned, 0).astype(jnp.bfloat16)
    update = jnp.einsum(
        "cij,cd->ijd", normed_product, weights_order, preferred_element_type=jnp.float32
    )
    gate_part = jax.nn.sigmoid(
        jnp.dot(flat_pair, tri_gate, preferred_element_type=jnp.float32)
    ).reshape(rows_here, cols_here, pair_width)
    return (pair_mid.astype(jnp.float32) + gate_part * update).astype(jnp.bfloat16)


def mul(a, b):
    return jnp.dot(a, b, preferred_element_type=F32)


def mul_t(a, b):
    return lax.dot_general(a, b, (((1,), (1,)), ((), ())), preferred_element_type=F32)


def ones_where(mask):
    return jnp.where(mask, 1.0, 0.0).astype(BF16)


def iotas(rows, cols):
    shape = (rows, cols)
    return lax.broadcasted_iota(jnp.int32, shape, 0), lax.broadcasted_iota(jnp.int32, shape, 1)


def identity(size):
    row, col = iotas(size, size)
    return ones_where(row == col)


def swap_rows(outer, inner):
    row, col = iotas(outer * inner, outer * inner)
    return ones_where(col == (row % outer) * inner + row // outer)


def normalize(values, axis):
    center = values - jnp.mean(values, axis=axis, keepdims=True)
    spread = jnp.mean(center * center, axis=axis, keepdims=True)
    return center * lax.rsqrt(spread + EPS)


def fetch(sems, pairs):
    copies = [
        pltpu.make_async_copy(source, target, sems.at[k]) for k, (source, target) in enumerate(pairs)
    ]
    for copy in copies:
        copy.start()
    return copies


def factors_kernel(sizes, align_in, left_in, right_in, *refs):
    n_far, n_near, n_core, rows, _ = sizes
    out_refs, (parts, align_ref, left_ref, right_ref, own_lane, picks, sems) = refs[:n_far], refs[n_far:]
    pairs = [(left_in, left_ref), (right_in, right_ref)]
    pairs += [(align_in, align_ref)]
    copies = fetch(sems, pairs)
    seqs, cols, width = align_ref.shape
    factor = left_ref.shape[0]
    chip_rows = n_core * rows
    row, col = iotas(chip_rows * factor, factor)
    widen = ones_where(row % factor == col)
    row, col = iotas(cols, chip_rows * factor)
    own_lane[...] = ones_where((row % chip_rows) == (col // factor))
    row, col = iotas(n_far * seqs * n_near, cols)
    chip_of_row = (row // (seqs * n_near)) * n_near + row % n_near
    chip_match = chip_of_row == col // chip_rows
    seq_of_row = (row // n_near) % seqs
    for n in range(seqs):
        picks[n] = ones_where(chip_match & (seq_of_row == n))
    copies[0].wait()
    copies[1].wait()
    left_wide = mul(widen, left_ref[...]).astype(BF16)
    right_rows, left_rows = [], None
    for n in range(seqs):
        if n == 0:
            copies[2].wait()
        normed = normalize(align_ref[n].astype(F32), 1).astype(BF16)
        right_rows.append(mul_t(right_ref[...], normed))
        spread = mul_t(normed, left_wide).astype(BF16) * own_lane[...]
        part = mul(picks[n], spread)
        left_rows = part if left_rows is None else left_rows + part
    right_block = jnp.concatenate(right_rows, 0).astype(BF16)
    part_rows = seqs * n_near
    pieces = n_core
    for far in range(n_far):
        for piece in range(pieces):
            parts[far, piece * part_rows : (piece + 1) * part_rows, :] = left_rows[
                far * part_rows : (far + 1) * part_rows, piece * cols : (piece + 1) * cols
            ].astype(BF16)
    here = lax.axis_index("row") // 2
    for k in range(n_far):
        out_refs[k][: seqs * factor, :] = right_block
        out_refs[k][seqs * factor :, :] = parts[here ^ k]


def regroup_kernel(sizes, factor, seqs, *refs):
    n_far, n_near, n_core, _, _ = sizes
    in_refs, out_refs, parts = refs[:n_far], refs[n_far : n_far + n_near], refs[-1]
    held = n_far * seqs
    half = 256 // held
    shuffle = swap_rows(held, half)
    for h in range(factor // half):
        block = jnp.concatenate(
            [
                ref[n * factor + h * half : n * factor + (h + 1) * half, :]
                for ref in in_refs
                for n in range(seqs)
            ],
            0,
        )
        block = mul(shuffle, block).astype(BF16)
        for ref in out_refs:
            ref[h * half * held : (h + 1) * half * held, :] = block
    part_rows = seqs * n_near
    base = seqs * factor
    pick = swap_rows(held, n_near)
    for piece in range(n_core):
        block = jnp.concatenate(
            [ref[base + piece * part_rows : base + (piece + 1) * part_rows, :] for ref in in_refs], 0
        )
        block = mul(pick, block).astype(BF16)
        for near in range(n_near):
            parts[near, piece * held : (piece + 1) * held, :] = block[
                near * held : (near + 1) * held
            ]
    n_y = n_near // 2
    here = (lax.axis_index("row") % 2) * n_y + lax.axis_index("seq") // n_core
    for k in range(n_near):
        out_refs[k][factor * held :, :] = parts[here ^ k]


def prepare_kernel(factor, *refs):
    n = (len(refs) - 6) // 2
    sources, (pair_t, out_t, tri_t, gate_t, final_t), targets = refs[:n], refs[n : n + 5], refs[n + 5 : -1]
    copies = fetch(refs[-1], list(zip(sources, targets, strict=True)))
    pair_ref, out_w, *tri, gate_w, final_w = targets
    eye = identity(pair_ref.shape[2])
    for copy in copies:
        copy.wait()
    for i in range(pair_ref.shape[0]):
        pair_t[i] = mul_t(eye, pair_ref[i]).astype(BF16)
    shuffle = swap_rows(256 // 16, 16)
    for q in range(0, factor, 16):
        for p in range(0, factor, 256 // 16):
            block = jnp.concatenate(
                [
                    out_w[(p + k) * factor + q : (p + k) * factor + q + 16, :]
                    for k in range(256 // 16)
                ],
                0,
            )
            block = mul(shuffle, block).astype(BF16)
            block = mul_t(eye, block).astype(BF16)
            at = (q // 16 * (factor // 16) + p // 16) * 256
            out_t[:, at : at + 256] = block
    for k, ref in enumerate(tri):
        width = ref.shape[1]
        tri_t[k * width : (k + 1) * width, :] = mul_t(eye, ref[...]).astype(BF16)
    gate_t[...] = mul_t(eye, gate_w[...]).astype(BF16)
    final_t[...] = mul_t(eye, final_w[...]).astype(BF16)


def gate_kernel(norm_ref, gate_w, gate_ref):
    for i in range(norm_ref.shape[0]):
        gate_ref[i] = jax.nn.sigmoid(mul(gate_w[...], norm_ref[i]))


def pair_kernel(sizes, held, scale, *refs):
    n_core, rows, n_dev = sizes[2], sizes[3], sizes[4]
    groups = refs[:-8]
    pair_ref, out_w, tri_w, send_ref, mid_ref, norm_ref, outer, both = refs[-8:]
    factor = groups[0].shape[0] // held - n_core
    hidden = tri_w.shape[0] // 4
    core = lax.axis_index("seq") % n_core
    at = pl.multiple_of((factor + core) * held, held)
    left = jnp.concatenate([ref[pl.ds(at, held), :] for ref in groups], 0)
    left_t = mul_t(identity(rows * factor), left).astype(BF16)
    for q in range(factor):
        right = jnp.concatenate([ref[q * held : (q + 1) * held, :] for ref in groups], 0)
        block = mul(left_t, right).astype(BF16)
        for i in range(rows):
            for p in range(0, factor, 16):
                at = (q // 16 * (factor // 16) + p // 16) * 256 + q % 16 * 16
                outer[i, at : at + 16, :] = block[i * factor + p : i * factor + p + 16]
    for i in range(rows):
        update = mul(out_w[...], outer[i])
        mid = (pair_ref[i].astype(F32) + update * scale).astype(BF16)
        mid_ref[i] = mid
        normed = normalize(mid.astype(F32), 0).astype(BF16)
        norm_ref[i] = normed
        for side in range(2):
            at = 2 * side * hidden
            gate = jax.nn.sigmoid(mul(tri_w[at : at + hidden, :], normed))
            value = mul(tri_w[at + hidden : at + 2 * hidden, :], normed)
            both[side, i] = (gate * value).astype(BF16)
    per = hidden // n_dev
    some = 256 // rows
    shuffle = swap_rows(rows, some)
    chunk = per * rows
    for side in range(2):
        for b in range(hidden // some):
            block = jnp.concatenate(
                [both[side, i, b * some : (b + 1) * some, :] for i in range(rows)], 0
            )
            block = mul(shuffle, block).astype(BF16)
            for d in range(some // per):
                to = ((b * some // per + d) * 2 + side) * chunk
                send_ref[to : to + chunk, :] = block[d * chunk : (d + 1) * chunk]


def product_kernel(sizes, per, recv_ref, send_ref, factors, total):
    rows, n_dev = sizes[3], sizes[4]
    chunk = per * rows
    for src in range(n_dev):
        for side in range(2):
            at = (src * 2 + side) * chunk
            block = recv_ref[at : at + chunk, :].astype(F32)
            for c in range(per):
                factors[side, c, src * rows : (src + 1) * rows, :] = block[c * rows : (c + 1) * rows]
    for c in range(per):
        prod = mul_t(factors[0, c].astype(BF16), factors[1, c].astype(BF16))
        for dst in range(n_dev):
            total[dst, c * rows : (c + 1) * rows, :] = prod[dst * rows : (dst + 1) * rows]
    for dst in range(n_dev):
        send_ref[dst * chunk : (dst + 1) * chunk, :] = total[dst].astype(BF16)


def finish_kernel(sizes, recv_ref, mid_ref, gate_ref, out_w, out_ref, apart, done_ref, sems):
    rows = sizes[3]
    _, width, cols = mid_ref.shape
    hidden = out_w.shape[1]
    some = 256 // rows
    blocks = hidden // some
    count = some * rows

    def piece(b):
        return recv_ref[b * count : (b + 1) * count, :].astype(F32).reshape(some, rows, cols)

    mean = sum(jnp.sum(piece(b), 0) for b in range(blocks)) * (1.0 / hidden)
    spread = sum(jnp.sum((piece(b) - mean) ** 2, 0) for b in range(blocks)) * (1.0 / hidden)
    factor = lax.rsqrt(spread + EPS)
    shuffle = swap_rows(some, rows)
    for b in range(blocks):
        normed = ((piece(b) - mean) * factor).reshape(count, cols).astype(BF16)
        normed = mul(shuffle, normed).astype(BF16)
        for i in range(rows):
            apart[i, b * some : (b + 1) * some, :] = normed[i * some : (i + 1) * some]
    eye = identity(cols)
    copies = []
    for i in range(rows):
        update = mul(out_w[...], apart[i])
        done = (mid_ref[i].astype(F32) + gate_ref[i] * update).astype(BF16)
        done_ref[i] = mul_t(eye, done).astype(BF16)
        copies.append(pltpu.make_async_copy(done_ref.at[i], out_ref.at[i], sems.at[i]))
        copies[i].start()
    for copy in copies:
        copy.wait()


def call(kernel, out_shape, scratch, grant, flops, *args, far_in=False, far_out=False):
    spaces = [pltpu.HBM if far else pltpu.VMEM for far in (far_in, far_out)]
    place = jax.ShapeDtypeStruct if far_out else pltpu.VMEM
    out_shape = [place(*s) if isinstance(s[0], tuple) else place(s, BF16) for s in out_shape]
    if far_in:
        args = [pltpu.with_memory_space_constraint(a, pltpu.HBM) for a in args]
    moved = sum(math.prod(a.shape) * jnp.dtype(a.dtype).itemsize for a in (*args, *out_shape))
    return pl.pallas_call(
        kernel,
        out_shape=out_shape,
        in_specs=[pl.BlockSpec(memory_space=spaces[0])] * len(args),
        out_specs=[pl.BlockSpec(memory_space=spaces[1])] * len(out_shape),
        scratch_shapes=scratch,
        compiler_params=pltpu.CompilerParams(vmem_limit_bytes=grant * 2**20),
        cost_estimate=pl.CostEstimate(flops=flops, bytes_accessed=moved, transcendentals=0),
    )(*args)


def factors_call(sizes, alignment, opm_left, opm_right):
    n_far, n_near, n_core, rows, _ = sizes
    seqs, cols, width = alignment.shape
    factor = opm_left.shape[1]
    return call(
        functools.partial(factors_kernel, sizes),
        [(seqs * factor + n_core * seqs * n_near, cols)] * n_far,
        [
            pltpu.VMEM((n_far, n_core * seqs * n_near, cols), BF16),
            pltpu.VMEM(alignment.shape, BF16),
            pltpu.VMEM(opm_left.shape[::-1], BF16),
            pltpu.VMEM(opm_right.shape[::-1], BF16),
            pltpu.VMEM((cols, n_core * rows * factor), BF16),
            pltpu.VMEM((seqs, n_far * seqs * n_near, cols), BF16),
            pltpu.SemaphoreType.DMA((2 + seqs,)),
        ],
        8,
        4 * seqs * cols * width * factor,
        alignment,
        opm_left.T,
        opm_right.T,
        far_in=True,
    )


def whole_channels(
    pair,
    alignment,
    opm_left,
    opm_right,
    opm_out,
    tri_left,
    tri_left_gate,
    tri_right,
    tri_right_gate,
    tri_gate,
    tri_out,
):
    rows, cols, width = pair.shape
    seqs = alignment.shape[0]
    factor = opm_left.shape[1]
    hidden = tri_left.shape[1]
    n_row, n_seq = lax.axis_size("row"), lax.axis_size("seq")
    n_dev = n_row * n_seq
    n_core = 2
    n_far, n_near = n_row // 2, 2 * (n_seq // n_core)
    n_y = n_near // 2
    sizes = (n_far, n_near, n_core, rows, n_dev)
    held = n_far * seqs
    per = hidden // n_dev

    def exchange(value, row_bits, seq_bits):
        pairs = [
            (r * n_seq + s, (r ^ row_bits) * n_seq + (s ^ seq_bits))
            for r in range(n_row)
            for s in range(n_seq)
        ]
        return lax.ppermute(value, BOTH, pairs)

    mine = factors_call(sizes, alignment, opm_left, opm_right)
    weights = (
        pair,
        opm_out,
        tri_left_gate,
        tri_left,
        tri_right_gate,
        tri_right,
        tri_gate,
        tri_out,
    )
    mine, weights = lax.optimization_barrier((mine, weights))
    far = [exchange(mine[k], 2 * k, 0) for k in range(n_far - 1, 0, -1)]
    far = [mine[0]] + far
    prepared = call(
        functools.partial(prepare_kernel, factor),
        [
            (rows, width, cols),
            (width, factor * factor),
            (4 * hidden, width),
            (width, width),
            (width, hidden),
        ],
        [pltpu.VMEM(w.shape, BF16) for w in weights] + [pltpu.SemaphoreType.DMA((len(weights),))],
        8,
        4 * rows * cols * width * width,
        *weights,
        far_in=True,
    )
    far, prepared = lax.optimization_barrier((far, prepared))
    pair_t, out_t, tri_t, gate_t, final_t = prepared
    message = ((factor + n_core) * held, cols)
    mine = call(
        functools.partial(regroup_kernel, sizes, factor, seqs),
        [message] * n_near,
        [pltpu.VMEM((n_near, n_core * held, cols), BF16)],
        8,
        2 * 256 * factor * held * cols,
        *far,
    )
    near = [
        exchange(mine[k], k // n_y, (k % n_y) * n_core) for k in range(n_near - 1, 0, -1)
    ]
    near = [mine[0]] + near
    groups = near + [exchange(block, 0, 1) for block in near]
    scale = 1.0 / (held * n_near * n_core)
    send, mid, normed = call(
        functools.partial(pair_kernel, sizes, held, scale),
        [(2 * hidden * rows, cols), (rows, width, cols), (rows, width, cols)],
        [
            pltpu.VMEM((rows, factor * factor, cols), BF16),
            pltpu.VMEM((2, rows, hidden, cols), BF16),
        ],
        16,
        4 * rows * cols * width * (factor * factor + hidden * 2),
        *groups,
        pair_t,
        out_t,
        tri_t,
    )
    (gate,) = call(
        gate_kernel,
        [((rows, width, cols), F32)],
        [],
        8,
        2 * rows * cols * width * width,
        normed,
        gate_t,
    )
    recv = lax.all_to_all(send, BOTH, split_axis=0, concat_axis=0, tiled=True)
    (send,) = call(
        functools.partial(product_kernel, sizes, per),
        [(hidden * rows, cols)],
        [
            pltpu.VMEM((2, per, rows * n_dev, cols), F32),
            pltpu.VMEM((n_dev, per * rows, cols), F32),
        ],
        16,
        2 * per * cols * cols * cols,
        recv,
    )
    recv = lax.all_to_all(send, BOTH, split_axis=0, concat_axis=0, tiled=True)
    (out,) = call(
        functools.partial(finish_kernel, sizes),
        [(rows, cols, width)],
        [
            pltpu.VMEM((rows, hidden, cols), BF16),
            pltpu.VMEM((rows, cols, width), BF16),
            pltpu.SemaphoreType.DMA((rows,)),
        ],
        16,
        4 * rows * cols * width * hidden,
        recv,
        mid,
        gate,
        final_t,
        far_out=True,
    )
    return out


def power_of_two(n):
    return n & (n - 1) == 0


def on_device(pair, alignment, opm_left, *rest):
    rows, cols, width = pair.shape
    factor, hidden = opm_left.shape[1], rest[2].shape[1]
    n_row, n_col, n_seq = (lax.axis_size(a) for a in ("row", "col", "seq"))
    n_dev = n_row * n_seq
    held = n_row // 2 * alignment.shape[0]
    fits = (
        n_col == 1
        and power_of_two(n_row)
        and power_of_two(n_seq)
        and power_of_two(rows)
        and n_row >= 4
        and n_seq >= 4
        and hidden % n_dev == 0
        and hidden == width
        and factor % 16 == 0
        and rows % 8 == 0
        and (hidden // n_dev * rows) % 16 == 0
        and cols % 256 == 0
        and rows * factor == cols
        and rows * n_dev == cols
        and held % 16 == 0
        and 256 % held == 0
        and factor % (256 // held) == 0
        and hidden % (256 // rows) == 0
        and power_of_two(held * n_seq * 2)
    )
    plan = whole_channels if fits else by_groups
    return plan(pair, alignment, opm_left, *rest)


def solution(mesh):
    return jax.shard_map(
        on_device,
        mesh=mesh,
        in_specs=(
            P(("row", "seq"), "col", None),
            P(("row", "seq"), "col", None),
            P(),
            P(),
            P(),
            P(),
            P(),
            P(),
            P(),
            P(),
            P(),
        ),
        out_specs=P(("row", "seq"), "col", None),
        check_vma=False,
    )
```

```python
import functools
import math

import jax
import jax.numpy as jnp
from jax import lax
from jax.experimental import pallas as pl
from jax.experimental.pallas import tpu as pltpu
from jax.sharding import PartitionSpec as P

EPS = 1e-05
BOTH = ("row", "seq")
BF16 = jnp.bfloat16
F32 = jnp.float32


def spread_2(shard, axis, root):
    mine = lax.axis_index(axis) == root
    return lax.psum(jnp.where(mine, shard, jnp.zeros_like(shard)), axis)


def layer_norm(values, axis):
    values = values.astype(jnp.float32)
    center = values - jnp.mean(values, axis=axis, keepdims=True)
    spread = jnp.mean(center * center, axis=axis, keepdims=True)
    return center * lax.rsqrt(spread + EPS)


def contract(local_rows, piece):
    return jnp.einsum("cik,cjk->cij", local_rows, piece, preferred_element_type=jnp.float32)


def by_groups(
    pair,
    alignment,
    opm_left,
    opm_right,
    opm_out,
    tri_left,
    tri_left_gate,
    tri_right,
    tri_right_gate,
    tri_gate,
    tri_out,
):
    rows_here, cols_here, pair_width = pair.shape
    seq_here = alignment.shape[0]
    model_width = alignment.shape[2]
    factor_width = opm_left.shape[1]
    hidden = tri_left.shape[1]
    n_row = lax.axis_size("row")
    n_col = lax.axis_size("col")
    n_seq = lax.axis_size("seq")
    seq_normed = (
        layer_norm(alignment, 2).astype(jnp.bfloat16).reshape(seq_here * cols_here, model_width)
    )
    left_proj = (
        jnp.dot(seq_normed, opm_left, preferred_element_type=jnp.float32)
        .astype(jnp.bfloat16)
        .reshape(seq_here, cols_here * factor_width)
    )
    right_proj = (
        jnp.dot(seq_normed, opm_right, preferred_element_type=jnp.float32)
        .astype(jnp.bfloat16)
        .reshape(seq_here, cols_here * factor_width)
    )
    per_col = n_row // n_col
    index_row = lax.axis_index("row")
    root_col = index_row // per_col
    right_all = lax.all_gather(right_proj, ("row", "seq"), axis=0, tiled=True)
    left_blocks = left_proj.reshape(seq_here, per_col * n_seq, rows_here * factor_width)
    left_send = jnp.tile(left_blocks, (1, n_col, 1))
    left_recv = lax.all_to_all(left_send, ("row", "seq"), split_axis=1, concat_axis=0, tiled=True)
    row_slice = left_recv.reshape(seq_here * n_row * n_seq, rows_here * factor_width)
    seqs_all = right_all.shape[0]
    row_factors = spread_2(row_slice, "col", root_col)
    right_wide = right_all.reshape(seqs_all, cols_here, factor_width)
    row_stack = jnp.swapaxes(row_factors.reshape(seqs_all, rows_here, factor_width), 0, 1)

    def outer_row(packed):
        row_vals, pair_row = packed
        outer_sum = jnp.einsum(
            "np,njq->jpq", row_vals, right_wide, preferred_element_type=jnp.float32
        )
        mean_outer = (
            (outer_sum * (1.0 / seqs_all))
            .astype(jnp.bfloat16)
            .reshape(cols_here, factor_width * factor_width)
        )
        return (
            pair_row.astype(jnp.float32)
            + jnp.dot(mean_outer, opm_out, preferred_element_type=jnp.float32)
        ).astype(jnp.bfloat16)

    pair_mid = lax.map(outer_row, (row_stack, pair))
    normed_pair = layer_norm(pair_mid, 2).astype(jnp.bfloat16)
    flat_pair = normed_pair.reshape(rows_here * cols_here, pair_width)

    def project(weight):
        return lax.dot_general(
            weight, flat_pair, (((0,), (1,)), ((), ())), preferred_element_type=jnp.float32
        )

    def gated(weight_gate, weight_value):
        gate_part = jax.nn.sigmoid(project(weight_gate))
        return (
            (gate_part * project(weight_value))
            .astype(jnp.bfloat16)
            .reshape(hidden, rows_here, cols_here)
        )

    left_first = gated(tri_left_gate, tri_left)
    right_first = gated(tri_right_gate, tri_right)
    left_local, right_local = (
        lax.all_to_all(
            lax.all_to_all(left_first, "col", split_axis=0, concat_axis=2, tiled=True),
            "seq",
            split_axis=0,
            concat_axis=1,
            tiled=True,
        ),
        lax.all_to_all(
            lax.all_to_all(right_first, "col", split_axis=0, concat_axis=2, tiled=True),
            "seq",
            split_axis=0,
            concat_axis=1,
            tiled=True,
        ),
    )
    product = contract(left_local, lax.all_gather(right_local, "row", axis=1, tiled=True))
    product = product.astype(jnp.bfloat16)
    returned = lax.all_to_all(
        lax.all_to_all(product, "col", split_axis=2, concat_axis=0, tiled=True),
        "seq",
        split_axis=1,
        concat_axis=0,
        tiled=True,
    )
    per_group = hidden // (n_col * n_seq)
    weights_order = (
        tri_out.reshape(n_col, n_seq, per_group, pair_width)
        .transpose(1, 0, 2, 3)
        .reshape(hidden, pair_width)
    )
    normed_product = layer_norm(returned, 0).astype(jnp.bfloat16)
    update = jnp.einsum(
        "cij,cd->ijd", normed_product, weights_order, preferred_element_type=jnp.float32
    )
    gate_part = jax.nn.sigmoid(
        jnp.dot(flat_pair, tri_gate, preferred_element_type=jnp.float32)
    ).reshape(rows_here, cols_here, pair_width)
    return (pair_mid.astype(jnp.float32) + gate_part * update).astype(jnp.bfloat16)


def mul(a, b):
    return jnp.dot(a, b, preferred_element_type=F32)


def mul_t(a, b):
    return lax.dot_general(a, b, (((1,), (1,)), ((), ())), preferred_element_type=F32)


def ones_where(mask):
    return jnp.where(mask, 1.0, 0.0).astype(BF16)


def iotas(rows, cols):
    shape = (rows, cols)
    return lax.broadcasted_iota(jnp.int32, shape, 0), lax.broadcasted_iota(jnp.int32, shape, 1)


def identity(size):
    row, col = iotas(size, size)
    return ones_where(row == col)


def swap_rows(outer, inner):
    row, col = iotas(outer * inner, outer * inner)
    return ones_where(col == (row % outer) * inner + row // outer)


def normalize(values, axis):
    center = values - jnp.mean(values, axis=axis, keepdims=True)
    spread = jnp.mean(center * center, axis=axis, keepdims=True)
    return center * lax.rsqrt(spread + EPS)


def fetch(sems, pairs):
    copies = [
        pltpu.make_async_copy(source, target, sems.at[k]) for k, (source, target) in enumerate(pairs)
    ]
    for copy in copies:
        copy.start()
    return copies


def factors_kernel(sizes, align_in, left_in, right_in, *refs):
    n_far, n_near, n_core, rows, _ = sizes
    out_refs, (parts, align_ref, left_ref, right_ref, own_lane, picks, sems) = refs[:n_far], refs[n_far:]
    pairs = [(left_in, left_ref), (right_in, right_ref)]
    pairs += [(align_in, align_ref)]
    copies = fetch(sems, pairs)
    seqs, cols, width = align_ref.shape
    factor = left_ref.shape[0]
    chip_rows = n_core * rows
    row, col = iotas(chip_rows * factor, factor)
    widen = ones_where(row % factor == col)
    row, col = iotas(cols, chip_rows * factor)
    own_lane[...] = ones_where((row % chip_rows) == (col // factor))
    row, col = iotas(n_far * seqs * n_near, cols)
    chip_of_row = (row // (seqs * n_near)) * n_near + row % n_near
    chip_match = chip_of_row == col // chip_rows
    seq_of_row = (row // n_near) % seqs
    for n in range(seqs):
        picks[n] = ones_where(chip_match & (seq_of_row == n))
    copies[0].wait()
    copies[1].wait()
    left_wide = mul(widen, left_ref[...]).astype(BF16)
    right_rows, left_rows = [], None
    for n in range(seqs):
        if n == 0:
            copies[2].wait()
        normed = normalize(align_ref[n].astype(F32), 1).astype(BF16)
        right_rows.append(mul_t(right_ref[...], normed))
        spread = mul_t(normed, left_wide).astype(BF16) * own_lane[...]
        part = mul(picks[n], spread)
        left_rows = part if left_rows is None else left_rows + part
    right_block = jnp.concatenate(right_rows, 0).astype(BF16)
    part_rows = seqs * n_near
    pieces = n_core
    for far in range(n_far):
        for piece in range(pieces):
            parts[far, piece * part_rows : (piece + 1) * part_rows, :] = left_rows[
                far * part_rows : (far + 1) * part_rows, piece * cols : (piece + 1) * cols
            ].astype(BF16)
    here = lax.axis_index("row") // 2
    for k in range(n_far):
        out_refs[k][: seqs * factor, :] = right_block
        out_refs[k][seqs * factor :, :] = parts[here ^ k]


def regroup_kernel(sizes, factor, seqs, *refs):
    n_far, n_near, n_core, _, _ = sizes
    in_refs, out_refs, parts = refs[:n_far], refs[n_far : n_far + n_near], refs[-1]
    held = n_far * seqs
    half = 256 // held
    shuffle = swap_rows(held, half)
    for h in range(factor // half):
        block = jnp.concatenate(
            [
                ref[n * factor + h * half : n * factor + (h + 1) * half, :]
                for ref in in_refs
                for n in range(seqs)
            ],
            0,
        )
        block = mul(shuffle, block).astype(BF16)
        for ref in out_refs:
            ref[h * half * held : (h + 1) * half * held, :] = block
    part_rows = seqs * n_near
    base = seqs * factor
    pick = swap_rows(held, n_near)
    for piece in range(n_core):
        block = jnp.concatenate(
            [ref[base + piece * part_rows : base + (piece + 1) * part_rows, :] for ref in in_refs], 0
        )
        block = mul(pick, block).astype(BF16)
        for near in range(n_near):
            parts[near, piece * held : (piece + 1) * held, :] = block[
                near * held : (near + 1) * held
            ]
    n_y = n_near // 2
    here = (lax.axis_index("row") % 2) * n_y + lax.axis_index("seq") // n_core
    for k in range(n_near):
        out_refs[k][factor * held :, :] = parts[here ^ k]


def prepare_kernel(factor, *refs):
    n = (len(refs) - 6) // 2
    sources, (pair_t, out_t, tri_t, gate_t, final_t), targets = refs[:n], refs[n : n + 5], refs[n + 5 : -1]
    copies = fetch(refs[-1], list(zip(sources, targets, strict=True)))
    pair_ref, out_w, *tri, gate_w, final_w = targets
    eye = identity(pair_ref.shape[2])
    for copy in copies:
        copy.wait()
    for i in range(pair_ref.shape[0]):
        pair_t[i] = mul_t(eye, pair_ref[i]).astype(BF16)
    shuffle = swap_rows(256 // 16, 16)
    for q in range(0, factor, 16):
        for p in range(0, factor, 256 // 16):
            block = jnp.concatenate(
                [
                    out_w[(p + k) * factor + q : (p + k) * factor + q + 16, :]
                    for k in range(256 // 16)
                ],
                0,
            )
            block = mul(shuffle, block).astype(BF16)
            block = mul_t(eye, block).astype(BF16)
            at = (q // 16 * (factor // 16) + p // 16) * 256
            out_t[:, at : at + 256] = block
    for k, ref in enumerate(tri):
        width = ref.shape[1]
        tri_t[k * width : (k + 1) * width, :] = mul_t(eye, ref[...]).astype(BF16)
    gate_t[...] = mul_t(eye, gate_w[...]).astype(BF16)
    final_t[...] = mul_t(eye, final_w[...]).astype(BF16)


def gate_kernel(norm_ref, gate_w, gate_ref):
    for i in range(norm_ref.shape[0]):
        gate_ref[i] = jax.nn.sigmoid(mul(gate_w[...], norm_ref[i]))


def pair_kernel(sizes, held, scale, *refs):
    n_core, rows, n_dev = sizes[2], sizes[3], sizes[4]
    groups = refs[:-8]
    pair_ref, out_w, tri_w, send_ref, mid_ref, norm_ref, outer, both = refs[-8:]
    factor = groups[0].shape[0] // held - n_core
    hidden = tri_w.shape[0] // 4
    core = lax.axis_index("seq") % n_core
    at = pl.multiple_of((factor + core) * held, held)
    left = jnp.concatenate([ref[pl.ds(at, held), :] for ref in groups], 0)
    left_t = mul_t(identity(rows * factor), left).astype(BF16)
    for q in range(factor):
        right = jnp.concatenate([ref[q * held : (q + 1) * held, :] for ref in groups], 0)
        block = mul(left_t, right).astype(BF16)
        for i in range(rows):
            for p in range(0, factor, 16):
                at = (q // 16 * (factor // 16) + p // 16) * 256 + q % 16 * 16
                outer[i, at : at + 16, :] = block[i * factor + p : i * factor + p + 16]
    updates = [mul(out_w[...], outer[i]) for i in range(rows)]
    for i in range(rows):
        update = updates[i]
        mid = (pair_ref[i].astype(F32) + update * scale).astype(BF16)
        mid_ref[i] = mid
        normed = normalize(mid.astype(F32), 0).astype(BF16)
        norm_ref[i] = normed
    for i in range(rows):
        parts = mul(tri_w[...], norm_ref[i])
        for side in range(2):
            at = 2 * side * hidden
            gate = jax.nn.sigmoid(parts[at : at + hidden])
            both[side, i] = (gate * parts[at + hidden : at + 2 * hidden]).astype(BF16)
    per = hidden // n_dev
    some = 256 // rows
    shuffle = swap_rows(rows, some)
    chunk = per * rows
    for side in range(2):
        for b in range(hidden // some):
            block = jnp.concatenate(
                [both[side, i, b * some : (b + 1) * some, :] for i in range(rows)], 0
            )
            block = mul(shuffle, block).astype(BF16)
            for d in range(some // per):
                to = ((b * some // per + d) * 2 + side) * chunk
                send_ref[to : to + chunk, :] = block[d * chunk : (d + 1) * chunk]


def product_kernel(sizes, per, recv_ref, send_ref, factors, total):
    rows, n_dev = sizes[3], sizes[4]
    chunk = per * rows
    for src in range(n_dev):
        for side in range(2):
            at = (src * 2 + side) * chunk
            block = recv_ref[at : at + chunk, :].astype(F32)
            for c in range(per):
                factors[side, c, src * rows : (src + 1) * rows, :] = block[c * rows : (c + 1) * rows]
    for c in range(per):
        prod = mul_t(factors[0, c].astype(BF16), factors[1, c].astype(BF16))
        for dst in range(n_dev):
            total[dst, c * rows : (c + 1) * rows, :] = prod[dst * rows : (dst + 1) * rows]
    for dst in range(n_dev):
        send_ref[dst * chunk : (dst + 1) * chunk, :] = total[dst].astype(BF16)


def finish_kernel(sizes, recv_ref, mid_ref, gate_ref, out_w, out_ref, apart, done_ref, sems):
    rows = sizes[3]
    _, width, cols = mid_ref.shape
    hidden = out_w.shape[1]
    some = 256 // rows
    blocks = hidden // some
    count = some * rows

    def piece(b):
        return recv_ref[b * count : (b + 1) * count, :].astype(F32).reshape(some, rows, cols)

    mean = sum(jnp.sum(piece(b), 0) for b in range(blocks)) * (1.0 / hidden)
    spread = sum(jnp.sum((piece(b) - mean) ** 2, 0) for b in range(blocks)) * (1.0 / hidden)
    factor = lax.rsqrt(spread + EPS)
    shuffle = swap_rows(some, rows)
    for b in range(blocks):
        normed = ((piece(b) - mean) * factor).reshape(count, cols).astype(BF16)
        normed = mul(shuffle, normed).astype(BF16)
        for i in range(rows):
            apart[i, b * some : (b + 1) * some, :] = normed[i * some : (i + 1) * some]
    eye = identity(cols)
    copies = []
    updates = [mul(out_w[...], apart[i]) for i in range(rows)]
    dones = [(mid_ref[i].astype(F32) + gate_ref[i] * updates[i]).astype(BF16) for i in range(rows)]
    for i in range(rows):
        done_ref[i] = mul_t(eye, dones[i]).astype(BF16)
        copies.append(pltpu.make_async_copy(done_ref.at[i], out_ref.at[i], sems.at[i]))
        copies[i].start()
    for copy in copies:
        copy.wait()


def call(kernel, out_shape, scratch, grant, flops, *args, far_in=False, far_out=False):
    spaces = [pltpu.HBM if far else pltpu.VMEM for far in (far_in, far_out)]
    place = jax.ShapeDtypeStruct if far_out else pltpu.VMEM
    out_shape = [place(*s) if isinstance(s[0], tuple) else place(s, BF16) for s in out_shape]
    if far_in:
        args = [pltpu.with_memory_space_constraint(a, pltpu.HBM) for a in args]
    moved = sum(math.prod(a.shape) * jnp.dtype(a.dtype).itemsize for a in (*args, *out_shape))
    return pl.pallas_call(
        kernel,
        out_shape=out_shape,
        in_specs=[pl.BlockSpec(memory_space=spaces[0])] * len(args),
        out_specs=[pl.BlockSpec(memory_space=spaces[1])] * len(out_shape),
        scratch_shapes=scratch,
        compiler_params=pltpu.CompilerParams(vmem_limit_bytes=grant * 2**20),
        cost_estimate=pl.CostEstimate(flops=flops, bytes_accessed=moved, transcendentals=0),
    )(*args)


def factors_call(sizes, alignment, opm_left, opm_right):
    n_far, n_near, n_core, rows, _ = sizes
    seqs, cols, width = alignment.shape
    factor = opm_left.shape[1]
    return call(
        functools.partial(factors_kernel, sizes),
        [(seqs * factor + n_core * seqs * n_near, cols)] * n_far,
        [
            pltpu.VMEM((n_far, n_core * seqs * n_near, cols), BF16),
            pltpu.VMEM(alignment.shape, BF16),
            pltpu.VMEM(opm_left.shape[::-1], BF16),
            pltpu.VMEM(opm_right.shape[::-1], BF16),
            pltpu.VMEM((cols, n_core * rows * factor), BF16),
            pltpu.VMEM((seqs, n_far * seqs * n_near, cols), BF16),
            pltpu.SemaphoreType.DMA((2 + seqs,)),
        ],
        8,
        4 * seqs * cols * width * factor,
        alignment,
        opm_left.T,
        opm_right.T,
        far_in=True,
    )


def whole_channels(
    pair,
    alignment,
    opm_left,
    opm_right,
    opm_out,
    tri_left,
    tri_left_gate,
    tri_right,
    tri_right_gate,
    tri_gate,
    tri_out,
):
    rows, cols, width = pair.shape
    seqs = alignment.shape[0]
    factor = opm_left.shape[1]
    hidden = tri_left.shape[1]
    n_row, n_seq = lax.axis_size("row"), lax.axis_size("seq")
    n_dev = n_row * n_seq
    n_core = 2
    n_far, n_near = n_row // 2, 2 * (n_seq // n_core)
    n_y = n_near // 2
    sizes = (n_far, n_near, n_core, rows, n_dev)
    held = n_far * seqs
    per = hidden // n_dev

    def exchange(value, row_bits, seq_bits):
        pairs = [
            (r * n_seq + s, (r ^ row_bits) * n_seq + (s ^ seq_bits))
            for r in range(n_row)
            for s in range(n_seq)
        ]
        return lax.ppermute(value, BOTH, pairs)

    mine = factors_call(sizes, alignment, opm_left, opm_right)
    weights = (
        pair,
        opm_out,
        tri_left_gate,
        tri_left,
        tri_right_gate,
        tri_right,
        tri_gate,
        tri_out,
    )
    mine, weights = lax.optimization_barrier((mine, weights))
    far = [exchange(mine[k], 2 * k, 0) for k in range(n_far - 1, 0, -1)]
    far = [mine[0]] + far
    prepared = call(
        functools.partial(prepare_kernel, factor),
        [
            (rows, width, cols),
            (width, factor * factor),
            (4 * hidden, width),
            (width, width),
            (width, hidden),
        ],
        [pltpu.VMEM(w.shape, BF16) for w in weights] + [pltpu.SemaphoreType.DMA((len(weights),))],
        8,
        4 * rows * cols * width * width,
        *weights,
        far_in=True,
    )
    far, prepared = lax.optimization_barrier((far, prepared))
    pair_t, out_t, tri_t, gate_t, final_t = prepared
    message = ((factor + n_core) * held, cols)
    mine = call(
        functools.partial(regroup_kernel, sizes, factor, seqs),
        [message] * n_near,
        [pltpu.VMEM((n_near, n_core * held, cols), BF16)],
        8,
        2 * 256 * factor * held * cols,
        *far,
    )
    near = [
        exchange(mine[k], k // n_y, (k % n_y) * n_core) for k in range(n_near - 1, 0, -1)
    ]
    near = [mine[0]] + near
    groups = near + [exchange(block, 0, 1) for block in near]
    scale = 1.0 / (held * n_near * n_core)
    send, mid, normed = call(
        functools.partial(pair_kernel, sizes, held, scale),
        [(2 * hidden * rows, cols), (rows, width, cols), (rows, width, cols)],
        [
            pltpu.VMEM((rows, factor * factor, cols), BF16),
            pltpu.VMEM((2, rows, hidden, cols), BF16),
        ],
        16,
        4 * rows * cols * width * (factor * factor + hidden * 2),
        *groups,
        pair_t,
        out_t,
        tri_t,
    )
    (gate,) = call(
        gate_kernel,
        [((rows, width, cols), F32)],
        [],
        8,
        2 * rows * cols * width * width,
        normed,
        gate_t,
    )
    recv = lax.all_to_all(send, BOTH, split_axis=0, concat_axis=0, tiled=True)
    (send,) = call(
        functools.partial(product_kernel, sizes, per),
        [(hidden * rows, cols)],
        [
            pltpu.VMEM((2, per, rows * n_dev, cols), F32),
            pltpu.VMEM((n_dev, per * rows, cols), F32),
        ],
        16,
        2 * per * cols * cols * cols,
        recv,
    )
    recv = lax.all_to_all(send, BOTH, split_axis=0, concat_axis=0, tiled=True)
    (out,) = call(
        functools.partial(finish_kernel, sizes),
        [(rows, cols, width)],
        [
            pltpu.VMEM((rows, hidden, cols), BF16),
            pltpu.VMEM((rows, cols, width), BF16),
            pltpu.SemaphoreType.DMA((rows,)),
        ],
        16,
        4 * rows * cols * width * hidden,
        recv,
        mid,
        gate,
        final_t,
        far_out=True,
    )
    return out


def power_of_two(n):
    return n & (n - 1) == 0


def on_device(pair, alignment, opm_left, *rest):
    rows, cols, width = pair.shape
    factor, hidden = opm_left.shape[1], rest[2].shape[1]
    n_row, n_col, n_seq = (lax.axis_size(a) for a in ("row", "col", "seq"))
    n_dev = n_row * n_seq
    held = n_row // 2 * alignment.shape[0]
    fits = (
        n_col == 1
        and power_of_two(n_row)
        and power_of_two(n_seq)
        and power_of_two(rows)
        and n_row >= 4
        and n_seq >= 4
        and hidden % n_dev == 0
        and hidden == width
        and factor % 16 == 0
        and rows % 8 == 0
        and (hidden // n_dev * rows) % 16 == 0
        and cols % 256 == 0
        and rows * factor == cols
        and rows * n_dev == cols
        and held % 16 == 0
        and 256 % held == 0
        and factor % (256 // held) == 0
        and hidden % (256 // rows) == 0
        and power_of_two(held * n_seq * 2)
    )
    plan = whole_channels if fits else by_groups
    return plan(pair, alignment, opm_left, *rest)


def solution(mesh):
    return jax.shard_map(
        on_device,
        mesh=mesh,
        in_specs=(
            P(("row", "seq"), "col", None),
            P(("row", "seq"), "col", None),
            P(),
            P(),
            P(),
            P(),
            P(),
            P(),
            P(),
            P(),
            P(),
        ),
        out_specs=P(("row", "seq"), "col", None),
        check_vma=False,
    )
```

```python
import functools
import math

import jax
import jax.numpy as jnp
from jax import lax
from jax.experimental import pallas as pl
from jax.experimental.pallas import tpu as pltpu
from jax.sharding import PartitionSpec as P

EPS = 1e-05
BOTH = ("row", "seq")
BF16 = jnp.bfloat16
F32 = jnp.float32


def spread_2(shard, axis, root):
    mine = lax.axis_index(axis) == root
    return lax.psum(jnp.where(mine, shard, jnp.zeros_like(shard)), axis)


def layer_norm(values, axis):
    values = values.astype(jnp.float32)
    center = values - jnp.mean(values, axis=axis, keepdims=True)
    spread = jnp.mean(center * center, axis=axis, keepdims=True)
    return center * lax.rsqrt(spread + EPS)


def contract(local_rows, piece):
    return jnp.einsum("cik,cjk->cij", local_rows, piece, preferred_element_type=jnp.float32)


def by_groups(
    pair,
    alignment,
    opm_left,
    opm_right,
    opm_out,
    tri_left,
    tri_left_gate,
    tri_right,
    tri_right_gate,
    tri_gate,
    tri_out,
):
    rows_here, cols_here, pair_width = pair.shape
    seq_here = alignment.shape[0]
    model_width = alignment.shape[2]
    factor_width = opm_left.shape[1]
    hidden = tri_left.shape[1]
    n_row = lax.axis_size("row")
    n_col = lax.axis_size("col")
    n_seq = lax.axis_size("seq")
    seq_normed = (
        layer_norm(alignment, 2).astype(jnp.bfloat16).reshape(seq_here * cols_here, model_width)
    )
    left_proj = (
        jnp.dot(seq_normed, opm_left, preferred_element_type=jnp.float32)
        .astype(jnp.bfloat16)
        .reshape(seq_here, cols_here * factor_width)
    )
    right_proj = (
        jnp.dot(seq_normed, opm_right, preferred_element_type=jnp.float32)
        .astype(jnp.bfloat16)
        .reshape(seq_here, cols_here * factor_width)
    )
    per_col = n_row // n_col
    index_row = lax.axis_index("row")
    root_col = index_row // per_col
    right_all = lax.all_gather(right_proj, ("row", "seq"), axis=0, tiled=True)
    left_blocks = left_proj.reshape(seq_here, per_col * n_seq, rows_here * factor_width)
    left_send = jnp.tile(left_blocks, (1, n_col, 1))
    left_recv = lax.all_to_all(left_send, ("row", "seq"), split_axis=1, concat_axis=0, tiled=True)
    row_slice = left_recv.reshape(seq_here * n_row * n_seq, rows_here * factor_width)
    seqs_all = right_all.shape[0]
    row_factors = spread_2(row_slice, "col", root_col)
    right_wide = right_all.reshape(seqs_all, cols_here, factor_width)
    row_stack = jnp.swapaxes(row_factors.reshape(seqs_all, rows_here, factor_width), 0, 1)

    def outer_row(packed):
        row_vals, pair_row = packed
        outer_sum = jnp.einsum(
            "np,njq->jpq", row_vals, right_wide, preferred_element_type=jnp.float32
        )
        mean_outer = (
            (outer_sum * (1.0 / seqs_all))
            .astype(jnp.bfloat16)
            .reshape(cols_here, factor_width * factor_width)
        )
        return (
            pair_row.astype(jnp.float32)
            + jnp.dot(mean_outer, opm_out, preferred_element_type=jnp.float32)
        ).astype(jnp.bfloat16)

    pair_mid = lax.map(outer_row, (row_stack, pair))
    normed_pair = layer_norm(pair_mid, 2).astype(jnp.bfloat16)
    flat_pair = normed_pair.reshape(rows_here * cols_here, pair_width)

    def project(weight):
        return lax.dot_general(
            weight, flat_pair, (((0,), (1,)), ((), ())), preferred_element_type=jnp.float32
        )

    def gated(weight_gate, weight_value):
        gate_part = jax.nn.sigmoid(project(weight_gate))
        return (
            (gate_part * project(weight_value))
            .astype(jnp.bfloat16)
            .reshape(hidden, rows_here, cols_here)
        )

    left_first = gated(tri_left_gate, tri_left)
    right_first = gated(tri_right_gate, tri_right)
    left_local, right_local = (
        lax.all_to_all(
            lax.all_to_all(left_first, "col", split_axis=0, concat_axis=2, tiled=True),
            "seq",
            split_axis=0,
            concat_axis=1,
            tiled=True,
        ),
        lax.all_to_all(
            lax.all_to_all(right_first, "col", split_axis=0, concat_axis=2, tiled=True),
            "seq",
            split_axis=0,
            concat_axis=1,
            tiled=True,
        ),
    )
    product = contract(left_local, lax.all_gather(right_local, "row", axis=1, tiled=True))
    product = product.astype(jnp.bfloat16)
    returned = lax.all_to_all(
        lax.all_to_all(product, "col", split_axis=2, concat_axis=0, tiled=True),
        "seq",
        split_axis=1,
        concat_axis=0,
        tiled=True,
    )
    per_group = hidden // (n_col * n_seq)
    weights_order = (
        tri_out.reshape(n_col, n_seq, per_group, pair_width)
        .transpose(1, 0, 2, 3)
        .reshape(hidden, pair_width)
    )
    normed_product = layer_norm(returned, 0).astype(jnp.bfloat16)
    update = jnp.einsum(
        "cij,cd->ijd", normed_product, weights_order, preferred_element_type=jnp.float32
    )
    gate_part = jax.nn.sigmoid(
        jnp.dot(flat_pair, tri_gate, preferred_element_type=jnp.float32)
    ).reshape(rows_here, cols_here, pair_width)
    return (pair_mid.astype(jnp.float32) + gate_part * update).astype(jnp.bfloat16)


def mul(a, b):
    return jnp.dot(a, b, preferred_element_type=F32)


def mul_t(a, b):
    return lax.dot_general(a, b, (((1,), (1,)), ((), ())), preferred_element_type=F32)


def ones_where(mask):
    return jnp.where(mask, 1.0, 0.0).astype(BF16)


def iotas(rows, cols):
    shape = (rows, cols)
    return lax.broadcasted_iota(jnp.int32, shape, 0), lax.broadcasted_iota(jnp.int32, shape, 1)


def identity(size):
    row, col = iotas(size, size)
    return ones_where(row == col)


def swap_rows(outer, inner):
    row, col = iotas(outer * inner, outer * inner)
    return ones_where(col == (row % outer) * inner + row // outer)


def normalize(values, axis):
    center = values - jnp.mean(values, axis=axis, keepdims=True)
    spread = jnp.mean(center * center, axis=axis, keepdims=True)
    return center * lax.rsqrt(spread + EPS)


def fetch(sems, pairs):
    copies = [
        pltpu.make_async_copy(source, target, sems.at[k]) for k, (source, target) in enumerate(pairs)
    ]
    for copy in copies:
        copy.start()
    return copies


def factors_kernel(sizes, align_in, left_in, right_in, *refs):
    n_far, n_near, n_core, rows, _ = sizes
    out_refs, (parts, align_ref, left_ref, right_ref, own_lane, picks, sems) = refs[:n_far], refs[n_far:]
    pairs = [(left_in, left_ref), (right_in, right_ref)]
    pairs += [(align_in, align_ref)]
    copies = fetch(sems, pairs)
    seqs, cols, width = align_ref.shape
    factor = left_ref.shape[0]
    chip_rows = n_core * rows
    row, col = iotas(chip_rows * factor, factor)
    widen = ones_where(row % factor == col)
    row, col = iotas(cols, chip_rows * factor)
    own_lane[...] = ones_where((row % chip_rows) == (col // factor))
    row, col = iotas(n_far * seqs * n_near, cols)
    chip_of_row = (row // (seqs * n_near)) * n_near + row % n_near
    chip_match = chip_of_row == col // chip_rows
    seq_of_row = (row // n_near) % seqs
    for n in range(seqs):
        picks[n] = ones_where(chip_match & (seq_of_row == n))
    copies[0].wait()
    copies[1].wait()
    left_wide = mul(widen, left_ref[...]).astype(BF16)
    right_rows, left_rows = [], None
    for n in range(seqs):
        if n == 0:
            copies[2].wait()
        normed = normalize(align_ref[n].astype(F32), 1).astype(BF16)
        right_rows.append(mul_t(right_ref[...], normed))
        spread = mul_t(normed, left_wide).astype(BF16) * own_lane[...]
        part = mul(picks[n], spread)
        left_rows = part if left_rows is None else left_rows + part
    right_block = jnp.concatenate(right_rows, 0).astype(BF16)
    part_rows = seqs * n_near
    pieces = n_core
    for far in range(n_far):
        for piece in range(pieces):
            parts[far, piece * part_rows : (piece + 1) * part_rows, :] = left_rows[
                far * part_rows : (far + 1) * part_rows, piece * cols : (piece + 1) * cols
            ].astype(BF16)
    here = lax.axis_index("row") // 2
    for k in range(n_far):
        out_refs[k][: seqs * factor, :] = right_block
        out_refs[k][seqs * factor :, :] = parts[here ^ k]


def near_index(n_near, n_core):
    return (lax.axis_index("row") % 2) * (n_near // 2) + lax.axis_index("seq") // n_core


def regroup(sizes, factor, seqs, blocks, out_refs):
    held = sizes[0] * seqs
    half = 256 // held
    shuffle = swap_rows(held, half)
    for h in range(factor // half):
        block = jnp.concatenate(
            [
                ref[at + n * factor + h * half : at + n * factor + (h + 1) * half, :]
                for ref, at in blocks
                for n in range(seqs)
            ],
            0,
        )
        block = mul(shuffle, block).astype(BF16)
        for ref in out_refs:
            ref[h * half * held : (h + 1) * half * held, :] = block


def regroup_kernel(sizes, factor, seqs, *refs):
    n_far, n_near, n_core, _, _ = sizes
    in_refs, out_refs, parts = refs[:n_far], refs[n_far : n_far + n_near], refs[-1]
    held, part_rows, base = n_far * seqs, seqs * n_near, seqs * factor
    regroup(sizes, factor, seqs, [(ref, 0) for ref in in_refs], out_refs[:-1])
    for far in range(1, n_far):
        out_refs[-1][(far - 1) * base : far * base, :] = in_refs[far][:base, :]
    pick = swap_rows(held, n_near)
    row, _ = iotas(held * n_near, held * n_near)
    pick_late = jnp.where(row % held < seqs, 0.0, pick.astype(F32)).astype(BF16)
    for piece in range(n_core):
        block = jnp.concatenate(
            [ref[base + piece * part_rows : base + (piece + 1) * part_rows, :] for ref in in_refs], 0
        )
        for late, matrix in enumerate((pick, pick_late)):
            rows = mul(matrix, block).astype(BF16)
            for near in range(n_near):
                parts[late, near, piece * held : (piece + 1) * held, :] = rows[
                    near * held : (near + 1) * held
                ]
    here = near_index(n_near, n_core)
    for k in range(n_near - 1):
        out_refs[k][factor * held :, :] = parts[0, here ^ k]
    out_refs[-1][(n_far - 1) * base :, :] = parts[1, here ^ (n_near - 1)]


def merge_kernel(sizes, factor, seqs, early_ref, late_ref, out_ref):
    n_far, n_near, n_core, _, _ = sizes
    held, part_rows, base = n_far * seqs, seqs * n_near, seqs * factor
    blocks = [(early_ref, 0)] + [(late_ref, far * base) for far in range(n_far - 1)]
    regroup(sizes, factor, seqs, blocks, [out_ref])
    row, col = iotas(n_core * held, n_core * part_rows)
    slot = row // held * part_rows + row % held * n_near + near_index(n_near, n_core)
    pick = ones_where((row % held < seqs) & (col == slot))
    own = mul(pick, early_ref[base:, :])
    out_ref[factor * held :, :] = (own + late_ref[(n_far - 1) * base :, :].astype(F32)).astype(BF16)


def prepare_kernel(factor, *refs):
    n = (len(refs) - 6) // 2
    sources, (pair_t, out_t, tri_t, gate_t, final_t), targets = refs[:n], refs[n : n + 5], refs[n + 5 : -1]
    copies = fetch(refs[-1], list(zip(sources, targets, strict=True)))
    pair_ref, out_w, *tri, gate_w, final_w = targets
    eye = identity(pair_ref.shape[2])
    for copy in copies:
        copy.wait()
    for i in range(pair_ref.shape[0]):
        pair_t[i] = mul_t(eye, pair_ref[i]).astype(BF16)
    shuffle = swap_rows(256 // 16, 16)
    for q in range(0, factor, 16):
        for p in range(0, factor, 256 // 16):
            block = jnp.concatenate(
                [
                    out_w[(p + k) * factor + q : (p + k) * factor + q + 16, :]
                    for k in range(256 // 16)
                ],
                0,
            )
            block = mul(shuffle, block).astype(BF16)
            block = mul_t(eye, block).astype(BF16)
            at = (q // 16 * (factor // 16) + p // 16) * 256
            out_t[:, at : at + 256] = block
    for k, ref in enumerate(tri):
        width = ref.shape[1]
        tri_t[k * width : (k + 1) * width, :] = mul_t(eye, ref[...]).astype(BF16)
    gate_t[...] = mul_t(eye, gate_w[...]).astype(BF16)
    final_t[...] = mul_t(eye, final_w[...]).astype(BF16)


def gate_kernel(norm_ref, gate_w, gate_ref):
    for i in range(norm_ref.shape[0]):
        gate_ref[i] = jax.nn.sigmoid(mul(gate_w[...], norm_ref[i]))


def pair_kernel(sizes, held, scale, *refs):
    n_core, rows, n_dev = sizes[2], sizes[3], sizes[4]
    groups = refs[:-8]
    pair_ref, out_w, tri_w, send_ref, mid_ref, norm_ref, outer, both = refs[-8:]
    factor = groups[0].shape[0] // held - n_core
    hidden = tri_w.shape[0] // 4
    core = lax.axis_index("seq") % n_core
    at = pl.multiple_of((factor + core) * held, held)
    left = jnp.concatenate([ref[pl.ds(at, held), :] for ref in groups], 0)
    left_t = mul_t(identity(rows * factor), left).astype(BF16)
    for q in range(factor):
        right = jnp.concatenate([ref[q * held : (q + 1) * held, :] for ref in groups], 0)
        block = mul(left_t, right).astype(BF16)
        for i in range(rows):
            for p in range(0, factor, 16):
                at = (q // 16 * (factor // 16) + p // 16) * 256 + q % 16 * 16
                outer[i, at : at + 16, :] = block[i * factor + p : i * factor + p + 16]
    updates = [mul(out_w[...], outer[i]) for i in range(rows)]
    for i in range(rows):
        update = updates[i]
        mid = (pair_ref[i].astype(F32) + update * scale).astype(BF16)
        mid_ref[i] = mid
        normed = normalize(mid.astype(F32), 0).astype(BF16)
        norm_ref[i] = normed
    for i in range(rows):
        parts = mul(tri_w[...], norm_ref[i])
        for side in range(2):
            at = 2 * side * hidden
            gate = jax.nn.sigmoid(parts[at : at + hidden])
            both[side, i] = (gate * parts[at + hidden : at + 2 * hidden]).astype(BF16)
    per = hidden // n_dev
    some = 256 // rows
    shuffle = swap_rows(rows, some)
    chunk = per * rows
    for side in range(2):
        for b in range(hidden // some):
            block = jnp.concatenate(
                [both[side, i, b * some : (b + 1) * some, :] for i in range(rows)], 0
            )
            block = mul(shuffle, block).astype(BF16)
            for d in range(some // per):
                to = ((b * some // per + d) * 2 + side) * chunk
                send_ref[to : to + chunk, :] = block[d * chunk : (d + 1) * chunk]


def product_kernel(sizes, per, recv_ref, send_ref, factors, total):
    rows, n_dev = sizes[3], sizes[4]
    chunk = per * rows
    for src in range(n_dev):
        for side in range(2):
            at = (src * 2 + side) * chunk
            block = recv_ref[at : at + chunk, :].astype(F32)
            for c in range(per):
                factors[side, c, src * rows : (src + 1) * rows, :] = block[c * rows : (c + 1) * rows]
    for c in range(per):
        prod = mul_t(factors[0, c].astype(BF16), factors[1, c].astype(BF16))
        for dst in range(n_dev):
            total[dst, c * rows : (c + 1) * rows, :] = prod[dst * rows : (dst + 1) * rows]
    for dst in range(n_dev):
        send_ref[dst * chunk : (dst + 1) * chunk, :] = total[dst].astype(BF16)


def finish_kernel(sizes, recv_ref, mid_ref, gate_ref, out_w, out_ref, apart, done_ref, sems):
    rows = sizes[3]
    _, width, cols = mid_ref.shape
    hidden = out_w.shape[1]
    some = 256 // rows
    blocks = hidden // some
    count = some * rows

    def piece(b):
        return recv_ref[b * count : (b + 1) * count, :].astype(F32).reshape(some, rows, cols)

    mean = sum(jnp.sum(piece(b), 0) for b in range(blocks)) * (1.0 / hidden)
    spread = sum(jnp.sum((piece(b) - mean) ** 2, 0) for b in range(blocks)) * (1.0 / hidden)
    factor = lax.rsqrt(spread + EPS)
    shuffle = swap_rows(some, rows)
    for b in range(blocks):
        normed = ((piece(b) - mean) * factor).reshape(count, cols).astype(BF16)
        normed = mul(shuffle, normed).astype(BF16)
        for i in range(rows):
            apart[i, b * some : (b + 1) * some, :] = normed[i * some : (i + 1) * some]
    eye = identity(cols)
    copies = []
    updates = [mul(out_w[...], apart[i]) for i in range(rows)]
    dones = [(mid_ref[i].astype(F32) + gate_ref[i] * updates[i]).astype(BF16) for i in range(rows)]
    for i in range(rows):
        done_ref[i] = mul_t(eye, dones[i]).astype(BF16)
        copies.append(pltpu.make_async_copy(done_ref.at[i], out_ref.at[i], sems.at[i]))
        copies[i].start()
    for copy in copies:
        copy.wait()


def call(kernel, out_shape, scratch, grant, flops, *args, far_in=False, far_out=False):
    spaces = [pltpu.HBM if far else pltpu.VMEM for far in (far_in, far_out)]
    place = jax.ShapeDtypeStruct if far_out else pltpu.VMEM
    out_shape = [place(*s) if isinstance(s[0], tuple) else place(s, BF16) for s in out_shape]
    if far_in:
        args = [pltpu.with_memory_space_constraint(a, pltpu.HBM) for a in args]
    moved = sum(math.prod(a.shape) * jnp.dtype(a.dtype).itemsize for a in (*args, *out_shape))
    return pl.pallas_call(
        kernel,
        out_shape=out_shape,
        in_specs=[pl.BlockSpec(memory_space=spaces[0])] * len(args),
        out_specs=[pl.BlockSpec(memory_space=spaces[1])] * len(out_shape),
        scratch_shapes=scratch,
        compiler_params=pltpu.CompilerParams(vmem_limit_bytes=grant * 2**20),
        cost_estimate=pl.CostEstimate(flops=flops, bytes_accessed=moved, transcendentals=0),
    )(*args)


def factors_call(sizes, alignment, opm_left, opm_right):
    n_far, n_near, n_core, rows, _ = sizes
    seqs, cols, width = alignment.shape
    factor = opm_left.shape[1]
    return call(
        functools.partial(factors_kernel, sizes),
        [(seqs * factor + n_core * seqs * n_near, cols)] * n_far,
        [
            pltpu.VMEM((n_far, n_core * seqs * n_near, cols), BF16),
            pltpu.VMEM(alignment.shape, BF16),
            pltpu.VMEM(opm_left.shape[::-1], BF16),
            pltpu.VMEM(opm_right.shape[::-1], BF16),
            pltpu.VMEM((cols, n_core * rows * factor), BF16),
            pltpu.VMEM((seqs, n_far * seqs * n_near, cols), BF16),
            pltpu.SemaphoreType.DMA((2 + seqs,)),
        ],
        8,
        4 * seqs * cols * width * factor,
        alignment,
        opm_left.T,
        opm_right.T,
        far_in=True,
    )


def whole_channels(
    pair,
    alignment,
    opm_left,
    opm_right,
    opm_out,
    tri_left,
    tri_left_gate,
    tri_right,
    tri_right_gate,
    tri_gate,
    tri_out,
):
    rows, cols, width = pair.shape
    seqs = alignment.shape[0]
    factor = opm_left.shape[1]
    hidden = tri_left.shape[1]
    n_row, n_seq = lax.axis_size("row"), lax.axis_size("seq")
    n_dev = n_row * n_seq
    n_core = 2
    n_far, n_near = n_row // 2, 2 * (n_seq // n_core)
    n_y = n_near // 2
    sizes = (n_far, n_near, n_core, rows, n_dev)
    held = n_far * seqs
    per = hidden // n_dev

    def exchange(value, row_bits, seq_bits):
        pairs = [
            (r * n_seq + s, (r ^ row_bits) * n_seq + (s ^ seq_bits))
            for r in range(n_row)
            for s in range(n_seq)
        ]
        return lax.ppermute(value, BOTH, pairs)

    mine = factors_call(sizes, alignment, opm_left, opm_right)
    weights = (
        pair,
        opm_out,
        tri_left_gate,
        tri_left,
        tri_right_gate,
        tri_right,
        tri_gate,
        tri_out,
    )
    mine, weights = lax.optimization_barrier((mine, weights))
    def to_near(value, k):
        return exchange(value, k // n_y, (k % n_y) * n_core)

    far = [exchange(mine[k], 2 * k, 0) for k in range(n_far - 1, 0, -1)]
    early = to_near(mine[0], n_near - 1)
    far = [mine[0]] + far
    prepared = call(
        functools.partial(prepare_kernel, factor),
        [
            (rows, width, cols),
            (width, factor * factor),
            (4 * hidden, width),
            (width, width),
            (width, hidden),
        ],
        [pltpu.VMEM(w.shape, BF16) for w in weights] + [pltpu.SemaphoreType.DMA((len(weights),))],
        8,
        4 * rows * cols * width * width,
        *weights,
        far_in=True,
    )
    far, early, prepared = lax.optimization_barrier((far, early, prepared))
    pair_t, out_t, tri_t, gate_t, final_t = prepared
    message = ((factor + n_core) * held, cols)
    late = ((n_far - 1) * seqs * factor + n_core * held, cols)
    mine = call(
        functools.partial(regroup_kernel, sizes, factor, seqs),
        [message] * (n_near - 1) + [late],
        [pltpu.VMEM((2, n_near, n_core * held, cols), BF16)],
        8,
        2 * 256 * factor * held * cols,
        *far,
    )
    near = [to_near(mine[k], k) for k in range(n_near - 1, 0, -1)]
    (near[0],) = call(
        functools.partial(merge_kernel, sizes, factor, seqs),
        [message],
        [],
        8,
        2 * 256 * factor * held * cols,
        early,
        near[0],
    )
    near = [mine[0]] + near
    groups = near + [exchange(block, 0, 1) for block in near]
    scale = 1.0 / (held * n_near * n_core)
    send, mid, normed = call(
        functools.partial(pair_kernel, sizes, held, scale),
        [(2 * hidden * rows, cols), (rows, width, cols), (rows, width, cols)],
        [
            pltpu.VMEM((rows, factor * factor, cols), BF16),
            pltpu.VMEM((2, rows, hidden, cols), BF16),
        ],
        16,
        4 * rows * cols * width * (factor * factor + hidden * 2),
        *groups,
        pair_t,
        out_t,
        tri_t,
    )
    (gate,) = call(
        gate_kernel,
        [((rows, width, cols), F32)],
        [],
        8,
        2 * rows * cols * width * width,
        normed,
        gate_t,
    )
    recv = lax.all_to_all(send, BOTH, split_axis=0, concat_axis=0, tiled=True)
    (send,) = call(
        functools.partial(product_kernel, sizes, per),
        [(hidden * rows, cols)],
        [
            pltpu.VMEM((2, per, rows * n_dev, cols), F32),
            pltpu.VMEM((n_dev, per * rows, cols), F32),
        ],
        16,
        2 * per * cols * cols * cols,
        recv,
    )
    recv = lax.all_to_all(send, BOTH, split_axis=0, concat_axis=0, tiled=True)
    (out,) = call(
        functools.partial(finish_kernel, sizes),
        [(rows, cols, width)],
        [
            pltpu.VMEM((rows, hidden, cols), BF16),
            pltpu.VMEM((rows, cols, width), BF16),
            pltpu.SemaphoreType.DMA((rows,)),
        ],
        16,
        4 * rows * cols * width * hidden,
        recv,
        mid,
        gate,
        final_t,
        far_out=True,
    )
    return out


def power_of_two(n):
    return n & (n - 1) == 0


def on_device(pair, alignment, opm_left, *rest):
    rows, cols, width = pair.shape
    factor, hidden = opm_left.shape[1], rest[2].shape[1]
    n_row, n_col, n_seq = (lax.axis_size(a) for a in ("row", "col", "seq"))
    n_dev = n_row * n_seq
    held = n_row // 2 * alignment.shape[0]
    fits = (
        n_col == 1
        and power_of_two(n_row)
        and power_of_two(n_seq)
        and power_of_two(rows)
        and n_row >= 4
        and n_seq >= 4
        and hidden % n_dev == 0
        and hidden == width
        and factor % 16 == 0
        and rows % 8 == 0
        and (hidden // n_dev * rows) % 16 == 0
        and cols % 256 == 0
        and rows * factor == cols
        and rows * n_dev == cols
        and held % 16 == 0
        and 256 % held == 0
        and factor % (256 // held) == 0
        and hidden % (256 // rows) == 0
        and power_of_two(held * n_seq * 2)
    )
    plan = whole_channels if fits else by_groups
    return plan(pair, alignment, opm_left, *rest)


def solution(mesh):
    return jax.shard_map(
        on_device,
        mesh=mesh,
        in_specs=(
            P(("row", "seq"), "col", None),
            P(("row", "seq"), "col", None),
            P(),
            P(),
            P(),
            P(),
            P(),
            P(),
            P(),
            P(),
            P(),
        ),
        out_specs=P(("row", "seq"), "col", None),
        check_vma=False,
    )
```

```python
import functools
import math

import jax
import jax.numpy as jnp
from jax import lax
from jax.experimental import pallas as pl
from jax.experimental.pallas import tpu as pltpu
from jax.sharding import PartitionSpec as P

EPS = 1e-05
BOTH = ("row", "seq")
BF16 = jnp.bfloat16
F32 = jnp.float32


def spread_2(shard, axis, root):
    mine = lax.axis_index(axis) == root
    return lax.psum(jnp.where(mine, shard, jnp.zeros_like(shard)), axis)


def layer_norm(values, axis):
    values = values.astype(jnp.float32)
    center = values - jnp.mean(values, axis=axis, keepdims=True)
    spread = jnp.mean(center * center, axis=axis, keepdims=True)
    return center * lax.rsqrt(spread + EPS)


def contract(local_rows, piece):
    return jnp.einsum("cik,cjk->cij", local_rows, piece, preferred_element_type=jnp.float32)


def by_groups(
    pair,
    alignment,
    opm_left,
    opm_right,
    opm_out,
    tri_left,
    tri_left_gate,
    tri_right,
    tri_right_gate,
    tri_gate,
    tri_out,
):
    rows_here, cols_here, pair_width = pair.shape
    seq_here = alignment.shape[0]
    model_width = alignment.shape[2]
    factor_width = opm_left.shape[1]
    hidden = tri_left.shape[1]
    n_row = lax.axis_size("row")
    n_col = lax.axis_size("col")
    n_seq = lax.axis_size("seq")
    seq_normed = (
        layer_norm(alignment, 2).astype(jnp.bfloat16).reshape(seq_here * cols_here, model_width)
    )
    left_proj = (
        jnp.dot(seq_normed, opm_left, preferred_element_type=jnp.float32)
        .astype(jnp.bfloat16)
        .reshape(seq_here, cols_here * factor_width)
    )
    right_proj = (
        jnp.dot(seq_normed, opm_right, preferred_element_type=jnp.float32)
        .astype(jnp.bfloat16)
        .reshape(seq_here, cols_here * factor_width)
    )
    per_col = n_row // n_col
    index_row = lax.axis_index("row")
    root_col = index_row // per_col
    right_all = lax.all_gather(right_proj, ("row", "seq"), axis=0, tiled=True)
    left_blocks = left_proj.reshape(seq_here, per_col * n_seq, rows_here * factor_width)
    left_send = jnp.tile(left_blocks, (1, n_col, 1))
    left_recv = lax.all_to_all(left_send, ("row", "seq"), split_axis=1, concat_axis=0, tiled=True)
    row_slice = left_recv.reshape(seq_here * n_row * n_seq, rows_here * factor_width)
    seqs_all = right_all.shape[0]
    row_factors = spread_2(row_slice, "col", root_col)
    right_wide = right_all.reshape(seqs_all, cols_here, factor_width)
    row_stack = jnp.swapaxes(row_factors.reshape(seqs_all, rows_here, factor_width), 0, 1)

    def outer_row(packed):
        row_vals, pair_row = packed
        outer_sum = jnp.einsum(
            "np,njq->jpq", row_vals, right_wide, preferred_element_type=jnp.float32
        )
        mean_outer = (
            (outer_sum * (1.0 / seqs_all))
            .astype(jnp.bfloat16)
            .reshape(cols_here, factor_width * factor_width)
        )
        return (
            pair_row.astype(jnp.float32)
            + jnp.dot(mean_outer, opm_out, preferred_element_type=jnp.float32)
        ).astype(jnp.bfloat16)

    pair_mid = lax.map(outer_row, (row_stack, pair))
    normed_pair = layer_norm(pair_mid, 2).astype(jnp.bfloat16)
    flat_pair = normed_pair.reshape(rows_here * cols_here, pair_width)

    def project(weight):
        return lax.dot_general(
            weight, flat_pair, (((0,), (1,)), ((), ())), preferred_element_type=jnp.float32
        )

    def gated(weight_gate, weight_value):
        gate_part = jax.nn.sigmoid(project(weight_gate))
        return (
            (gate_part * project(weight_value))
            .astype(jnp.bfloat16)
            .reshape(hidden, rows_here, cols_here)
        )

    left_first = gated(tri_left_gate, tri_left)
    right_first = gated(tri_right_gate, tri_right)
    left_local, right_local = (
        lax.all_to_all(
            lax.all_to_all(left_first, "col", split_axis=0, concat_axis=2, tiled=True),
            "seq",
            split_axis=0,
            concat_axis=1,
            tiled=True,
        ),
        lax.all_to_all(
            lax.all_to_all(right_first, "col", split_axis=0, concat_axis=2, tiled=True),
            "seq",
            split_axis=0,
            concat_axis=1,
            tiled=True,
        ),
    )
    product = contract(left_local, lax.all_gather(right_local, "row", axis=1, tiled=True))
    product = product.astype(jnp.bfloat16)
    returned = lax.all_to_all(
        lax.all_to_all(product, "col", split_axis=2, concat_axis=0, tiled=True),
        "seq",
        split_axis=1,
        concat_axis=0,
        tiled=True,
    )
    per_group = hidden // (n_col * n_seq)
    weights_order = (
        tri_out.reshape(n_col, n_seq, per_group, pair_width)
        .transpose(1, 0, 2, 3)
        .reshape(hidden, pair_width)
    )
    normed_product = layer_norm(returned, 0).astype(jnp.bfloat16)
    update = jnp.einsum(
        "cij,cd->ijd", normed_product, weights_order, preferred_element_type=jnp.float32
    )
    gate_part = jax.nn.sigmoid(
        jnp.dot(flat_pair, tri_gate, preferred_element_type=jnp.float32)
    ).reshape(rows_here, cols_here, pair_width)
    return (pair_mid.astype(jnp.float32) + gate_part * update).astype(jnp.bfloat16)


def mul(a, b):
    return jnp.dot(a, b, preferred_element_type=F32)


def mul_t(a, b):
    return lax.dot_general(a, b, (((1,), (1,)), ((), ())), preferred_element_type=F32)


def ones_where(mask):
    return jnp.where(mask, 1.0, 0.0).astype(BF16)


def iotas(rows, cols):
    shape = (rows, cols)
    return lax.broadcasted_iota(jnp.int32, shape, 0), lax.broadcasted_iota(jnp.int32, shape, 1)


def identity(size):
    row, col = iotas(size, size)
    return ones_where(row == col)


def swap_rows(outer, inner):
    row, col = iotas(outer * inner, outer * inner)
    return ones_where(col == (row % outer) * inner + row // outer)


def normalize(values, axis):
    center = values - jnp.mean(values, axis=axis, keepdims=True)
    spread = jnp.mean(center * center, axis=axis, keepdims=True)
    return center * lax.rsqrt(spread + EPS)


def fetch(sems, pairs):
    copies = [
        pltpu.make_async_copy(source, target, sems.at[k]) for k, (source, target) in enumerate(pairs)
    ]
    for copy in copies:
        copy.start()
    return copies


def factors_kernel(sizes, align_in, left_in, right_in, *refs):
    n_far, n_near, n_core, rows, _ = sizes
    out_refs, (parts, align_ref, left_ref, right_ref, own_lane, picks, sems) = refs[:n_far], refs[n_far:]
    pairs = [(left_in, left_ref), (right_in, right_ref)]
    pairs += [(align_in, align_ref)]
    copies = fetch(sems, pairs)
    seqs, cols, width = align_ref.shape
    factor = left_ref.shape[0]
    chip_rows = n_core * rows
    row, col = iotas(chip_rows * factor, factor)
    widen = ones_where(row % factor == col)
    row, col = iotas(cols, chip_rows * factor)
    own_lane[...] = ones_where((row % chip_rows) == (col // factor))
    row, col = iotas(n_far * seqs * n_near, cols)
    chip_of_row = (row // (seqs * n_near)) * n_near + row % n_near
    chip_match = chip_of_row == col // chip_rows
    seq_of_row = (row // n_near) % seqs
    for n in range(seqs):
        picks[n] = ones_where(chip_match & (seq_of_row == n))
    copies[0].wait()
    copies[1].wait()
    left_wide = mul(widen, left_ref[...]).astype(BF16)
    right_rows, left_rows = [], None
    for n in range(seqs):
        if n == 0:
            copies[2].wait()
        normed = normalize(align_ref[n].astype(F32), 1).astype(BF16)
        right_rows.append(mul_t(right_ref[...], normed))
        spread = mul_t(normed, left_wide).astype(BF16) * own_lane[...]
        part = mul(picks[n], spread)
        left_rows = part if left_rows is None else left_rows + part
    right_block = jnp.concatenate(right_rows, 0).astype(BF16)
    part_rows = seqs * n_near
    pieces = n_core
    for far in range(n_far):
        for piece in range(pieces):
            parts[far, piece * part_rows : (piece + 1) * part_rows, :] = left_rows[
                far * part_rows : (far + 1) * part_rows, piece * cols : (piece + 1) * cols
            ].astype(BF16)
    here = lax.axis_index("row") // 2
    for k in range(n_far):
        out_refs[k][: seqs * factor, :] = right_block
        out_refs[k][seqs * factor :, :] = parts[here ^ k]


def near_index(n_near, n_core):
    return (lax.axis_index("row") % 2) * (n_near // 2) + lax.axis_index("seq") // n_core


def regroup(sizes, factor, seqs, blocks, out_refs):
    held = sizes[0] * seqs
    half = 256 // held
    shuffle = swap_rows(held, half)
    for h in range(factor // half):
        block = jnp.concatenate(
            [
                ref[at + n * factor + h * half : at + n * factor + (h + 1) * half, :]
                for ref, at in blocks
                for n in range(seqs)
            ],
            0,
        )
        block = mul(shuffle, block).astype(BF16)
        for ref in out_refs:
            ref[h * half * held : (h + 1) * half * held, :] = block


def regroup_kernel(sizes, factor, seqs, *refs):
    n_far, n_near, n_core, _, _ = sizes
    in_refs, out_refs, parts = refs[:n_far], refs[n_far : n_far + n_near], refs[-1]
    held, part_rows, base = n_far * seqs, seqs * n_near, seqs * factor
    regroup(sizes, factor, seqs, [(ref, 0) for ref in in_refs], out_refs[:-1])
    for far in range(1, n_far):
        out_refs[-1][(far - 1) * base : far * base, :] = in_refs[far][:base, :]
    pick = swap_rows(held, n_near)
    row, _ = iotas(held * n_near, held * n_near)
    pick_late = jnp.where(row % held < seqs, 0.0, pick.astype(F32)).astype(BF16)
    for piece in range(n_core):
        block = jnp.concatenate(
            [ref[base + piece * part_rows : base + (piece + 1) * part_rows, :] for ref in in_refs], 0
        )
        for late, matrix in enumerate((pick, pick_late)):
            rows = mul(matrix, block).astype(BF16)
            for near in range(n_near):
                parts[late, near, piece * held : (piece + 1) * held, :] = rows[
                    near * held : (near + 1) * held
                ]
    here = near_index(n_near, n_core)
    for k in range(n_near - 1):
        out_refs[k][factor * held :, :] = parts[0, here ^ k]
    out_refs[-1][(n_far - 1) * base :, :] = parts[1, here ^ (n_near - 1)]


def merge_kernel(sizes, factor, seqs, early_ref, late_ref, out_ref):
    n_far, n_near, n_core, _, _ = sizes
    held, part_rows, base = n_far * seqs, seqs * n_near, seqs * factor
    blocks = [(early_ref, 0)] + [(late_ref, far * base) for far in range(n_far - 1)]
    regroup(sizes, factor, seqs, blocks, [out_ref])
    row, col = iotas(n_core * held, n_core * part_rows)
    slot = row // held * part_rows + row % held * n_near + near_index(n_near, n_core)
    pick = ones_where((row % held < seqs) & (col == slot))
    own = mul(pick, early_ref[base:, :])
    out_ref[factor * held :, :] = (own + late_ref[(n_far - 1) * base :, :].astype(F32)).astype(BF16)


def prepare_kernel(factor, *refs):
    n = (len(refs) - 6) // 2
    sources, (pair_t, out_t, tri_t, gate_t, final_t), targets = refs[:n], refs[n : n + 5], refs[n + 5 : -1]
    copies = fetch(refs[-1], list(zip(sources, targets, strict=True)))
    pair_ref, out_w, *tri, gate_w, final_w = targets
    eye = identity(pair_ref.shape[2])
    for copy in copies:
        copy.wait()
    for i in range(pair_ref.shape[0]):
        pair_t[i] = mul_t(eye, pair_ref[i]).astype(BF16)
    shuffle = swap_rows(256 // 16, 16)
    for q in range(0, factor, 16):
        for p in range(0, factor, 256 // 16):
            block = jnp.concatenate(
                [
                    out_w[(p + k) * factor + q : (p + k) * factor + q + 16, :]
                    for k in range(256 // 16)
                ],
                0,
            )
            block = mul(shuffle, block).astype(BF16)
            block = mul_t(eye, block).astype(BF16)
            at = (q // 16 * (factor // 16) + p // 16) * 256
            out_t[:, at : at + 256] = block
    for k, ref in enumerate(tri):
        width = ref.shape[1]
        tri_t[k * width : (k + 1) * width, :] = mul_t(eye, ref[...]).astype(BF16)
    gate_t[...] = mul_t(eye, gate_w[...]).astype(BF16)
    final_t[...] = mul_t(eye, final_w[...]).astype(BF16)


def gate_kernel(norm_ref, gate_w, gate_ref):
    for i in range(norm_ref.shape[0]):
        gate_ref[i] = jax.nn.sigmoid(mul(gate_w[...], norm_ref[i]))


def pair_kernel(sizes, held, scale, *refs):
    n_core, rows, n_dev = sizes[2], sizes[3], sizes[4]
    groups = refs[:-10]
    pair_ref, out_w, tri_w, send_ref, own_ref, other_ref, mid_ref, norm_ref, outer, both = refs[-10:]
    factor = groups[0].shape[0] // held - n_core
    hidden = tri_w.shape[0] // 4
    core = lax.axis_index("seq") % n_core
    at = pl.multiple_of((factor + core) * held, held)
    left = jnp.concatenate([ref[pl.ds(at, held), :] for ref in groups], 0)
    left_t = mul_t(identity(rows * factor), left).astype(BF16)
    for q in range(factor):
        right = jnp.concatenate([ref[q * held : (q + 1) * held, :] for ref in groups], 0)
        block = mul(left_t, right).astype(BF16)
        for i in range(rows):
            for p in range(0, factor, 16):
                at = (q // 16 * (factor // 16) + p // 16) * 256 + q % 16 * 16
                outer[i, at : at + 16, :] = block[i * factor + p : i * factor + p + 16]
    updates = [mul(out_w[...], outer[i]) for i in range(rows)]
    for i in range(rows):
        update = updates[i]
        mid = (pair_ref[i].astype(F32) + update * scale).astype(BF16)
        mid_ref[i] = mid
        normed = normalize(mid.astype(F32), 0).astype(BF16)
        norm_ref[i] = normed
    for i in range(rows):
        parts = mul(tri_w[...], norm_ref[i])
        for side in range(2):
            at = 2 * side * hidden
            gate = jax.nn.sigmoid(parts[at : at + hidden])
            both[side, i] = (gate * parts[at + hidden : at + 2 * hidden]).astype(BF16)
    half = n_dev // 2
    chunk = hidden // half * rows
    some = 256 // rows
    shuffle = swap_rows(rows, some)
    per = some * rows // chunk
    for b in range(hidden // some):
        left, right = (
            mul(
                shuffle,
                jnp.concatenate(
                    [both[side, i, b * some : (b + 1) * some, :] for i in range(rows)], 0
                ),
            ).astype(BF16)
            for side in range(2)
        )
        for d in range(per):
            for side in range(2):
                to = (side * half + b * per + d) * chunk
                send_ref[to : to + chunk, :] = right[d * chunk : (d + 1) * chunk]
        for d in range(0, per, n_core):
            to = (b * per + d) // n_core * chunk
            even = left[d * chunk : (d + 1) * chunk]
            odd = left[(d + 1) * chunk : (d + 2) * chunk]
            own_ref[to : to + chunk, :] = jnp.where(core == 0, even, odd)
            other_ref[to : to + chunk, :] = jnp.where(core == 0, odd, even)


def half_index(sizes):
    n_far, n_near, n_core, _, _ = sizes
    n_y = n_near // 2
    row = lax.axis_index("row") % n_far
    return row * n_y + lax.axis_index("seq") // n_core


def left_kernel(sizes, own_ref, came_ref, *out_refs):
    n_core = sizes[2]
    chunk = own_ref.shape[0] // len(out_refs)
    core = lax.axis_index("seq") % n_core
    here = half_index(sizes)
    own_at = pl.multiple_of(core * chunk, chunk)
    came_at = pl.multiple_of((1 - core) * chunk, chunk)
    for k, ref in enumerate(out_refs):
        at = pl.multiple_of((here ^ k) * chunk, chunk)
        ref[pl.ds(own_at, chunk), :] = own_ref[pl.ds(at, chunk), :]
        ref[pl.ds(came_at, chunk), :] = came_ref[pl.ds(at, chunk), :]


def product_kernel(sizes, per, recv_ref, *refs):
    n_core, rows, n_dev = sizes[2], sizes[3], sizes[4]
    half, chunk = n_dev // 2, per * rows
    chips = half // n_core
    left_refs, (send_ref, left, right, total) = refs[:chips], refs[chips:]
    here = half_index(sizes)
    for src in range(n_dev):
        block = recv_ref[src * chunk : (src + 1) * chunk, :].astype(F32)
        for c in range(per):
            right[c, src * rows : (src + 1) * rows, :] = block[c * rows : (c + 1) * rows]
    for k, ref in enumerate(left_refs):
        for core in range(n_core):
            block = ref[core * chunk : (core + 1) * chunk, :].astype(F32)
            at = pl.multiple_of(((here ^ k) * n_core + core) * rows, rows)
            for c in range(per):
                left[c, pl.ds(at, rows), :] = block[c * rows : (c + 1) * rows]
    for c in range(per):
        prod = mul_t(left[c].astype(BF16), right[c].astype(BF16))
        for dst in range(half):
            total[dst, c * rows : (c + 1) * rows, :] = prod[dst * rows : (dst + 1) * rows]
    for dst in range(half):
        send_ref[dst * chunk : (dst + 1) * chunk, :] = total[dst].astype(BF16)


def finish_kernel(sizes, recv_ref, mid_ref, gate_ref, out_w, out_ref, apart, done_ref, sems):
    rows = sizes[3]
    _, width, cols = mid_ref.shape
    hidden = out_w.shape[1]
    some = 256 // rows
    blocks = hidden // some
    count = some * rows

    def piece(b):
        return recv_ref[b * count : (b + 1) * count, :].astype(F32).reshape(some, rows, cols)

    mean = sum(jnp.sum(piece(b), 0) for b in range(blocks)) * (1.0 / hidden)
    spread = sum(jnp.sum((piece(b) - mean) ** 2, 0) for b in range(blocks)) * (1.0 / hidden)
    factor = lax.rsqrt(spread + EPS)
    shuffle = swap_rows(some, rows)
    for b in range(blocks):
        normed = ((piece(b) - mean) * factor).reshape(count, cols).astype(BF16)
        normed = mul(shuffle, normed).astype(BF16)
        for i in range(rows):
            apart[i, b * some : (b + 1) * some, :] = normed[i * some : (i + 1) * some]
    eye = identity(cols)
    copies = []
    updates = [mul(out_w[...], apart[i]) for i in range(rows)]
    dones = [(mid_ref[i].astype(F32) + gate_ref[i] * updates[i]).astype(BF16) for i in range(rows)]
    for i in range(rows):
        done_ref[i] = mul_t(eye, dones[i]).astype(BF16)
        copies.append(pltpu.make_async_copy(done_ref.at[i], out_ref.at[i], sems.at[i]))
        copies[i].start()
    for copy in copies:
        copy.wait()


def call(kernel, out_shape, scratch, grant, flops, *args, far_in=False, far_out=False):
    spaces = [pltpu.HBM if far else pltpu.VMEM for far in (far_in, far_out)]
    place = jax.ShapeDtypeStruct if far_out else pltpu.VMEM
    out_shape = [place(*s) if isinstance(s[0], tuple) else place(s, BF16) for s in out_shape]
    if far_in:
        args = [pltpu.with_memory_space_constraint(a, pltpu.HBM) for a in args]
    moved = sum(math.prod(a.shape) * jnp.dtype(a.dtype).itemsize for a in (*args, *out_shape))
    return pl.pallas_call(
        kernel,
        out_shape=out_shape,
        in_specs=[pl.BlockSpec(memory_space=spaces[0])] * len(args),
        out_specs=[pl.BlockSpec(memory_space=spaces[1])] * len(out_shape),
        scratch_shapes=scratch,
        compiler_params=pltpu.CompilerParams(vmem_limit_bytes=grant * 2**20),
        cost_estimate=pl.CostEstimate(flops=flops, bytes_accessed=moved, transcendentals=0),
    )(*args)


def factors_call(sizes, alignment, opm_left, opm_right):
    n_far, n_near, n_core, rows, _ = sizes
    seqs, cols, width = alignment.shape
    factor = opm_left.shape[1]
    return call(
        functools.partial(factors_kernel, sizes),
        [(seqs * factor + n_core * seqs * n_near, cols)] * n_far,
        [
            pltpu.VMEM((n_far, n_core * seqs * n_near, cols), BF16),
            pltpu.VMEM(alignment.shape, BF16),
            pltpu.VMEM(opm_left.shape[::-1], BF16),
            pltpu.VMEM(opm_right.shape[::-1], BF16),
            pltpu.VMEM((cols, n_core * rows * factor), BF16),
            pltpu.VMEM((seqs, n_far * seqs * n_near, cols), BF16),
            pltpu.SemaphoreType.DMA((2 + seqs,)),
        ],
        8,
        4 * seqs * cols * width * factor,
        alignment,
        opm_left.T,
        opm_right.T,
        far_in=True,
    )


def whole_channels(
    pair,
    alignment,
    opm_left,
    opm_right,
    opm_out,
    tri_left,
    tri_left_gate,
    tri_right,
    tri_right_gate,
    tri_gate,
    tri_out,
):
    rows, cols, width = pair.shape
    seqs = alignment.shape[0]
    factor = opm_left.shape[1]
    hidden = tri_left.shape[1]
    n_row, n_seq = lax.axis_size("row"), lax.axis_size("seq")
    n_dev = n_row * n_seq
    n_core = 2
    n_far, n_near = n_row // 2, 2 * (n_seq // n_core)
    n_y = n_near // 2
    sizes = (n_far, n_near, n_core, rows, n_dev)
    held = n_far * seqs
    half = n_dev // 2
    per = hidden // half
    chips = half // n_core

    def exchange(value, row_bits, seq_bits):
        pairs = [
            (r * n_seq + s, (r ^ row_bits) * n_seq + (s ^ seq_bits))
            for r in range(n_row)
            for s in range(n_seq)
        ]
        return lax.ppermute(value, BOTH, pairs)

    mine = factors_call(sizes, alignment, opm_left, opm_right)
    weights = (
        pair,
        opm_out,
        tri_left_gate,
        tri_left,
        tri_right_gate,
        tri_right,
        tri_gate,
        tri_out,
    )
    mine, weights = lax.optimization_barrier((mine, weights))
    def to_near(value, k):
        return exchange(value, k // n_y, (k % n_y) * n_core)

    far = [exchange(mine[k], 2 * k, 0) for k in range(n_far - 1, 0, -1)]
    early = to_near(mine[0], n_near - 1)
    far = [mine[0]] + far
    prepared = call(
        functools.partial(prepare_kernel, factor),
        [
            (rows, width, cols),
            (width, factor * factor),
            (4 * hidden, width),
            (width, width),
            (width, hidden),
        ],
        [pltpu.VMEM(w.shape, BF16) for w in weights] + [pltpu.SemaphoreType.DMA((len(weights),))],
        8,
        4 * rows * cols * width * width,
        *weights,
        far_in=True,
    )
    far, early, prepared = lax.optimization_barrier((far, early, prepared))
    pair_t, out_t, tri_t, gate_t, final_t = prepared
    message = ((factor + n_core) * held, cols)
    late = ((n_far - 1) * seqs * factor + n_core * held, cols)
    mine = call(
        functools.partial(regroup_kernel, sizes, factor, seqs),
        [message] * (n_near - 1) + [late],
        [pltpu.VMEM((2, n_near, n_core * held, cols), BF16)],
        8,
        2 * 256 * factor * held * cols,
        *far,
    )
    near = [to_near(mine[k], k) for k in range(n_near - 1, 0, -1)]
    (near[0],) = call(
        functools.partial(merge_kernel, sizes, factor, seqs),
        [message],
        [],
        8,
        2 * 256 * factor * held * cols,
        early,
        near[0],
    )
    near = [mine[0]] + near
    groups = near + [exchange(block, 0, 1) for block in near]
    scale = 1.0 / (held * n_near * n_core)
    send, own, other, mid, normed = call(
        functools.partial(pair_kernel, sizes, held, scale),
        [
            (2 * hidden * rows, cols),
            (chips * per * rows, cols),
            (chips * per * rows, cols),
            (rows, width, cols),
            (rows, width, cols),
        ],
        [
            pltpu.VMEM((rows, factor * factor, cols), BF16),
            pltpu.VMEM((2, rows, hidden, cols), BF16),
        ],
        16,
        4 * rows * cols * width * (factor * factor + hidden * 2),
        *groups,
        pair_t,
        out_t,
        tri_t,
    )
    (gate,) = call(
        gate_kernel,
        [((rows, width, cols), F32)],
        [],
        8,
        2 * rows * cols * width * width,
        normed,
        gate_t,
    )
    recv = lax.all_to_all(send, BOTH, split_axis=0, concat_axis=0, tiled=True)
    mine = call(
        functools.partial(left_kernel, sizes),
        [(n_core * per * rows, cols)] * chips,
        [],
        8,
        0,
        own,
        exchange(other, 0, 1),
    )
    lefts = [mine[0]]
    for k in range(1, chips):
        lefts.append(exchange(mine[k], k // n_y, k % n_y * n_core))
    (send,) = call(
        functools.partial(product_kernel, sizes, per),
        [(hidden * rows, cols)],
        [
            pltpu.VMEM((per, rows * half, cols), F32),
            pltpu.VMEM((per, rows * n_dev, cols), F32),
            pltpu.VMEM((half, per * rows, cols), F32),
        ],
        16,
        2 * per * cols * cols * cols // 2,
        recv,
        *lefts,
    )
    halves = [list(range(half)), list(range(half, n_dev))]
    recv = lax.all_to_all(
        send, BOTH, split_axis=0, concat_axis=0, tiled=True, axis_index_groups=halves
    )
    (out,) = call(
        functools.partial(finish_kernel, sizes),
        [(rows, cols, width)],
        [
            pltpu.VMEM((rows, hidden, cols), BF16),
            pltpu.VMEM((rows, cols, width), BF16),
            pltpu.SemaphoreType.DMA((rows,)),
        ],
        16,
        4 * rows * cols * width * hidden,
        recv,
        mid,
        gate,
        final_t,
        far_out=True,
    )
    return out


def power_of_two(n):
    return n & (n - 1) == 0


def on_device(pair, alignment, opm_left, *rest):
    rows, cols, width = pair.shape
    factor, hidden = opm_left.shape[1], rest[2].shape[1]
    n_row, n_col, n_seq = (lax.axis_size(a) for a in ("row", "col", "seq"))
    n_dev = n_row * n_seq
    held = n_row // 2 * alignment.shape[0]
    fits = (
        n_col == 1
        and power_of_two(n_row)
        and power_of_two(n_seq)
        and power_of_two(rows)
        and n_row >= 4
        and n_seq >= 4
        and hidden % n_dev == 0
        and hidden == width
        and factor % 16 == 0
        and rows % 8 == 0
        and (hidden // n_dev * rows) % 16 == 0
        and cols % 256 == 0
        and rows * factor == cols
        and rows * n_dev == cols
        and held % 16 == 0
        and 256 % held == 0
        and factor % (256 // held) == 0
        and hidden % (256 // rows) == 0
        and power_of_two(held * n_seq * 2)
    )
    plan = whole_channels if fits else by_groups
    return plan(pair, alignment, opm_left, *rest)


def solution(mesh):
    return jax.shard_map(
        on_device,
        mesh=mesh,
        in_specs=(
            P(("row", "seq"), "col", None),
            P(("row", "seq"), "col", None),
            P(),
            P(),
            P(),
            P(),
            P(),
            P(),
            P(),
            P(),
            P(),
        ),
        out_specs=P(("row", "seq"), "col", None),
        check_vma=False,
    )
```

```python
import functools
import math

import jax
import jax.numpy as jnp
from jax import lax
from jax.experimental import pallas as pl
from jax.experimental.pallas import tpu as pltpu
from jax.sharding import PartitionSpec as P

EPS = 1e-05
BOTH = ("row", "seq")
BF16 = jnp.bfloat16
F32 = jnp.float32


def spread_2(shard, axis, root):
    mine = lax.axis_index(axis) == root
    return lax.psum(jnp.where(mine, shard, jnp.zeros_like(shard)), axis)


def layer_norm(values, axis):
    values = values.astype(jnp.float32)
    center = values - jnp.mean(values, axis=axis, keepdims=True)
    spread = jnp.mean(center * center, axis=axis, keepdims=True)
    return center * lax.rsqrt(spread + EPS)


def contract(local_rows, piece):
    return jnp.einsum("cik,cjk->cij", local_rows, piece, preferred_element_type=jnp.float32)


def by_groups(
    pair,
    alignment,
    opm_left,
    opm_right,
    opm_out,
    tri_left,
    tri_left_gate,
    tri_right,
    tri_right_gate,
    tri_gate,
    tri_out,
):
    rows_here, cols_here, pair_width = pair.shape
    seq_here = alignment.shape[0]
    model_width = alignment.shape[2]
    factor_width = opm_left.shape[1]
    hidden = tri_left.shape[1]
    n_row = lax.axis_size("row")
    n_col = lax.axis_size("col")
    n_seq = lax.axis_size("seq")
    seq_normed = (
        layer_norm(alignment, 2).astype(jnp.bfloat16).reshape(seq_here * cols_here, model_width)
    )
    left_proj = (
        jnp.dot(seq_normed, opm_left, preferred_element_type=jnp.float32)
        .astype(jnp.bfloat16)
        .reshape(seq_here, cols_here * factor_width)
    )
    right_proj = (
        jnp.dot(seq_normed, opm_right, preferred_element_type=jnp.float32)
        .astype(jnp.bfloat16)
        .reshape(seq_here, cols_here * factor_width)
    )
    per_col = n_row // n_col
    index_row = lax.axis_index("row")
    root_col = index_row // per_col
    right_all = lax.all_gather(right_proj, ("row", "seq"), axis=0, tiled=True)
    left_blocks = left_proj.reshape(seq_here, per_col * n_seq, rows_here * factor_width)
    left_send = jnp.tile(left_blocks, (1, n_col, 1))
    left_recv = lax.all_to_all(left_send, ("row", "seq"), split_axis=1, concat_axis=0, tiled=True)
    row_slice = left_recv.reshape(seq_here * n_row * n_seq, rows_here * factor_width)
    seqs_all = right_all.shape[0]
    row_factors = spread_2(row_slice, "col", root_col)
    right_wide = right_all.reshape(seqs_all, cols_here, factor_width)
    row_stack = jnp.swapaxes(row_factors.reshape(seqs_all, rows_here, factor_width), 0, 1)

    def outer_row(packed):
        row_vals, pair_row = packed
        outer_sum = jnp.einsum(
            "np,njq->jpq", row_vals, right_wide, preferred_element_type=jnp.float32
        )
        mean_outer = (
            (outer_sum * (1.0 / seqs_all))
            .astype(jnp.bfloat16)
            .reshape(cols_here, factor_width * factor_width)
        )
        return (
            pair_row.astype(jnp.float32)
            + jnp.dot(mean_outer, opm_out, preferred_element_type=jnp.float32)
        ).astype(jnp.bfloat16)

    pair_mid = lax.map(outer_row, (row_stack, pair))
    normed_pair = layer_norm(pair_mid, 2).astype(jnp.bfloat16)
    flat_pair = normed_pair.reshape(rows_here * cols_here, pair_width)

    def project(weight):
        return lax.dot_general(
            weight, flat_pair, (((0,), (1,)), ((), ())), preferred_element_type=jnp.float32
        )

    def gated(weight_gate, weight_value):
        gate_part = jax.nn.sigmoid(project(weight_gate))
        return (
            (gate_part * project(weight_value))
            .astype(jnp.bfloat16)
            .reshape(hidden, rows_here, cols_here)
        )

    left_first = gated(tri_left_gate, tri_left)
    right_first = gated(tri_right_gate, tri_right)
    left_local, right_local = (
        lax.all_to_all(
            lax.all_to_all(left_first, "col", split_axis=0, concat_axis=2, tiled=True),
            "seq",
            split_axis=0,
            concat_axis=1,
            tiled=True,
        ),
        lax.all_to_all(
            lax.all_to_all(right_first, "col", split_axis=0, concat_axis=2, tiled=True),
            "seq",
            split_axis=0,
            concat_axis=1,
            tiled=True,
        ),
    )
    product = contract(left_local, lax.all_gather(right_local, "row", axis=1, tiled=True))
    product = product.astype(jnp.bfloat16)
    returned = lax.all_to_all(
        lax.all_to_all(product, "col", split_axis=2, concat_axis=0, tiled=True),
        "seq",
        split_axis=1,
        concat_axis=0,
        tiled=True,
    )
    per_group = hidden // (n_col * n_seq)
    weights_order = (
        tri_out.reshape(n_col, n_seq, per_group, pair_width)
        .transpose(1, 0, 2, 3)
        .reshape(hidden, pair_width)
    )
    normed_product = layer_norm(returned, 0).astype(jnp.bfloat16)
    update = jnp.einsum(
        "cij,cd->ijd", normed_product, weights_order, preferred_element_type=jnp.float32
    )
    gate_part = jax.nn.sigmoid(
        jnp.dot(flat_pair, tri_gate, preferred_element_type=jnp.float32)
    ).reshape(rows_here, cols_here, pair_width)
    return (pair_mid.astype(jnp.float32) + gate_part * update).astype(jnp.bfloat16)


def mul(a, b):
    return jnp.dot(a, b, preferred_element_type=F32)


def mul_t(a, b):
    return lax.dot_general(a, b, (((1,), (1,)), ((), ())), preferred_element_type=F32)


def ones_where(mask):
    return jnp.where(mask, 1.0, 0.0).astype(BF16)


def iotas(rows, cols):
    shape = (rows, cols)
    return lax.broadcasted_iota(jnp.int32, shape, 0), lax.broadcasted_iota(jnp.int32, shape, 1)


def identity(size):
    row, col = iotas(size, size)
    return ones_where(row == col)


def swap_rows(outer, inner):
    row, col = iotas(outer * inner, outer * inner)
    return ones_where(col == (row % outer) * inner + row // outer)


def normalize(values, axis):
    center = values - jnp.mean(values, axis=axis, keepdims=True)
    spread = jnp.mean(center * center, axis=axis, keepdims=True)
    return center * lax.rsqrt(spread + EPS)


def fetch(sems, pairs):
    copies = [
        pltpu.make_async_copy(source, target, sems.at[k]) for k, (source, target) in enumerate(pairs)
    ]
    for copy in copies:
        copy.start()
    return copies


def factors_kernel(sizes, align_in, left_in, right_in, *refs):
    n_far, n_near, n_core, rows, _ = sizes
    out_refs, (parts, align_ref, left_ref, right_ref, own_lane, picks, sems) = refs[:n_far], refs[n_far:]
    pairs = [(left_in, left_ref), (right_in, right_ref)]
    pairs += [(align_in, align_ref)]
    copies = fetch(sems, pairs)
    seqs, cols, width = align_ref.shape
    factor = left_ref.shape[0]
    chip_rows = n_core * rows
    row, col = iotas(chip_rows * factor, factor)
    widen = ones_where(row % factor == col)
    row, col = iotas(cols, chip_rows * factor)
    own_lane[...] = ones_where((row % chip_rows) == (col // factor))
    row, col = iotas(n_far * seqs * n_near, cols)
    chip_of_row = (row // (seqs * n_near)) * n_near + row % n_near
    chip_match = chip_of_row == col // chip_rows
    seq_of_row = (row // n_near) % seqs
    for n in range(seqs):
        picks[n] = ones_where(chip_match & (seq_of_row == n))
    copies[0].wait()
    copies[1].wait()
    left_wide = mul(widen, left_ref[...]).astype(BF16)
    right_rows, left_rows = [], None
    for n in range(seqs):
        if n == 0:
            copies[2].wait()
        normed = normalize(align_ref[n].astype(F32), 1).astype(BF16)
        right_rows.append(mul_t(right_ref[...], normed))
        spread = mul_t(normed, left_wide).astype(BF16) * own_lane[...]
        part = mul(picks[n], spread)
        left_rows = part if left_rows is None else left_rows + part
    right_block = jnp.concatenate(right_rows, 0).astype(BF16)
    part_rows = seqs * n_near
    pieces = n_core
    for far in range(n_far):
        for piece in range(pieces):
            parts[far, piece * part_rows : (piece + 1) * part_rows, :] = left_rows[
                far * part_rows : (far + 1) * part_rows, piece * cols : (piece + 1) * cols
            ].astype(BF16)
    here = lax.axis_index("row") // 2
    for k in range(n_far):
        out_refs[k][: seqs * factor, :] = right_block
        out_refs[k][seqs * factor :, :] = parts[here ^ k]


def near_index(n_near, n_core):
    return (lax.axis_index("row") % 2) * (n_near // 2) + lax.axis_index("seq") // n_core


def regroup(sizes, factor, seqs, blocks, out_refs):
    held = sizes[0] * seqs
    half = 256 // held
    shuffle = swap_rows(held, half)
    for h in range(factor // half):
        block = jnp.concatenate(
            [
                ref[at + n * factor + h * half : at + n * factor + (h + 1) * half, :]
                for ref, at in blocks
                for n in range(seqs)
            ],
            0,
        )
        block = mul(shuffle, block).astype(BF16)
        for ref in out_refs:
            ref[h * half * held : (h + 1) * half * held, :] = block


def regroup_kernel(sizes, factor, seqs, *refs):
    n_far, n_near, n_core, _, _ = sizes
    in_refs, out_refs, parts = refs[:n_far], refs[n_far : n_far + n_near], refs[-1]
    held, part_rows, base = n_far * seqs, seqs * n_near, seqs * factor
    regroup(sizes, factor, seqs, [(ref, 0) for ref in in_refs], out_refs[:-1])
    for far in range(1, n_far):
        out_refs[-1][(far - 1) * base : far * base, :] = in_refs[far][:base, :]
    pick = swap_rows(held, n_near)
    row, _ = iotas(held * n_near, held * n_near)
    pick_late = jnp.where(row % held < seqs, 0.0, pick.astype(F32)).astype(BF16)
    for piece in range(n_core):
        block = jnp.concatenate(
            [ref[base + piece * part_rows : base + (piece + 1) * part_rows, :] for ref in in_refs], 0
        )
        for late, matrix in enumerate((pick, pick_late)):
            rows = mul(matrix, block).astype(BF16)
            for near in range(n_near):
                parts[late, near, piece * held : (piece + 1) * held, :] = rows[
                    near * held : (near + 1) * held
                ]
    here = near_index(n_near, n_core)
    for k in range(n_near - 1):
        out_refs[k][factor * held :, :] = parts[0, here ^ k]
    out_refs[-1][(n_far - 1) * base :, :] = parts[1, here ^ (n_near - 1)]


def merge_kernel(sizes, factor, seqs, early_ref, late_ref, out_ref):
    n_far, n_near, n_core, _, _ = sizes
    held, part_rows, base = n_far * seqs, seqs * n_near, seqs * factor
    blocks = [(early_ref, 0)] + [(late_ref, far * base) for far in range(n_far - 1)]
    regroup(sizes, factor, seqs, blocks, [out_ref])
    row, col = iotas(n_core * held, n_core * part_rows)
    slot = row // held * part_rows + row % held * n_near + near_index(n_near, n_core)
    pick = ones_where((row % held < seqs) & (col == slot))
    own = mul(pick, early_ref[base:, :])
    out_ref[factor * held :, :] = (own + late_ref[(n_far - 1) * base :, :].astype(F32)).astype(BF16)


def prepare_kernel(factor, *refs):
    n = (len(refs) - 6) // 2
    sources, (pair_t, out_t, tri_t, gate_t, final_t), targets = refs[:n], refs[n : n + 5], refs[n + 5 : -1]
    copies = fetch(refs[-1], list(zip(sources, targets, strict=True)))
    pair_ref, out_w, *tri, gate_w, final_w = targets
    eye = identity(pair_ref.shape[2])
    for copy in copies:
        copy.wait()
    for i in range(pair_ref.shape[0]):
        pair_t[i] = mul_t(eye, pair_ref[i]).astype(BF16)
    shuffle = swap_rows(256 // 16, 16)
    for q in range(0, factor, 16):
        for p in range(0, factor, 256 // 16):
            block = jnp.concatenate(
                [
                    out_w[(p + k) * factor + q : (p + k) * factor + q + 16, :]
                    for k in range(256 // 16)
                ],
                0,
            )
            block = mul(shuffle, block).astype(BF16)
            block = mul_t(eye, block).astype(BF16)
            at = (q // 16 * (factor // 16) + p // 16) * 256
            out_t[:, at : at + 256] = block
    for k, ref in enumerate(tri):
        width = ref.shape[1]
        tri_t[k * width : (k + 1) * width, :] = mul_t(eye, ref[...]).astype(BF16)
    gate_t[...] = mul_t(eye, gate_w[...]).astype(BF16)
    final_t[...] = mul_t(eye, final_w[...]).astype(BF16)


def gate_kernel(norm_ref, gate_w, gate_ref):
    for i in range(norm_ref.shape[0]):
        gate_ref[i] = jax.nn.sigmoid(mul(gate_w[...], norm_ref[i]))


def pair_kernel(sizes, held, scale, *refs):
    n_core, rows, n_dev = sizes[2], sizes[3], sizes[4]
    groups = refs[:-11]
    pair_ref, out_w, tri_w, send_ref, left_ref, mid_ref, norm_ref, outer, both, right_ref, sems = refs[-11:]
    factor = groups[0].shape[0] // held - n_core
    hidden = tri_w.shape[0] // 4
    core = lax.axis_index("seq") % n_core
    at = pl.multiple_of((factor + core) * held, held)
    left = jnp.concatenate([ref[pl.ds(at, held), :] for ref in groups], 0)
    left_t = mul_t(identity(rows * factor), left).astype(BF16)
    for q in range(factor):
        right = jnp.concatenate([ref[q * held : (q + 1) * held, :] for ref in groups], 0)
        block = mul(left_t, right).astype(BF16)
        for i in range(rows):
            for p in range(0, factor, 16):
                at = (q // 16 * (factor // 16) + p // 16) * 256 + q % 16 * 16
                outer[i, at : at + 16, :] = block[i * factor + p : i * factor + p + 16]
    updates = [mul(out_w[...], outer[i]) for i in range(rows)]
    for i in range(rows):
        update = updates[i]
        mid = (pair_ref[i].astype(F32) + update * scale).astype(BF16)
        mid_ref[i] = mid
        normed = normalize(mid.astype(F32), 0).astype(BF16)
        norm_ref[i] = normed
    half = n_dev // 2
    chunk = hidden // half * rows
    some = 256 // rows
    shuffle = swap_rows(rows, some)
    per = some * rows // chunk

    def by_channels(side):
        at = 2 * side * hidden
        for i in range(rows):
            parts = mul(tri_w[at : at + 2 * hidden, :], norm_ref[i])
            both[side, i] = (jax.nn.sigmoid(parts[:hidden]) * parts[hidden:]).astype(BF16)
        blocks = [
            jnp.concatenate([both[side, i, b * some : (b + 1) * some, :] for i in range(rows)], 0)
            for b in range(hidden // some)
        ]
        return [mul(shuffle, block).astype(BF16) for block in blocks]

    for b, block in enumerate(by_channels(1)):
        right_ref[b * per * chunk : (b + 1) * per * chunk, :] = block
    targets = [send_ref.at[pl.ds(h * half * chunk, half * chunk)] for h in range(2)]
    copies = fetch(sems, [(right_ref, target) for target in targets])
    for b, block in enumerate(by_channels(0)):
        for d in range(per):
            to = (d % n_core * half + b * per + d) // n_core * chunk
            left_ref[to : to + chunk, :] = block[d * chunk : (d + 1) * chunk]
    for copy in copies:
        copy.wait()


def half_index(sizes):
    n_far, n_near, n_core, _, _ = sizes
    n_y = n_near // 2
    row = lax.axis_index("row") % n_far
    return row * n_y + lax.axis_index("seq") // n_core


def left_kernel(sizes, own_ref, came_ref, *out_refs):
    n_core = sizes[2]
    chunk = own_ref.shape[0] // len(out_refs) // n_core
    core = lax.axis_index("seq") % n_core
    here = half_index(sizes)
    rows = sizes[3]
    per, cols = chunk // rows, own_ref.shape[1]
    for k, ref in enumerate(out_refs):
        at = pl.multiple_of((core * len(out_refs) + (here ^ k)) * chunk, chunk)
        own = own_ref[pl.ds(at, chunk), :].astype(F32).reshape(per, rows, cols)
        came = came_ref[pl.ds(at, chunk), :].astype(F32).reshape(per, rows, cols)
        pair = [jnp.where(core == 0, own, came), jnp.where(core == 0, came, own)]
        ref[...] = jnp.concatenate(pair, 1).reshape(n_core * chunk, cols).astype(BF16)


def product_kernel(sizes, per, recv_ref, *refs):
    n_core, rows, n_dev = sizes[2], sizes[3], sizes[4]
    half, chunk = n_dev // 2, per * rows
    chips = half // n_core
    left_refs, (send_ref, left, right, total) = refs[:chips], refs[chips:]
    here = half_index(sizes)
    for src in range(n_dev):
        block = recv_ref[src * chunk : (src + 1) * chunk, :].astype(F32)
        for c in range(per):
            right[c, src * rows : (src + 1) * rows, :] = block[c * rows : (c + 1) * rows]
    for k, ref in enumerate(left_refs):
        at = pl.multiple_of((here ^ k) * n_core * rows, n_core * rows)
        for c in range(per):
            left[c, pl.ds(at, n_core * rows), :] = ref[c * n_core * rows : (c + 1) * n_core * rows, :]
    for c in range(per):
        prod = mul_t(left[c], right[c].astype(BF16))
        for dst in range(half):
            total[dst, c * rows : (c + 1) * rows, :] = prod[dst * rows : (dst + 1) * rows]
    for dst in range(half):
        send_ref[dst * chunk : (dst + 1) * chunk, :] = total[dst].astype(BF16)


def finish_kernel(sizes, recv_ref, mid_ref, gate_ref, out_w, out_ref, apart, done_ref, sems):
    rows = sizes[3]
    _, width, cols = mid_ref.shape
    hidden = out_w.shape[1]
    some = 256 // rows
    blocks = hidden // some
    count = some * rows

    def piece(b):
        return recv_ref[b * count : (b + 1) * count, :].astype(F32).reshape(some, rows, cols)

    mean = sum(jnp.sum(piece(b), 0) for b in range(blocks)) * (1.0 / hidden)
    spread = sum(jnp.sum((piece(b) - mean) ** 2, 0) for b in range(blocks)) * (1.0 / hidden)
    factor = lax.rsqrt(spread + EPS)
    shuffle = swap_rows(some, rows)
    for b in range(blocks):
        normed = ((piece(b) - mean) * factor).reshape(count, cols).astype(BF16)
        normed = mul(shuffle, normed).astype(BF16)
        for i in range(rows):
            apart[i, b * some : (b + 1) * some, :] = normed[i * some : (i + 1) * some]
    eye = identity(cols)
    copies = []
    updates = [mul(out_w[...], apart[i]) for i in range(rows)]
    dones = [(mid_ref[i].astype(F32) + gate_ref[i] * updates[i]).astype(BF16) for i in range(rows)]
    for i in range(rows):
        done_ref[i] = mul_t(eye, dones[i]).astype(BF16)
        copies.append(pltpu.make_async_copy(done_ref.at[i], out_ref.at[i], sems.at[i]))
        copies[i].start()
    for copy in copies:
        copy.wait()


def call(kernel, out_shape, scratch, grant, flops, *args, far_in=False, far_out=False):
    if isinstance(far_out, bool):
        far_out = [far_out] * len(out_shape)
    out_specs = [pl.BlockSpec(memory_space=pltpu.HBM if far else pltpu.VMEM) for far in far_out]
    out_shape = [
        (jax.ShapeDtypeStruct if far else pltpu.VMEM)(*(s if isinstance(s[0], tuple) else (s, BF16)))
        for s, far in zip(out_shape, far_out, strict=True)
    ]
    if far_in:
        args = [pltpu.with_memory_space_constraint(a, pltpu.HBM) for a in args]
    moved = sum(math.prod(a.shape) * jnp.dtype(a.dtype).itemsize for a in (*args, *out_shape))
    return pl.pallas_call(
        kernel,
        out_shape=out_shape,
        in_specs=[pl.BlockSpec(memory_space=pltpu.HBM if far_in else pltpu.VMEM)] * len(args),
        out_specs=out_specs,
        scratch_shapes=scratch,
        compiler_params=pltpu.CompilerParams(vmem_limit_bytes=grant * 2**20),
        cost_estimate=pl.CostEstimate(flops=flops, bytes_accessed=moved, transcendentals=0),
    )(*args)


def factors_call(sizes, alignment, opm_left, opm_right):
    n_far, n_near, n_core, rows, _ = sizes
    seqs, cols, width = alignment.shape
    factor = opm_left.shape[1]
    return call(
        functools.partial(factors_kernel, sizes),
        [(seqs * factor + n_core * seqs * n_near, cols)] * n_far,
        [
            pltpu.VMEM((n_far, n_core * seqs * n_near, cols), BF16),
            pltpu.VMEM(alignment.shape, BF16),
            pltpu.VMEM(opm_left.shape[::-1], BF16),
            pltpu.VMEM(opm_right.shape[::-1], BF16),
            pltpu.VMEM((cols, n_core * rows * factor), BF16),
            pltpu.VMEM((seqs, n_far * seqs * n_near, cols), BF16),
            pltpu.SemaphoreType.DMA((2 + seqs,)),
        ],
        8,
        4 * seqs * cols * width * factor,
        alignment,
        opm_left.T,
        opm_right.T,
        far_in=True,
    )


def whole_channels(
    pair,
    alignment,
    opm_left,
    opm_right,
    opm_out,
    tri_left,
    tri_left_gate,
    tri_right,
    tri_right_gate,
    tri_gate,
    tri_out,
):
    rows, cols, width = pair.shape
    seqs = alignment.shape[0]
    factor = opm_left.shape[1]
    hidden = tri_left.shape[1]
    n_row, n_seq = lax.axis_size("row"), lax.axis_size("seq")
    n_dev = n_row * n_seq
    n_core = 2
    n_far, n_near = n_row // 2, 2 * (n_seq // n_core)
    n_y = n_near // 2
    sizes = (n_far, n_near, n_core, rows, n_dev)
    held = n_far * seqs
    half = n_dev // 2
    per = hidden // half
    chips = half // n_core

    def exchange(value, row_bits, seq_bits):
        pairs = [
            (r * n_seq + s, (r ^ row_bits) * n_seq + (s ^ seq_bits))
            for r in range(n_row)
            for s in range(n_seq)
        ]
        return lax.ppermute(value, BOTH, pairs)

    mine = factors_call(sizes, alignment, opm_left, opm_right)
    weights = (
        pair,
        opm_out,
        tri_left_gate,
        tri_left,
        tri_right_gate,
        tri_right,
        tri_gate,
        tri_out,
    )
    mine, weights = lax.optimization_barrier((mine, weights))
    def to_near(value, k):
        return exchange(value, k // n_y, (k % n_y) * n_core)

    far = [exchange(mine[k], 2 * k, 0) for k in range(n_far - 1, 0, -1)]
    early = to_near(mine[0], n_near - 1)
    far = [mine[0]] + far
    prepared = call(
        functools.partial(prepare_kernel, factor),
        [
            (rows, width, cols),
            (width, factor * factor),
            (4 * hidden, width),
            (width, width),
            (width, hidden),
        ],
        [pltpu.VMEM(w.shape, BF16) for w in weights] + [pltpu.SemaphoreType.DMA((len(weights),))],
        8,
        4 * rows * cols * width * width,
        *weights,
        far_in=True,
    )
    far, early, prepared = lax.optimization_barrier((far, early, prepared))
    pair_t, out_t, tri_t, gate_t, final_t = prepared
    message = ((factor + n_core) * held, cols)
    late = ((n_far - 1) * seqs * factor + n_core * held, cols)
    mine = call(
        functools.partial(regroup_kernel, sizes, factor, seqs),
        [message] * (n_near - 1) + [late],
        [pltpu.VMEM((2, n_near, n_core * held, cols), BF16)],
        8,
        2 * 256 * factor * held * cols,
        *far,
    )
    near = [to_near(mine[k], k) for k in range(n_near - 1, 0, -1)]
    (near[0],) = call(
        functools.partial(merge_kernel, sizes, factor, seqs),
        [message],
        [],
        8,
        2 * 256 * factor * held * cols,
        early,
        near[0],
    )
    near = [mine[0]] + near
    groups = near + [exchange(block, 0, 1) for block in near]
    scale = 1.0 / (held * n_near * n_core)
    send, left, mid, normed = call(
        functools.partial(pair_kernel, sizes, held, scale),
        [
            (2 * hidden * rows, cols),
            (hidden * rows, cols),
            (rows, width, cols),
            (rows, width, cols),
        ],
        [
            pltpu.VMEM((rows, factor * factor, cols), BF16),
            pltpu.VMEM((2, rows, hidden, cols), BF16),
            pltpu.VMEM((hidden * rows, cols), BF16),
            pltpu.SemaphoreType.DMA((2,)),
        ],
        16,
        4 * rows * cols * width * (factor * factor + hidden * 2),
        *groups,
        pair_t,
        out_t,
        tri_t,
        far_out=(True, False, False, False),
    )
    (gate,) = call(
        gate_kernel,
        [((rows, width, cols), F32)],
        [],
        8,
        2 * rows * cols * width * width,
        normed,
        gate_t,
    )
    recv = lax.all_to_all(send, BOTH, split_axis=0, concat_axis=0, tiled=True)
    mine = call(
        functools.partial(left_kernel, sizes),
        [(n_core * per * rows, cols)] * chips,
        [],
        8,
        0,
        left,
        exchange(left, 0, 1),
    )
    lefts = [mine[0]]
    for k in range(1, chips):
        lefts.append(exchange(mine[k], k // n_y, k % n_y * n_core))
    (send,) = call(
        functools.partial(product_kernel, sizes, per),
        [(hidden * rows, cols)],
        [
            pltpu.VMEM((per, rows * half, cols), BF16),
            pltpu.VMEM((per, rows * n_dev, cols), F32),
            pltpu.VMEM((half, per * rows, cols), F32),
        ],
        16,
        2 * per * cols * cols * cols // 2,
        recv,
        *lefts,
    )
    halves = [list(range(half)), list(range(half, n_dev))]
    recv = lax.all_to_all(
        send, BOTH, split_axis=0, concat_axis=0, tiled=True, axis_index_groups=halves
    )
    (out,) = call(
        functools.partial(finish_kernel, sizes),
        [(rows, cols, width)],
        [
            pltpu.VMEM((rows, hidden, cols), BF16),
            pltpu.VMEM((rows, cols, width), BF16),
            pltpu.SemaphoreType.DMA((rows,)),
        ],
        16,
        4 * rows * cols * width * hidden,
        recv,
        mid,
        gate,
        final_t,
        far_out=True,
    )
    return out


def power_of_two(n):
    return n & (n - 1) == 0


def on_device(pair, alignment, opm_left, *rest):
    rows, cols, width = pair.shape
    factor, hidden = opm_left.shape[1], rest[2].shape[1]
    n_row, n_col, n_seq = (lax.axis_size(a) for a in ("row", "col", "seq"))
    n_dev = n_row * n_seq
    held = n_row // 2 * alignment.shape[0]
    fits = (
        n_col == 1
        and power_of_two(n_row)
        and power_of_two(n_seq)
        and power_of_two(rows)
        and n_row >= 4
        and n_seq >= 4
        and hidden % n_dev == 0
        and hidden == width
        and factor % 16 == 0
        and rows % 8 == 0
        and (hidden // n_dev * rows) % 16 == 0
        and cols % 256 == 0
        and rows * factor == cols
        and rows * n_dev == cols
        and held % 16 == 0
        and 256 % held == 0
        and factor % (256 // held) == 0
        and hidden % (256 // rows) == 0
        and power_of_two(held * n_seq * 2)
    )
    plan = whole_channels if fits else by_groups
    return plan(pair, alignment, opm_left, *rest)


def solution(mesh):
    return jax.shard_map(
        on_device,
        mesh=mesh,
        in_specs=(
            P(("row", "seq"), "col", None),
            P(("row", "seq"), "col", None),
            P(),
            P(),
            P(),
            P(),
            P(),
            P(),
            P(),
            P(),
            P(),
        ),
        out_specs=P(("row", "seq"), "col", None),
        check_vma=False,
    )
```

```python
import functools
import math

import jax
import jax.numpy as jnp
from jax import lax
from jax.experimental import pallas as pl
from jax.experimental.pallas import tpu as pltpu
from jax.sharding import PartitionSpec as P

EPS = 1e-05
BOTH = ("row", "seq")
BF16 = jnp.bfloat16
F32 = jnp.float32


def spread_2(shard, axis, root):
    mine = lax.axis_index(axis) == root
    return lax.psum(jnp.where(mine, shard, jnp.zeros_like(shard)), axis)


def layer_norm(values, axis):
    values = values.astype(jnp.float32)
    center = values - jnp.mean(values, axis=axis, keepdims=True)
    spread = jnp.mean(center * center, axis=axis, keepdims=True)
    return center * lax.rsqrt(spread + EPS)


def contract(local_rows, piece):
    return jnp.einsum("cik,cjk->cij", local_rows, piece, preferred_element_type=jnp.float32)


def by_groups(
    pair,
    alignment,
    opm_left,
    opm_right,
    opm_out,
    tri_left,
    tri_left_gate,
    tri_right,
    tri_right_gate,
    tri_gate,
    tri_out,
):
    rows_here, cols_here, pair_width = pair.shape
    seq_here = alignment.shape[0]
    model_width = alignment.shape[2]
    factor_width = opm_left.shape[1]
    hidden = tri_left.shape[1]
    n_row = lax.axis_size("row")
    n_col = lax.axis_size("col")
    n_seq = lax.axis_size("seq")
    seq_normed = (
        layer_norm(alignment, 2).astype(jnp.bfloat16).reshape(seq_here * cols_here, model_width)
    )
    left_proj = (
        jnp.dot(seq_normed, opm_left, preferred_element_type=jnp.float32)
        .astype(jnp.bfloat16)
        .reshape(seq_here, cols_here * factor_width)
    )
    right_proj = (
        jnp.dot(seq_normed, opm_right, preferred_element_type=jnp.float32)
        .astype(jnp.bfloat16)
        .reshape(seq_here, cols_here * factor_width)
    )
    per_col = n_row // n_col
    index_row = lax.axis_index("row")
    root_col = index_row // per_col
    right_all = lax.all_gather(right_proj, ("row", "seq"), axis=0, tiled=True)
    left_blocks = left_proj.reshape(seq_here, per_col * n_seq, rows_here * factor_width)
    left_send = jnp.tile(left_blocks, (1, n_col, 1))
    left_recv = lax.all_to_all(left_send, ("row", "seq"), split_axis=1, concat_axis=0, tiled=True)
    row_slice = left_recv.reshape(seq_here * n_row * n_seq, rows_here * factor_width)
    seqs_all = right_all.shape[0]
    row_factors = spread_2(row_slice, "col", root_col)
    right_wide = right_all.reshape(seqs_all, cols_here, factor_width)
    row_stack = jnp.swapaxes(row_factors.reshape(seqs_all, rows_here, factor_width), 0, 1)

    def outer_row(packed):
        row_vals, pair_row = packed
        outer_sum = jnp.einsum(
            "np,njq->jpq", row_vals, right_wide, preferred_element_type=jnp.float32
        )
        mean_outer = (
            (outer_sum * (1.0 / seqs_all))
            .astype(jnp.bfloat16)
            .reshape(cols_here, factor_width * factor_width)
        )
        return (
            pair_row.astype(jnp.float32)
            + jnp.dot(mean_outer, opm_out, preferred_element_type=jnp.float32)
        ).astype(jnp.bfloat16)

    pair_mid = lax.map(outer_row, (row_stack, pair))
    normed_pair = layer_norm(pair_mid, 2).astype(jnp.bfloat16)
    flat_pair = normed_pair.reshape(rows_here * cols_here, pair_width)

    def project(weight):
        return lax.dot_general(
            weight, flat_pair, (((0,), (1,)), ((), ())), preferred_element_type=jnp.float32
        )

    def gated(weight_gate, weight_value):
        gate_part = jax.nn.sigmoid(project(weight_gate))
        return (
            (gate_part * project(weight_value))
            .astype(jnp.bfloat16)
            .reshape(hidden, rows_here, cols_here)
        )

    left_first = gated(tri_left_gate, tri_left)
    right_first = gated(tri_right_gate, tri_right)
    left_local, right_local = (
        lax.all_to_all(
            lax.all_to_all(left_first, "col", split_axis=0, concat_axis=2, tiled=True),
            "seq",
            split_axis=0,
            concat_axis=1,
            tiled=True,
        ),
        lax.all_to_all(
            lax.all_to_all(right_first, "col", split_axis=0, concat_axis=2, tiled=True),
            "seq",
            split_axis=0,
            concat_axis=1,
            tiled=True,
        ),
    )
    product = contract(left_local, lax.all_gather(right_local, "row", axis=1, tiled=True))
    product = product.astype(jnp.bfloat16)
    returned = lax.all_to_all(
        lax.all_to_all(product, "col", split_axis=2, concat_axis=0, tiled=True),
        "seq",
        split_axis=1,
        concat_axis=0,
        tiled=True,
    )
    per_group = hidden // (n_col * n_seq)
    weights_order = (
        tri_out.reshape(n_col, n_seq, per_group, pair_width)
        .transpose(1, 0, 2, 3)
        .reshape(hidden, pair_width)
    )
    normed_product = layer_norm(returned, 0).astype(jnp.bfloat16)
    update = jnp.einsum(
        "cij,cd->ijd", normed_product, weights_order, preferred_element_type=jnp.float32
    )
    gate_part = jax.nn.sigmoid(
        jnp.dot(flat_pair, tri_gate, preferred_element_type=jnp.float32)
    ).reshape(rows_here, cols_here, pair_width)
    return (pair_mid.astype(jnp.float32) + gate_part * update).astype(jnp.bfloat16)


def mul(a, b):
    return jnp.dot(a, b, preferred_element_type=F32)


def mul_t(a, b):
    return lax.dot_general(a, b, (((1,), (1,)), ((), ())), preferred_element_type=F32)


def ones_where(mask):
    return jnp.where(mask, 1.0, 0.0).astype(BF16)


def iotas(rows, cols):
    shape = (rows, cols)
    return lax.broadcasted_iota(jnp.int32, shape, 0), lax.broadcasted_iota(jnp.int32, shape, 1)


def identity(size):
    row, col = iotas(size, size)
    return ones_where(row == col)


def swap_rows(outer, inner):
    row, col = iotas(outer * inner, outer * inner)
    return ones_where(col == (row % outer) * inner + row // outer)


def normalize(values, axis):
    center = values - jnp.mean(values, axis=axis, keepdims=True)
    spread = jnp.mean(center * center, axis=axis, keepdims=True)
    return center * lax.rsqrt(spread + EPS)


def fetch(sems, pairs):
    copies = [
        pltpu.make_async_copy(source, target, sems.at[k]) for k, (source, target) in enumerate(pairs)
    ]
    for copy in copies:
        copy.start()
    return copies


def factors_kernel(sizes, align_in, left_in, right_in, *refs):
    n_far, n_near, n_core, rows, _ = sizes
    out_refs, (parts, align_ref, left_ref, right_ref, own_lane, picks, sems) = refs[:n_far], refs[n_far:]
    pairs = [(left_in, left_ref), (right_in, right_ref)]
    pairs += [(align_in, align_ref)]
    copies = fetch(sems, pairs)
    seqs, cols, width = align_ref.shape
    factor = left_ref.shape[0]
    chip_rows = n_core * rows
    row, col = iotas(chip_rows * factor, factor)
    widen = ones_where(row % factor == col)
    row, col = iotas(cols, chip_rows * factor)
    own_lane[...] = ones_where((row % chip_rows) == (col // factor))
    row, col = iotas(n_far * seqs * n_near, cols)
    chip_of_row = (row // (seqs * n_near)) * n_near + row % n_near
    chip_match = chip_of_row == col // chip_rows
    seq_of_row = (row // n_near) % seqs
    for n in range(seqs):
        picks[n] = ones_where(chip_match & (seq_of_row == n))
    copies[0].wait()
    copies[1].wait()
    left_wide = mul(widen, left_ref[...]).astype(BF16)
    right_rows, left_rows = [], None
    for n in range(seqs):
        if n == 0:
            copies[2].wait()
        normed = normalize(align_ref[n].astype(F32), 1).astype(BF16)
        right_rows.append(mul_t(right_ref[...], normed))
        spread = mul_t(normed, left_wide).astype(BF16) * own_lane[...]
        part = mul(picks[n], spread)
        left_rows = part if left_rows is None else left_rows + part
    right_block = jnp.concatenate(right_rows, 0).astype(BF16)
    part_rows = seqs * n_near
    pieces = n_core
    for far in range(n_far):
        for piece in range(pieces):
            parts[far, piece * part_rows : (piece + 1) * part_rows, :] = left_rows[
                far * part_rows : (far + 1) * part_rows, piece * cols : (piece + 1) * cols
            ].astype(BF16)
    here = lax.axis_index("row") // 2
    for k in range(n_far):
        out_refs[k][: seqs * factor, :] = right_block
        out_refs[k][seqs * factor :, :] = parts[here ^ k]


def near_index(n_near, n_core):
    return (lax.axis_index("row") % 2) * (n_near // 2) + lax.axis_index("seq") // n_core


def regroup(sizes, factor, seqs, blocks, out_refs):
    held = sizes[0] * seqs
    half = 256 // held
    shuffle = swap_rows(held, half)
    for h in range(factor // half):
        block = jnp.concatenate(
            [
                ref[at + n * factor + h * half : at + n * factor + (h + 1) * half, :]
                for ref, at in blocks
                for n in range(seqs)
            ],
            0,
        )
        block = mul(shuffle, block).astype(BF16)
        for ref in out_refs:
            ref[h * half * held : (h + 1) * half * held, :] = block


def regroup_kernel(sizes, factor, seqs, *refs):
    n_far, n_near, n_core, _, _ = sizes
    in_refs, out_refs, parts = refs[:n_far], refs[n_far : n_far + n_near], refs[-1]
    held, part_rows, base = n_far * seqs, seqs * n_near, seqs * factor
    regroup(sizes, factor, seqs, [(ref, 0) for ref in in_refs], out_refs[:-1])
    for far in range(1, n_far):
        out_refs[-1][(far - 1) * base : far * base, :] = in_refs[far][:base, :]
    pick = swap_rows(held, n_near)
    row, _ = iotas(held * n_near, held * n_near)
    pick_late = jnp.where(row % held < seqs, 0.0, pick.astype(F32)).astype(BF16)
    for piece in range(n_core):
        block = jnp.concatenate(
            [ref[base + piece * part_rows : base + (piece + 1) * part_rows, :] for ref in in_refs], 0
        )
        for late, matrix in enumerate((pick, pick_late)):
            rows = mul(matrix, block).astype(BF16)
            for near in range(n_near):
                parts[late, near, piece * held : (piece + 1) * held, :] = rows[
                    near * held : (near + 1) * held
                ]
    here = near_index(n_near, n_core)
    for k in range(n_near - 1):
        out_refs[k][factor * held :, :] = parts[0, here ^ k]
    out_refs[-1][(n_far - 1) * base :, :] = parts[1, here ^ (n_near - 1)]


def merge_kernel(sizes, factor, seqs, early_ref, late_ref, out_ref):
    n_far, n_near, n_core, _, _ = sizes
    held, part_rows, base = n_far * seqs, seqs * n_near, seqs * factor
    blocks = [(early_ref, 0)] + [(late_ref, far * base) for far in range(n_far - 1)]
    regroup(sizes, factor, seqs, blocks, [out_ref])
    row, col = iotas(n_core * held, n_core * part_rows)
    slot = row // held * part_rows + row % held * n_near + near_index(n_near, n_core)
    pick = ones_where((row % held < seqs) & (col == slot))
    own = mul(pick, early_ref[base:, :])
    out_ref[factor * held :, :] = (own + late_ref[(n_far - 1) * base :, :].astype(F32)).astype(BF16)


def prepare_kernel(factor, *refs):
    n = (len(refs) - 6) // 2
    sources, (pair_t, out_t, tri_t, gate_t, final_t), targets = refs[:n], refs[n : n + 5], refs[n + 5 : -1]
    copies = fetch(refs[-1], list(zip(sources, targets, strict=True)))
    pair_ref, out_w, *tri, gate_w, final_w = targets
    eye = identity(pair_ref.shape[2])
    for copy in copies:
        copy.wait()
    for i in range(pair_ref.shape[0]):
        pair_t[i] = mul_t(eye, pair_ref[i]).astype(BF16)
    shuffle = swap_rows(256 // 16, 16)
    for q in range(0, factor, 16):
        for p in range(0, factor, 256 // 16):
            block = jnp.concatenate(
                [
                    out_w[(p + k) * factor + q : (p + k) * factor + q + 16, :]
                    for k in range(256 // 16)
                ],
                0,
            )
            block = mul(shuffle, block).astype(BF16)
            block = mul_t(eye, block).astype(BF16)
            at = (q // 16 * (factor // 16) + p // 16) * 256
            out_t[:, at : at + 256] = block
    for k, ref in enumerate(tri):
        width = ref.shape[1]
        tri_t[k * width : (k + 1) * width, :] = mul_t(eye, ref[...]).astype(BF16)
    gate_t[...] = mul_t(eye, gate_w[...]).astype(BF16)
    final_t[...] = mul_t(eye, final_w[...]).astype(BF16)


def pair_kernel(sizes, held, scale, *refs):
    n_core, rows, n_dev = sizes[2], sizes[3], sizes[4]
    groups = refs[:-11]
    pair_ref, out_w, tri_w, send_ref, left_ref, mid_ref, norm_ref, outer, both, right_ref, sems = refs[-11:]
    factor = groups[0].shape[0] // held - n_core
    hidden = tri_w.shape[0] // 4
    core = lax.axis_index("seq") % n_core
    at = pl.multiple_of((factor + core) * held, held)
    left = jnp.concatenate([ref[pl.ds(at, held), :] for ref in groups], 0)
    left_t = mul_t(identity(rows * factor), left).astype(BF16)
    for q in range(factor):
        right = jnp.concatenate([ref[q * held : (q + 1) * held, :] for ref in groups], 0)
        block = mul(left_t, right).astype(BF16)
        for i in range(rows):
            for p in range(0, factor, 16):
                at = (q // 16 * (factor // 16) + p // 16) * 256 + q % 16 * 16
                outer[i, at : at + 16, :] = block[i * factor + p : i * factor + p + 16]
    updates = [mul(out_w[...], outer[i]) for i in range(rows)]
    for i in range(rows):
        update = updates[i]
        mid = (pair_ref[i].astype(F32) + update * scale).astype(BF16)
        mid_ref[i] = mid
        normed = normalize(mid.astype(F32), 0).astype(BF16)
        norm_ref[i] = normed
    half = n_dev // 2
    chunk = hidden // half * rows
    some = 256 // rows
    shuffle = swap_rows(rows, some)
    per = some * rows // chunk

    def by_channels(side):
        at = 2 * side * hidden
        for i in range(rows):
            parts = mul(tri_w[at : at + 2 * hidden, :], norm_ref[i])
            both[side, i] = (jax.nn.sigmoid(parts[:hidden]) * parts[hidden:]).astype(BF16)
        blocks = [
            jnp.concatenate([both[side, i, b * some : (b + 1) * some, :] for i in range(rows)], 0)
            for b in range(hidden // some)
        ]
        return [mul(shuffle, block).astype(BF16) for block in blocks]

    copies = []
    for b, block in enumerate(by_channels(1)):
        right_ref[b * per * chunk : (b + 1) * per * chunk, :] = block
        if b % 2 == 1:
            size = 2 * per * chunk
            source = right_ref.at[pl.ds((b - 1) * per * chunk, size)]
            for h in range(2):
                target = send_ref.at[pl.ds((h * half + (b - 1) * per) * chunk, size)]
                copies.append(pltpu.make_async_copy(source, target, sems.at[len(copies)]))
                copies[-1].start()
    for b, block in enumerate(by_channels(0)):
        for d in range(per):
            to = (d % n_core * half + b * per + d) // n_core * chunk
            left_ref[to : to + chunk, :] = block[d * chunk : (d + 1) * chunk]
    for copy in copies:
        copy.wait()


def half_index(sizes):
    n_far, n_near, n_core, _, _ = sizes
    n_y = n_near // 2
    row = lax.axis_index("row") % n_far
    return row * n_y + lax.axis_index("seq") // n_core


def left_kernel(sizes, own_ref, came_ref, *out_refs):
    n_core = sizes[2]
    chunk = own_ref.shape[0] // len(out_refs) // n_core
    core = lax.axis_index("seq") % n_core
    here = half_index(sizes)
    rows = sizes[3]
    per, cols = chunk // rows, own_ref.shape[1]
    for k, ref in enumerate(out_refs):
        at = pl.multiple_of((core * len(out_refs) + (here ^ k)) * chunk, chunk)
        own = own_ref[pl.ds(at, chunk), :].astype(F32).reshape(per, rows, cols)
        came = came_ref[pl.ds(at, chunk), :].astype(F32).reshape(per, rows, cols)
        pair = [jnp.where(core == 0, own, came), jnp.where(core == 0, came, own)]
        ref[...] = jnp.concatenate(pair, 1).reshape(n_core * chunk, cols).astype(BF16)


def product_kernel(sizes, per, recv_ref, *refs):
    n_core, rows, n_dev = sizes[2], sizes[3], sizes[4]
    half, chunk = n_dev // 2, per * rows
    chips = half // n_core
    left_refs, (send_ref, left, right, total) = refs[:chips], refs[chips:]
    here = half_index(sizes)
    for src in range(n_dev):
        block = recv_ref[src * chunk : (src + 1) * chunk, :].astype(F32)
        for c in range(per):
            right[c, src * rows : (src + 1) * rows, :] = block[c * rows : (c + 1) * rows]
    for k, ref in enumerate(left_refs):
        at = pl.multiple_of((here ^ k) * n_core * rows, n_core * rows)
        for c in range(per):
            left[c, pl.ds(at, n_core * rows), :] = ref[c * n_core * rows : (c + 1) * n_core * rows, :]
    for c in range(per):
        prod = mul_t(left[c], right[c].astype(BF16))
        for dst in range(half):
            total[dst, c * rows : (c + 1) * rows, :] = prod[dst * rows : (dst + 1) * rows]
    for dst in range(half):
        send_ref[dst * chunk : (dst + 1) * chunk, :] = total[dst].astype(BF16)


def finish_kernel(sizes, recv_ref, mid_ref, norm_ref, gate_w, out_w, out_ref, apart, done_ref, sems):
    rows = sizes[3]
    _, width, cols = mid_ref.shape
    hidden = out_w.shape[1]
    some = 256 // rows
    blocks = hidden // some
    count = some * rows

    def piece(b):
        return recv_ref[b * count : (b + 1) * count, :].astype(F32).reshape(some, rows, cols)

    mean = sum(jnp.sum(piece(b), 0) for b in range(blocks)) * (1.0 / hidden)
    spread = sum(jnp.sum((piece(b) - mean) ** 2, 0) for b in range(blocks)) * (1.0 / hidden)
    factor = lax.rsqrt(spread + EPS)
    shuffle = swap_rows(some, rows)
    for b in range(blocks):
        normed = ((piece(b) - mean) * factor).reshape(count, cols).astype(BF16)
        normed = mul(shuffle, normed).astype(BF16)
        for i in range(rows):
            apart[i, b * some : (b + 1) * some, :] = normed[i * some : (i + 1) * some]
    eye = identity(cols)
    copies = []
    gates = [jax.nn.sigmoid(mul(gate_w[...], norm_ref[i])) for i in range(rows)]
    updates = [mul(out_w[...], apart[i]) for i in range(rows)]
    dones = [(mid_ref[i].astype(F32) + gates[i] * updates[i]).astype(BF16) for i in range(rows)]
    for i in range(rows):
        done_ref[i] = mul_t(eye, dones[i]).astype(BF16)
        copies.append(pltpu.make_async_copy(done_ref.at[i], out_ref.at[i], sems.at[i]))
        copies[i].start()
    for copy in copies:
        copy.wait()


def call(kernel, out_shape, scratch, grant, flops, *args, far_in=False, far_out=False):
    if isinstance(far_out, bool):
        far_out = [far_out] * len(out_shape)
    out_specs = [pl.BlockSpec(memory_space=pltpu.HBM if far else pltpu.VMEM) for far in far_out]
    out_shape = [
        (jax.ShapeDtypeStruct if far else pltpu.VMEM)(*(s if isinstance(s[0], tuple) else (s, BF16)))
        for s, far in zip(out_shape, far_out, strict=True)
    ]
    if far_in:
        args = [pltpu.with_memory_space_constraint(a, pltpu.HBM) for a in args]
    moved = sum(math.prod(a.shape) * jnp.dtype(a.dtype).itemsize for a in (*args, *out_shape))
    return pl.pallas_call(
        kernel,
        out_shape=out_shape,
        in_specs=[pl.BlockSpec(memory_space=pltpu.HBM if far_in else pltpu.VMEM)] * len(args),
        out_specs=out_specs,
        scratch_shapes=scratch,
        compiler_params=pltpu.CompilerParams(vmem_limit_bytes=grant * 2**20),
        cost_estimate=pl.CostEstimate(flops=flops, bytes_accessed=moved, transcendentals=0),
    )(*args)


def factors_call(sizes, alignment, opm_left, opm_right):
    n_far, n_near, n_core, rows, _ = sizes
    seqs, cols, width = alignment.shape
    factor = opm_left.shape[1]
    return call(
        functools.partial(factors_kernel, sizes),
        [(seqs * factor + n_core * seqs * n_near, cols)] * n_far,
        [
            pltpu.VMEM((n_far, n_core * seqs * n_near, cols), BF16),
            pltpu.VMEM(alignment.shape, BF16),
            pltpu.VMEM(opm_left.shape[::-1], BF16),
            pltpu.VMEM(opm_right.shape[::-1], BF16),
            pltpu.VMEM((cols, n_core * rows * factor), BF16),
            pltpu.VMEM((seqs, n_far * seqs * n_near, cols), BF16),
            pltpu.SemaphoreType.DMA((2 + seqs,)),
        ],
        8,
        4 * seqs * cols * width * factor,
        alignment,
        opm_left.T,
        opm_right.T,
        far_in=True,
    )


def whole_channels(
    pair,
    alignment,
    opm_left,
    opm_right,
    opm_out,
    tri_left,
    tri_left_gate,
    tri_right,
    tri_right_gate,
    tri_gate,
    tri_out,
):
    rows, cols, width = pair.shape
    seqs = alignment.shape[0]
    factor = opm_left.shape[1]
    hidden = tri_left.shape[1]
    n_row, n_seq = lax.axis_size("row"), lax.axis_size("seq")
    n_dev = n_row * n_seq
    n_core = 2
    n_far, n_near = n_row // 2, 2 * (n_seq // n_core)
    n_y = n_near // 2
    sizes = (n_far, n_near, n_core, rows, n_dev)
    held = n_far * seqs
    half = n_dev // 2
    per = hidden // half
    chips = half // n_core

    def exchange(value, row_bits, seq_bits):
        pairs = [
            (r * n_seq + s, (r ^ row_bits) * n_seq + (s ^ seq_bits))
            for r in range(n_row)
            for s in range(n_seq)
        ]
        return lax.ppermute(value, BOTH, pairs)

    mine = factors_call(sizes, alignment, opm_left, opm_right)
    weights = (
        pair,
        opm_out,
        tri_left_gate,
        tri_left,
        tri_right_gate,
        tri_right,
        tri_gate,
        tri_out,
    )
    mine, weights = lax.optimization_barrier((mine, weights))
    def to_near(value, k):
        return exchange(value, k // n_y, (k % n_y) * n_core)

    far = [exchange(mine[k], 2 * k, 0) for k in range(n_far - 1, 0, -1)]
    early = to_near(mine[0], n_near - 1)
    far = [mine[0]] + far
    prepared = call(
        functools.partial(prepare_kernel, factor),
        [
            (rows, width, cols),
            (width, factor * factor),
            (4 * hidden, width),
            (width, width),
            (width, hidden),
        ],
        [pltpu.VMEM(w.shape, BF16) for w in weights] + [pltpu.SemaphoreType.DMA((len(weights),))],
        8,
        4 * rows * cols * width * width,
        *weights,
        far_in=True,
    )
    far, early, prepared = lax.optimization_barrier((far, early, prepared))
    pair_t, out_t, tri_t, gate_t, final_t = prepared
    message = ((factor + n_core) * held, cols)
    late = ((n_far - 1) * seqs * factor + n_core * held, cols)
    mine = call(
        functools.partial(regroup_kernel, sizes, factor, seqs),
        [message] * (n_near - 1) + [late],
        [pltpu.VMEM((2, n_near, n_core * held, cols), BF16)],
        8,
        2 * 256 * factor * held * cols,
        *far,
    )
    near = [to_near(mine[k], k) for k in range(n_near - 1, 0, -1)]
    (near[0],) = call(
        functools.partial(merge_kernel, sizes, factor, seqs),
        [message],
        [],
        8,
        2 * 256 * factor * held * cols,
        early,
        near[0],
    )
    near = [mine[0]] + near
    groups = near + [exchange(block, 0, 1) for block in near]
    scale = 1.0 / (held * n_near * n_core)
    send, left, mid, normed = call(
        functools.partial(pair_kernel, sizes, held, scale),
        [
            (2 * hidden * rows, cols),
            (hidden * rows, cols),
            (rows, width, cols),
            (rows, width, cols),
        ],
        [
            pltpu.VMEM((rows, factor * factor, cols), BF16),
            pltpu.VMEM((2, rows, hidden, cols), BF16),
            pltpu.VMEM((hidden * rows, cols), BF16),
            pltpu.SemaphoreType.DMA((hidden * rows // 256,)),
        ],
        16,
        4 * rows * cols * width * (factor * factor + hidden * 2),
        *groups,
        pair_t,
        out_t,
        tri_t,
        far_out=(True, False, False, False),
    )
    recv = lax.all_to_all(send, BOTH, split_axis=0, concat_axis=0, tiled=True)
    mine = call(
        functools.partial(left_kernel, sizes),
        [(n_core * per * rows, cols)] * chips,
        [],
        8,
        0,
        left,
        exchange(left, 0, 1),
    )
    lefts = [mine[0]]
    for k in range(1, chips):
        lefts.append(exchange(mine[k], k // n_y, k % n_y * n_core))
    (send,) = call(
        functools.partial(product_kernel, sizes, per),
        [(hidden * rows, cols)],
        [
            pltpu.VMEM((per, rows * half, cols), BF16),
            pltpu.VMEM((per, rows * n_dev, cols), F32),
            pltpu.VMEM((half, per * rows, cols), F32),
        ],
        16,
        2 * per * cols * cols * cols // 2,
        recv,
        *lefts,
    )
    halves = [list(range(half)), list(range(half, n_dev))]
    recv = lax.all_to_all(
        send, BOTH, split_axis=0, concat_axis=0, tiled=True, axis_index_groups=halves
    )
    (out,) = call(
        functools.partial(finish_kernel, sizes),
        [(rows, cols, width)],
        [
            pltpu.VMEM((rows, hidden, cols), BF16),
            pltpu.VMEM((rows, cols, width), BF16),
            pltpu.SemaphoreType.DMA((rows,)),
        ],
        16,
        4 * rows * cols * width * hidden,
        recv,
        mid,
        normed,
        gate_t,
        final_t,
        far_out=True,
    )
    return out


def power_of_two(n):
    return n & (n - 1) == 0


def on_device(pair, alignment, opm_left, *rest):
    rows, cols, width = pair.shape
    factor, hidden = opm_left.shape[1], rest[2].shape[1]
    n_row, n_col, n_seq = (lax.axis_size(a) for a in ("row", "col", "seq"))
    n_dev = n_row * n_seq
    held = n_row // 2 * alignment.shape[0]
    fits = (
        n_col == 1
        and power_of_two(n_row)
        and power_of_two(n_seq)
        and power_of_two(rows)
        and n_row >= 4
        and n_seq >= 4
        and hidden % n_dev == 0
        and hidden == width
        and factor % 16 == 0
        and rows % 8 == 0
        and (hidden // n_dev * rows) % 16 == 0
        and cols % 256 == 0
        and rows * factor == cols
        and rows * n_dev == cols
        and held % 16 == 0
        and 256 % held == 0
        and factor % (256 // held) == 0
        and hidden % (256 // rows) == 0
        and power_of_two(held * n_seq * 2)
    )
    plan = whole_channels if fits else by_groups
    return plan(pair, alignment, opm_left, *rest)


def solution(mesh):
    return jax.shard_map(
        on_device,
        mesh=mesh,
        in_specs=(
            P(("row", "seq"), "col", None),
            P(("row", "seq"), "col", None),
            P(),
            P(),
            P(),
            P(),
            P(),
            P(),
            P(),
            P(),
            P(),
        ),
        out_specs=P(("row", "seq"), "col", None),
        check_vma=False,
    )
```

```python
import functools
import math

import jax
import jax.numpy as jnp
from jax import lax
from jax.experimental import pallas as pl
from jax.experimental.pallas import tpu as pltpu
from jax.sharding import PartitionSpec as P

EPS = 1e-05
BOTH = ("row", "seq")
BF16 = jnp.bfloat16
F32 = jnp.float32


def spread_2(shard, axis, root):
    mine = lax.axis_index(axis) == root
    return lax.psum(jnp.where(mine, shard, jnp.zeros_like(shard)), axis)


def layer_norm(values, axis):
    values = values.astype(jnp.float32)
    center = values - jnp.mean(values, axis=axis, keepdims=True)
    spread = jnp.mean(center * center, axis=axis, keepdims=True)
    return center * lax.rsqrt(spread + EPS)


def contract(local_rows, piece):
    return jnp.einsum("cik,cjk->cij", local_rows, piece, preferred_element_type=jnp.float32)


def by_groups(
    pair,
    alignment,
    opm_left,
    opm_right,
    opm_out,
    tri_left,
    tri_left_gate,
    tri_right,
    tri_right_gate,
    tri_gate,
    tri_out,
):
    rows_here, cols_here, pair_width = pair.shape
    seq_here = alignment.shape[0]
    model_width = alignment.shape[2]
    factor_width = opm_left.shape[1]
    hidden = tri_left.shape[1]
    n_row = lax.axis_size("row")
    n_col = lax.axis_size("col")
    n_seq = lax.axis_size("seq")
    seq_normed = (
        layer_norm(alignment, 2).astype(jnp.bfloat16).reshape(seq_here * cols_here, model_width)
    )
    left_proj = (
        jnp.dot(seq_normed, opm_left, preferred_element_type=jnp.float32)
        .astype(jnp.bfloat16)
        .reshape(seq_here, cols_here * factor_width)
    )
    right_proj = (
        jnp.dot(seq_normed, opm_right, preferred_element_type=jnp.float32)
        .astype(jnp.bfloat16)
        .reshape(seq_here, cols_here * factor_width)
    )
    per_col = n_row // n_col
    index_row = lax.axis_index("row")
    root_col = index_row // per_col
    right_all = lax.all_gather(right_proj, ("row", "seq"), axis=0, tiled=True)
    left_blocks = left_proj.reshape(seq_here, per_col * n_seq, rows_here * factor_width)
    left_send = jnp.tile(left_blocks, (1, n_col, 1))
    left_recv = lax.all_to_all(left_send, ("row", "seq"), split_axis=1, concat_axis=0, tiled=True)
    row_slice = left_recv.reshape(seq_here * n_row * n_seq, rows_here * factor_width)
    seqs_all = right_all.shape[0]
    row_factors = spread_2(row_slice, "col", root_col)
    right_wide = right_all.reshape(seqs_all, cols_here, factor_width)
    row_stack = jnp.swapaxes(row_factors.reshape(seqs_all, rows_here, factor_width), 0, 1)

    def outer_row(packed):
        row_vals, pair_row = packed
        outer_sum = jnp.einsum(
            "np,njq->jpq", row_vals, right_wide, preferred_element_type=jnp.float32
        )
        mean_outer = (
            (outer_sum * (1.0 / seqs_all))
            .astype(jnp.bfloat16)
            .reshape(cols_here, factor_width * factor_width)
        )
        return (
            pair_row.astype(jnp.float32)
            + jnp.dot(mean_outer, opm_out, preferred_element_type=jnp.float32)
        ).astype(jnp.bfloat16)

    pair_mid = lax.map(outer_row, (row_stack, pair))
    normed_pair = layer_norm(pair_mid, 2).astype(jnp.bfloat16)
    flat_pair = normed_pair.reshape(rows_here * cols_here, pair_width)

    def project(weight):
        return lax.dot_general(
            weight, flat_pair, (((0,), (1,)), ((), ())), preferred_element_type=jnp.float32
        )

    def gated(weight_gate, weight_value):
        gate_part = jax.nn.sigmoid(project(weight_gate))
        return (
            (gate_part * project(weight_value))
            .astype(jnp.bfloat16)
            .reshape(hidden, rows_here, cols_here)
        )

    left_first = gated(tri_left_gate, tri_left)
    right_first = gated(tri_right_gate, tri_right)
    left_local, right_local = (
        lax.all_to_all(
            lax.all_to_all(left_first, "col", split_axis=0, concat_axis=2, tiled=True),
            "seq",
            split_axis=0,
            concat_axis=1,
            tiled=True,
        ),
        lax.all_to_all(
            lax.all_to_all(right_first, "col", split_axis=0, concat_axis=2, tiled=True),
            "seq",
            split_axis=0,
            concat_axis=1,
            tiled=True,
        ),
    )
    product = contract(left_local, lax.all_gather(right_local, "row", axis=1, tiled=True))
    product = product.astype(jnp.bfloat16)
    returned = lax.all_to_all(
        lax.all_to_all(product, "col", split_axis=2, concat_axis=0, tiled=True),
        "seq",
        split_axis=1,
        concat_axis=0,
        tiled=True,
    )
    per_group = hidden // (n_col * n_seq)
    weights_order = (
        tri_out.reshape(n_col, n_seq, per_group, pair_width)
        .transpose(1, 0, 2, 3)
        .reshape(hidden, pair_width)
    )
    normed_product = layer_norm(returned, 0).astype(jnp.bfloat16)
    update = jnp.einsum(
        "cij,cd->ijd", normed_product, weights_order, preferred_element_type=jnp.float32
    )
    gate_part = jax.nn.sigmoid(
        jnp.dot(flat_pair, tri_gate, preferred_element_type=jnp.float32)
    ).reshape(rows_here, cols_here, pair_width)
    return (pair_mid.astype(jnp.float32) + gate_part * update).astype(jnp.bfloat16)


def mul(a, b):
    return jnp.dot(a, b, preferred_element_type=F32)


def mul_t(a, b):
    return lax.dot_general(a, b, (((1,), (1,)), ((), ())), preferred_element_type=F32)


def ones_where(mask):
    return jnp.where(mask, 1.0, 0.0).astype(BF16)


def iotas(rows, cols):
    shape = (rows, cols)
    return lax.broadcasted_iota(jnp.int32, shape, 0), lax.broadcasted_iota(jnp.int32, shape, 1)


def identity(size):
    row, col = iotas(size, size)
    return ones_where(row == col)


def swap_rows(outer, inner):
    row, col = iotas(outer * inner, outer * inner)
    return ones_where(col == (row % outer) * inner + row // outer)


def normalize(values, axis):
    center = values - jnp.mean(values, axis=axis, keepdims=True)
    spread = jnp.mean(center * center, axis=axis, keepdims=True)
    return center * lax.rsqrt(spread + EPS)


def fetch(sems, pairs):
    copies = [
        pltpu.make_async_copy(source, target, sems.at[k]) for k, (source, target) in enumerate(pairs)
    ]
    for copy in copies:
        copy.start()
    return copies


def factors_kernel(sizes, align_in, left_in, right_in, *refs):
    n_far, n_near, n_core, rows, _ = sizes
    out_refs, (parts, align_ref, left_ref, right_ref, own_lane, picks, sems) = refs[:n_far], refs[n_far:]
    pairs = [(left_in, left_ref), (right_in, right_ref)]
    pairs += [(align_in, align_ref)]
    copies = fetch(sems, pairs)
    seqs, cols, width = align_ref.shape
    factor = left_ref.shape[0]
    chip_rows = n_core * rows
    row, col = iotas(chip_rows * factor, factor)
    widen = ones_where(row % factor == col)
    row, col = iotas(cols, chip_rows * factor)
    own_lane[...] = ones_where((row % chip_rows) == (col // factor))
    row, col = iotas(n_far * seqs * n_near, cols)
    chip_of_row = (row // (seqs * n_near)) * n_near + row % n_near
    chip_match = chip_of_row == col // chip_rows
    seq_of_row = (row // n_near) % seqs
    for n in range(seqs):
        picks[n] = ones_where(chip_match & (seq_of_row == n))
    copies[0].wait()
    copies[1].wait()
    left_wide = mul(widen, left_ref[...]).astype(BF16)
    right_rows, left_rows = [], None
    for n in range(seqs):
        if n == 0:
            copies[2].wait()
        normed = normalize(align_ref[n].astype(F32), 1).astype(BF16)
        right_rows.append(mul_t(right_ref[...], normed))
        spread = mul_t(normed, left_wide).astype(BF16) * own_lane[...]
        part = mul(picks[n], spread)
        left_rows = part if left_rows is None else left_rows + part
    right_block = jnp.concatenate(right_rows, 0).astype(BF16)
    part_rows = seqs * n_near
    pieces = n_core
    for far in range(n_far):
        for piece in range(pieces):
            parts[far, piece * part_rows : (piece + 1) * part_rows, :] = left_rows[
                far * part_rows : (far + 1) * part_rows, piece * cols : (piece + 1) * cols
            ].astype(BF16)
    here = lax.axis_index("row") // 2
    for k in range(n_far):
        out_refs[k][: seqs * factor, :] = right_block
        out_refs[k][seqs * factor :, :] = parts[here ^ k]


def near_index(n_near, n_core):
    return (lax.axis_index("row") % 2) * (n_near // 2) + lax.axis_index("seq") // n_core


def regroup(sizes, factor, seqs, blocks, out_refs):
    held = sizes[0] * seqs
    half = 256 // held
    shuffle = swap_rows(held, half)
    for h in range(factor // half):
        block = jnp.concatenate(
            [
                ref[at + n * factor + h * half : at + n * factor + (h + 1) * half, :]
                for ref, at in blocks
                for n in range(seqs)
            ],
            0,
        )
        block = mul(shuffle, block).astype(BF16)
        for ref in out_refs:
            ref[h * half * held : (h + 1) * half * held, :] = block


def regroup_kernel(sizes, factor, seqs, *refs):
    n_far, n_near, n_core, _, _ = sizes
    in_refs, out_refs, parts = refs[:n_far], refs[n_far : n_far + n_near], refs[-1]
    held, part_rows, base = n_far * seqs, seqs * n_near, seqs * factor
    regroup(sizes, factor, seqs, [(ref, 0) for ref in in_refs], out_refs[:-1])
    for far in range(1, n_far):
        out_refs[-1][(far - 1) * base : far * base, :] = in_refs[far][:base, :]
    pick = swap_rows(held, n_near)
    row, _ = iotas(held * n_near, held * n_near)
    pick_late = jnp.where(row % held < seqs, 0.0, pick.astype(F32)).astype(BF16)
    for piece in range(n_core):
        block = jnp.concatenate(
            [ref[base + piece * part_rows : base + (piece + 1) * part_rows, :] for ref in in_refs], 0
        )
        for late, matrix in enumerate((pick, pick_late)):
            rows = mul(matrix, block).astype(BF16)
            for near in range(n_near):
                parts[late, near, piece * held : (piece + 1) * held, :] = rows[
                    near * held : (near + 1) * held
                ]
    here = near_index(n_near, n_core)
    for k in range(n_near - 1):
        out_refs[k][factor * held :, :] = parts[0, here ^ k]
    out_refs[-1][(n_far - 1) * base :, :] = parts[1, here ^ (n_near - 1)]


def merge_kernel(sizes, factor, seqs, early_ref, late_ref, out_ref):
    n_far, n_near, n_core, _, _ = sizes
    held, part_rows, base = n_far * seqs, seqs * n_near, seqs * factor
    blocks = [(early_ref, 0)] + [(late_ref, far * base) for far in range(n_far - 1)]
    regroup(sizes, factor, seqs, blocks, [out_ref])
    row, col = iotas(n_core * held, n_core * part_rows)
    slot = row // held * part_rows + row % held * n_near + near_index(n_near, n_core)
    pick = ones_where((row % held < seqs) & (col == slot))
    own = mul(pick, early_ref[base:, :])
    out_ref[factor * held :, :] = (own + late_ref[(n_far - 1) * base :, :].astype(F32)).astype(BF16)


def prepare_kernel(factor, *refs):
    n = (len(refs) - 6) // 2
    sources, (pair_t, out_t, tri_t, gate_t, final_t), targets = refs[:n], refs[n : n + 5], refs[n + 5 : -1]
    copies = fetch(refs[-1], list(zip(sources, targets, strict=True)))
    pair_ref, out_w, *tri, gate_w, final_w = targets
    eye = identity(pair_ref.shape[2])
    for copy in copies:
        copy.wait()
    for i in range(pair_ref.shape[0]):
        pair_t[i] = mul_t(eye, pair_ref[i]).astype(BF16)
    shuffle = swap_rows(256 // 16, 16)
    for q in range(0, factor, 16):
        for p in range(0, factor, 256 // 16):
            block = jnp.concatenate(
                [
                    out_w[(p + k) * factor + q : (p + k) * factor + q + 16, :]
                    for k in range(256 // 16)
                ],
                0,
            )
            block = mul(shuffle, block).astype(BF16)
            block = mul_t(eye, block).astype(BF16)
            at = (q // 16 * (factor // 16) + p // 16) * 256
            out_t[:, at : at + 256] = block
    for k, ref in enumerate(tri):
        width = ref.shape[1]
        tri_t[k * width : (k + 1) * width, :] = mul_t(eye, ref[...]).astype(BF16)
    gate_t[...] = mul_t(eye, gate_w[...]).astype(BF16)
    final_t[...] = mul_t(eye, final_w[...]).astype(BF16)


def pair_kernel(sizes, held, scale, *refs):
    n_core, rows, n_dev = sizes[2], sizes[3], sizes[4]
    groups = refs[:-11]
    pair_ref, out_w, tri_w, send_ref, left_ref, mid_ref, norm_ref, outer, both, right_ref, sems = refs[-11:]
    factor = groups[0].shape[0] // held - n_core
    hidden = tri_w.shape[0] // 4
    core = lax.axis_index("seq") % n_core
    at = pl.multiple_of((factor + core) * held, held)
    left = jnp.concatenate([ref[pl.ds(at, held), :] for ref in groups], 0)
    left_t = mul_t(identity(rows * factor), left).astype(BF16)
    for q in range(factor):
        right = jnp.concatenate([ref[q * held : (q + 1) * held, :] for ref in groups], 0)
        block = mul(left_t, right).astype(BF16)
        for i in range(rows):
            for p in range(0, factor, 16):
                at = (q // 16 * (factor // 16) + p // 16) * 256 + q % 16 * 16
                outer[i, at : at + 16, :] = block[i * factor + p : i * factor + p + 16]
    updates = [mul(out_w[...], outer[i]) for i in range(rows)]
    for i in range(rows):
        update = updates[i]
        mid = (pair_ref[i].astype(F32) + update * scale).astype(BF16)
        mid_ref[i] = mid
        normed = normalize(mid.astype(F32), 0).astype(BF16)
        norm_ref[i] = normed
    half = n_dev // 2
    chunk = hidden // half * rows
    some = 256 // rows
    shuffle = swap_rows(rows, some)
    per = some * rows // chunk

    def by_channels(side):
        at = 2 * side * hidden
        for i in range(rows):
            parts = mul(tri_w[at : at + 2 * hidden, :], norm_ref[i])
            both[side, i] = (jax.nn.sigmoid(parts[:hidden]) * parts[hidden:]).astype(BF16)
        blocks = [
            jnp.concatenate([both[side, i, b * some : (b + 1) * some, :] for i in range(rows)], 0)
            for b in range(hidden // some)
        ]
        return [mul(shuffle, block).astype(BF16) for block in blocks]

    copies = []
    for b, block in enumerate(by_channels(1)):
        right_ref[b * per * chunk : (b + 1) * per * chunk, :] = block
        if b % 2 == 1:
            size = 2 * per * chunk
            source = right_ref.at[pl.ds((b - 1) * per * chunk, size)]
            for h in range(2):
                target = send_ref.at[pl.ds((h * half + (b - 1) * per) * chunk, size)]
                copies.append(pltpu.make_async_copy(source, target, sems.at[len(copies)]))
                copies[-1].start()
    for b, block in enumerate(by_channels(0)):
        for d in range(per):
            to = (d % n_core * half + b * per + d) // n_core * chunk
            left_ref[to : to + chunk, :] = block[d * chunk : (d + 1) * chunk]
    for copy in copies:
        copy.wait()


def half_index(sizes):
    n_far, n_near, n_core, _, _ = sizes
    n_y = n_near // 2
    row = lax.axis_index("row") % n_far
    return row * n_y + lax.axis_index("seq") // n_core


def left_kernel(sizes, own_ref, came_ref, *out_refs):
    n_core = sizes[2]
    chunk = own_ref.shape[0] // len(out_refs) // n_core
    core = lax.axis_index("seq") % n_core
    here = half_index(sizes)
    rows = sizes[3]
    per, cols = chunk // rows, own_ref.shape[1]
    for k, ref in enumerate(out_refs):
        at = pl.multiple_of((core * len(out_refs) + (here ^ k)) * chunk, chunk)
        own = own_ref[pl.ds(at, chunk), :].astype(F32).reshape(per, rows, cols)
        came = came_ref[pl.ds(at, chunk), :].astype(F32).reshape(per, rows, cols)
        pair = [jnp.where(core == 0, own, came), jnp.where(core == 0, came, own)]
        ref[...] = jnp.concatenate(pair, 1).reshape(n_core * chunk, cols).astype(BF16)


def product_kernel(sizes, per, recv_ref, *refs):
    n_core, rows, n_dev = sizes[2], sizes[3], sizes[4]
    half, chunk = n_dev // 2, per * rows
    chips = half // n_core
    left_refs, (send_ref, left, right, total) = refs[:chips], refs[chips:]
    here = half_index(sizes)
    for src in range(n_dev):
        block = recv_ref[src * chunk : (src + 1) * chunk, :].astype(F32)
        for c in range(per):
            right[c, src * rows : (src + 1) * rows, :] = block[c * rows : (c + 1) * rows]
    for k, ref in enumerate(left_refs):
        at = pl.multiple_of((here ^ k) * n_core * rows, n_core * rows)
        for c in range(per):
            left[c, pl.ds(at, n_core * rows), :] = ref[c * n_core * rows : (c + 1) * n_core * rows, :]
    for c in range(per):
        prod = mul_t(left[c], right[c].astype(BF16))
        for dst in range(half):
            total[dst, c * rows : (c + 1) * rows, :] = prod[dst * rows : (dst + 1) * rows]
    for dst in range(half):
        send_ref[dst * chunk : (dst + 1) * chunk, :] = total[dst].astype(BF16)


def finish_kernel(sizes, recv_ref, mid_ref, norm_ref, gate_w, out_w, out_ref, apart, done_ref, sems):
    rows = sizes[3]
    _, width, cols = mid_ref.shape
    hidden = out_w.shape[1]
    some = 256 // rows
    blocks = hidden // some
    count = some * rows

    def piece(b):
        return recv_ref[b * count : (b + 1) * count, :].astype(F32).reshape(some, rows, cols)

    mean = sum(jnp.sum(piece(b), 0) for b in range(blocks)) * (1.0 / hidden)
    spread = sum(jnp.sum((piece(b) - mean) ** 2, 0) for b in range(blocks)) * (1.0 / hidden)
    factor = lax.rsqrt(spread + EPS)
    shuffle = swap_rows(some, rows)
    normed = [
        ((piece(b) - mean) * factor).reshape(count, cols).astype(BF16) for b in range(blocks)
    ]
    normed = [mul(shuffle, block).astype(BF16) for block in normed]
    for b in range(blocks):
        for i in range(rows):
            apart[i, b * some : (b + 1) * some, :] = normed[b][i * some : (i + 1) * some]
    eye = identity(cols)
    copies = []
    gates = [mul(gate_w[...], norm_ref[i]) for i in range(rows)]
    updates = [mul(out_w[...], apart[i]) for i in range(rows)]
    dones = [(mid_ref[i].astype(F32) + jax.nn.sigmoid(gates[i]) * updates[i]).astype(BF16) for i in range(rows)]
    for i in range(rows):
        done_ref[i] = mul_t(eye, dones[i]).astype(BF16)
        copies.append(pltpu.make_async_copy(done_ref.at[i], out_ref.at[i], sems.at[i]))
        copies[i].start()
    for copy in copies:
        copy.wait()


def call(kernel, out_shape, scratch, grant, flops, *args, far_in=False, far_out=False):
    if isinstance(far_out, bool):
        far_out = [far_out] * len(out_shape)
    out_specs = [pl.BlockSpec(memory_space=pltpu.HBM if far else pltpu.VMEM) for far in far_out]
    out_shape = [
        (jax.ShapeDtypeStruct if far else pltpu.VMEM)(*(s if isinstance(s[0], tuple) else (s, BF16)))
        for s, far in zip(out_shape, far_out, strict=True)
    ]
    if far_in:
        args = [pltpu.with_memory_space_constraint(a, pltpu.HBM) for a in args]
    moved = sum(math.prod(a.shape) * jnp.dtype(a.dtype).itemsize for a in (*args, *out_shape))
    return pl.pallas_call(
        kernel,
        out_shape=out_shape,
        in_specs=[pl.BlockSpec(memory_space=pltpu.HBM if far_in else pltpu.VMEM)] * len(args),
        out_specs=out_specs,
        scratch_shapes=scratch,
        compiler_params=pltpu.CompilerParams(vmem_limit_bytes=grant * 2**20),
        cost_estimate=pl.CostEstimate(flops=flops, bytes_accessed=moved, transcendentals=0),
    )(*args)


def factors_call(sizes, alignment, opm_left, opm_right):
    n_far, n_near, n_core, rows, _ = sizes
    seqs, cols, width = alignment.shape
    factor = opm_left.shape[1]
    return call(
        functools.partial(factors_kernel, sizes),
        [(seqs * factor + n_core * seqs * n_near, cols)] * n_far,
        [
            pltpu.VMEM((n_far, n_core * seqs * n_near, cols), BF16),
            pltpu.VMEM(alignment.shape, BF16),
            pltpu.VMEM(opm_left.shape[::-1], BF16),
            pltpu.VMEM(opm_right.shape[::-1], BF16),
            pltpu.VMEM((cols, n_core * rows * factor), BF16),
            pltpu.VMEM((seqs, n_far * seqs * n_near, cols), BF16),
            pltpu.SemaphoreType.DMA((2 + seqs,)),
        ],
        8,
        4 * seqs * cols * width * factor,
        alignment,
        opm_left.T,
        opm_right.T,
        far_in=True,
    )


def whole_channels(
    pair,
    alignment,
    opm_left,
    opm_right,
    opm_out,
    tri_left,
    tri_left_gate,
    tri_right,
    tri_right_gate,
    tri_gate,
    tri_out,
):
    rows, cols, width = pair.shape
    seqs = alignment.shape[0]
    factor = opm_left.shape[1]
    hidden = tri_left.shape[1]
    n_row, n_seq = lax.axis_size("row"), lax.axis_size("seq")
    n_dev = n_row * n_seq
    n_core = 2
    n_far, n_near = n_row // 2, 2 * (n_seq // n_core)
    n_y = n_near // 2
    sizes = (n_far, n_near, n_core, rows, n_dev)
    held = n_far * seqs
    half = n_dev // 2
    per = hidden // half
    chips = half // n_core

    def exchange(value, row_bits, seq_bits):
        pairs = [
            (r * n_seq + s, (r ^ row_bits) * n_seq + (s ^ seq_bits))
            for r in range(n_row)
            for s in range(n_seq)
        ]
        return lax.ppermute(value, BOTH, pairs)

    mine = factors_call(sizes, alignment, opm_left, opm_right)
    weights = (
        pair,
        opm_out,
        tri_left_gate,
        tri_left,
        tri_right_gate,
        tri_right,
        tri_gate,
        tri_out,
    )
    mine, weights = lax.optimization_barrier((mine, weights))
    def to_near(value, k):
        return exchange(value, k // n_y, (k % n_y) * n_core)

    far = [exchange(mine[k], 2 * k, 0) for k in range(n_far - 1, 0, -1)]
    early = to_near(mine[0], n_near - 1)
    far = [mine[0], far[0], far[2], far[1]]
    prepared = call(
        functools.partial(prepare_kernel, factor),
        [
            (rows, width, cols),
            (width, factor * factor),
            (4 * hidden, width),
            (width, width),
            (width, hidden),
        ],
        [pltpu.VMEM(w.shape, BF16) for w in weights] + [pltpu.SemaphoreType.DMA((len(weights),))],
        8,
        4 * rows * cols * width * width,
        *weights,
        far_in=True,
    )
    far, early, prepared = lax.optimization_barrier((far, early, prepared))
    pair_t, out_t, tri_t, gate_t, final_t = prepared
    message = ((factor + n_core) * held, cols)
    late = ((n_far - 1) * seqs * factor + n_core * held, cols)
    mine = call(
        functools.partial(regroup_kernel, sizes, factor, seqs),
        [message] * (n_near - 1) + [late],
        [pltpu.VMEM((2, n_near, n_core * held, cols), BF16)],
        8,
        2 * 256 * factor * held * cols,
        *far,
    )
    near = [to_near(mine[k], k) for k in range(n_near - 1, 0, -1)]
    (near[0],) = call(
        functools.partial(merge_kernel, sizes, factor, seqs),
        [message],
        [],
        8,
        2 * 256 * factor * held * cols,
        early,
        near[0],
    )
    near = [mine[0]] + near
    groups = near + [exchange(block, 0, 1) for block in near]
    scale = 1.0 / (held * n_near * n_core)
    send, left, mid, normed = call(
        functools.partial(pair_kernel, sizes, held, scale),
        [
            (2 * hidden * rows, cols),
            (hidden * rows, cols),
            (rows, width, cols),
            (rows, width, cols),
        ],
        [
            pltpu.VMEM((rows, factor * factor, cols), BF16),
            pltpu.VMEM((2, rows, hidden, cols), BF16),
            pltpu.VMEM((hidden * rows, cols), BF16),
            pltpu.SemaphoreType.DMA((hidden * rows // 256,)),
        ],
        16,
        4 * rows * cols * width * (factor * factor + hidden * 2),
        *groups,
        pair_t,
        out_t,
        tri_t,
        far_out=(True, False, False, False),
    )
    recv = lax.all_to_all(send, BOTH, split_axis=0, concat_axis=0, tiled=True)
    mine = call(
        functools.partial(left_kernel, sizes),
        [(n_core * per * rows, cols)] * chips,
        [],
        8,
        0,
        left,
        exchange(left, 0, 1),
    )
    lefts = [mine[0]]
    for k in range(1, chips):
        lefts.append(exchange(mine[k], k // n_y, k % n_y * n_core))
    (send,) = call(
        functools.partial(product_kernel, sizes, per),
        [(hidden * rows, cols)],
        [
            pltpu.VMEM((per, rows * half, cols), BF16),
            pltpu.VMEM((per, rows * n_dev, cols), F32),
            pltpu.VMEM((half, per * rows, cols), F32),
        ],
        16,
        2 * per * cols * cols * cols // 2,
        recv,
        *lefts,
    )
    halves = [list(range(half)), list(range(half, n_dev))]
    recv = lax.all_to_all(
        send, BOTH, split_axis=0, concat_axis=0, tiled=True, axis_index_groups=halves
    )
    (out,) = call(
        functools.partial(finish_kernel, sizes),
        [(rows, cols, width)],
        [
            pltpu.VMEM((rows, hidden, cols), BF16),
            pltpu.VMEM((rows, cols, width), BF16),
            pltpu.SemaphoreType.DMA((rows,)),
        ],
        16,
        4 * rows * cols * width * hidden,
        recv,
        mid,
        normed,
        gate_t,
        final_t,
        far_out=True,
    )
    return out


def power_of_two(n):
    return n & (n - 1) == 0


def on_device(pair, alignment, opm_left, *rest):
    rows, cols, width = pair.shape
    factor, hidden = opm_left.shape[1], rest[2].shape[1]
    n_row, n_col, n_seq = (lax.axis_size(a) for a in ("row", "col", "seq"))
    n_dev = n_row * n_seq
    held = n_row // 2 * alignment.shape[0]
    fits = (
        n_col == 1
        and power_of_two(n_row)
        and power_of_two(n_seq)
        and power_of_two(rows)
        and n_row >= 4
        and n_seq >= 4
        and hidden % n_dev == 0
        and hidden == width
        and factor % 16 == 0
        and rows % 8 == 0
        and (hidden // n_dev * rows) % 16 == 0
        and cols % 256 == 0
        and rows * factor == cols
        and rows * n_dev == cols
        and held % 16 == 0
        and 256 % held == 0
        and factor % (256 // held) == 0
        and hidden % (256 // rows) == 0
        and power_of_two(held * n_seq * 2)
    )
    plan = whole_channels if fits else by_groups
    return plan(pair, alignment, opm_left, *rest)


def solution(mesh):
    return jax.shard_map(
        on_device,
        mesh=mesh,
        in_specs=(
            P(("row", "seq"), "col", None),
            P(("row", "seq"), "col", None),
            P(),
            P(),
            P(),
            P(),
            P(),
            P(),
            P(),
            P(),
            P(),
        ),
        out_specs=P(("row", "seq"), "col", None),
        check_vma=False,
    )
```

```python
import functools
import math

import jax
import jax.numpy as jnp
from jax import lax
from jax.experimental import pallas as pl
from jax.experimental.pallas import tpu as pltpu
from jax.sharding import PartitionSpec as P

EPS = 1e-05
BOTH = ("row", "seq")
BF16 = jnp.bfloat16
F32 = jnp.float32


def spread_2(shard, axis, root):
    mine = lax.axis_index(axis) == root
    return lax.psum(jnp.where(mine, shard, jnp.zeros_like(shard)), axis)


def layer_norm(values, axis):
    values = values.astype(jnp.float32)
    center = values - jnp.mean(values, axis=axis, keepdims=True)
    spread = jnp.mean(center * center, axis=axis, keepdims=True)
    return center * lax.rsqrt(spread + EPS)


def contract(local_rows, piece):
    return jnp.einsum("cik,cjk->cij", local_rows, piece, preferred_element_type=jnp.float32)


def by_groups(
    pair,
    alignment,
    opm_left,
    opm_right,
    opm_out,
    tri_left,
    tri_left_gate,
    tri_right,
    tri_right_gate,
    tri_gate,
    tri_out,
):
    rows_here, cols_here, pair_width = pair.shape
    seq_here = alignment.shape[0]
    model_width = alignment.shape[2]
    factor_width = opm_left.shape[1]
    hidden = tri_left.shape[1]
    n_row = lax.axis_size("row")
    n_col = lax.axis_size("col")
    n_seq = lax.axis_size("seq")
    seq_normed = (
        layer_norm(alignment, 2).astype(jnp.bfloat16).reshape(seq_here * cols_here, model_width)
    )
    left_proj = (
        jnp.dot(seq_normed, opm_left, preferred_element_type=jnp.float32)
        .astype(jnp.bfloat16)
        .reshape(seq_here, cols_here * factor_width)
    )
    right_proj = (
        jnp.dot(seq_normed, opm_right, preferred_element_type=jnp.float32)
        .astype(jnp.bfloat16)
        .reshape(seq_here, cols_here * factor_width)
    )
    per_col = n_row // n_col
    index_row = lax.axis_index("row")
    root_col = index_row // per_col
    right_all = lax.all_gather(right_proj, ("row", "seq"), axis=0, tiled=True)
    left_blocks = left_proj.reshape(seq_here, per_col * n_seq, rows_here * factor_width)
    left_send = jnp.tile(left_blocks, (1, n_col, 1))
    left_recv = lax.all_to_all(left_send, ("row", "seq"), split_axis=1, concat_axis=0, tiled=True)
    row_slice = left_recv.reshape(seq_here * n_row * n_seq, rows_here * factor_width)
    seqs_all = right_all.shape[0]
    row_factors = spread_2(row_slice, "col", root_col)
    right_wide = right_all.reshape(seqs_all, cols_here, factor_width)
    row_stack = jnp.swapaxes(row_factors.reshape(seqs_all, rows_here, factor_width), 0, 1)

    def outer_row(packed):
        row_vals, pair_row = packed
        outer_sum = jnp.einsum(
            "np,njq->jpq", row_vals, right_wide, preferred_element_type=jnp.float32
        )
        mean_outer = (
            (outer_sum * (1.0 / seqs_all))
            .astype(jnp.bfloat16)
            .reshape(cols_here, factor_width * factor_width)
        )
        return (
            pair_row.astype(jnp.float32)
            + jnp.dot(mean_outer, opm_out, preferred_element_type=jnp.float32)
        ).astype(jnp.bfloat16)

    pair_mid = lax.map(outer_row, (row_stack, pair))
    normed_pair = layer_norm(pair_mid, 2).astype(jnp.bfloat16)
    flat_pair = normed_pair.reshape(rows_here * cols_here, pair_width)

    def project(weight):
        return lax.dot_general(
            weight, flat_pair, (((0,), (1,)), ((), ())), preferred_element_type=jnp.float32
        )

    def gated(weight_gate, weight_value):
        gate_part = jax.nn.sigmoid(project(weight_gate))
        return (
            (gate_part * project(weight_value))
            .astype(jnp.bfloat16)
            .reshape(hidden, rows_here, cols_here)
        )

    left_first = gated(tri_left_gate, tri_left)
    right_first = gated(tri_right_gate, tri_right)
    left_local, right_local = (
        lax.all_to_all(
            lax.all_to_all(left_first, "col", split_axis=0, concat_axis=2, tiled=True),
            "seq",
            split_axis=0,
            concat_axis=1,
            tiled=True,
        ),
        lax.all_to_all(
            lax.all_to_all(right_first, "col", split_axis=0, concat_axis=2, tiled=True),
            "seq",
            split_axis=0,
            concat_axis=1,
            tiled=True,
        ),
    )
    product = contract(left_local, lax.all_gather(right_local, "row", axis=1, tiled=True))
    product = product.astype(jnp.bfloat16)
    returned = lax.all_to_all(
        lax.all_to_all(product, "col", split_axis=2, concat_axis=0, tiled=True),
        "seq",
        split_axis=1,
        concat_axis=0,
        tiled=True,
    )
    per_group = hidden // (n_col * n_seq)
    weights_order = (
        tri_out.reshape(n_col, n_seq, per_group, pair_width)
        .transpose(1, 0, 2, 3)
        .reshape(hidden, pair_width)
    )
    normed_product = layer_norm(returned, 0).astype(jnp.bfloat16)
    update = jnp.einsum(
        "cij,cd->ijd", normed_product, weights_order, preferred_element_type=jnp.float32
    )
    gate_part = jax.nn.sigmoid(
        jnp.dot(flat_pair, tri_gate, preferred_element_type=jnp.float32)
    ).reshape(rows_here, cols_here, pair_width)
    return (pair_mid.astype(jnp.float32) + gate_part * update).astype(jnp.bfloat16)


def mul(a, b):
    return jnp.dot(a, b, preferred_element_type=F32)


def mul_t(a, b):
    return lax.dot_general(a, b, (((1,), (1,)), ((), ())), preferred_element_type=F32)


def ones_where(mask):
    return jnp.where(mask, 1.0, 0.0).astype(BF16)


def iotas(rows, cols):
    shape = (rows, cols)
    return lax.broadcasted_iota(jnp.int32, shape, 0), lax.broadcasted_iota(jnp.int32, shape, 1)


def identity(size):
    row, col = iotas(size, size)
    return ones_where(row == col)


def swap_rows(outer, inner):
    row, col = iotas(outer * inner, outer * inner)
    return ones_where(col == (row % outer) * inner + row // outer)


def normalize(values, axis):
    center = values - jnp.mean(values, axis=axis, keepdims=True)
    spread = jnp.mean(center * center, axis=axis, keepdims=True)
    return center * lax.rsqrt(spread + EPS)


def fetch(sems, pairs):
    copies = [
        pltpu.make_async_copy(source, target, sems.at[k]) for k, (source, target) in enumerate(pairs)
    ]
    for copy in copies:
        copy.start()
    return copies


def factors_kernel(sizes, align_in, left_in, right_in, *refs):
    n_far, n_near, n_core, rows, _ = sizes
    out_refs, (parts, align_ref, left_ref, right_ref, own_lane, picks, sems) = refs[:n_far], refs[n_far:]
    pairs = [(left_in, left_ref), (right_in, right_ref)]
    pairs += [(align_in, align_ref)]
    copies = fetch(sems, pairs)
    seqs, cols, width = align_ref.shape
    factor = left_ref.shape[0]
    chip_rows = n_core * rows
    row, col = iotas(chip_rows * factor, factor)
    widen = ones_where(row % factor == col)
    row, col = iotas(cols, chip_rows * factor)
    own_lane[...] = ones_where((row % chip_rows) == (col // factor))
    row, col = iotas(n_far * seqs * n_near, cols)
    chip_of_row = (row // (seqs * n_near)) * n_near + row % n_near
    chip_match = chip_of_row == col // chip_rows
    seq_of_row = (row // n_near) % seqs
    for n in range(seqs):
        picks[n] = ones_where(chip_match & (seq_of_row == n))
    copies[0].wait()
    copies[1].wait()
    left_wide = mul(widen, left_ref[...]).astype(BF16)
    right_rows, left_rows = [], None
    for n in range(seqs):
        if n == 0:
            copies[2].wait()
        normed = normalize(align_ref[n].astype(F32), 1).astype(BF16)
        right_rows.append(mul_t(right_ref[...], normed))
        spread = mul_t(normed, left_wide).astype(BF16) * own_lane[...]
        part = mul(picks[n], spread)
        left_rows = part if left_rows is None else left_rows + part
    right_block = jnp.concatenate(right_rows, 0).astype(BF16)
    part_rows = seqs * n_near
    pieces = n_core
    for far in range(n_far):
        for piece in range(pieces):
            parts[far, piece * part_rows : (piece + 1) * part_rows, :] = left_rows[
                far * part_rows : (far + 1) * part_rows, piece * cols : (piece + 1) * cols
            ].astype(BF16)
    here = lax.axis_index("row") // 2
    for k in range(n_far):
        out_refs[k][: seqs * factor, :] = right_block
        out_refs[k][seqs * factor :, :] = parts[here ^ k]


def near_index(n_near, n_core):
    return (lax.axis_index("row") % 2) * (n_near // 2) + lax.axis_index("seq") // n_core


def regroup(sizes, factor, seqs, blocks, out_refs):
    held = sizes[0] * seqs
    half = 256 // held
    shuffle = swap_rows(held, half)
    for h in range(factor // half):
        block = jnp.concatenate(
            [
                ref[at + n * factor + h * half : at + n * factor + (h + 1) * half, :]
                for ref, at in blocks
                for n in range(seqs)
            ],
            0,
        )
        block = mul(shuffle, block).astype(BF16)
        for ref in out_refs:
            ref[h * half * held : (h + 1) * half * held, :] = block


def regroup_kernel(sizes, factor, seqs, *refs):
    n_far, n_near, n_core, _, _ = sizes
    in_refs, out_refs, parts = refs[:n_far], refs[n_far : n_far + n_near], refs[-1]
    held, part_rows, base = n_far * seqs, seqs * n_near, seqs * factor
    regroup(sizes, factor, seqs, [(ref, 0) for ref in in_refs], out_refs[:-1])
    for far in range(1, n_far):
        out_refs[-1][(far - 1) * base : far * base, :] = in_refs[far][:base, :]
    pick = swap_rows(held, n_near)
    row, _ = iotas(held * n_near, held * n_near)
    pick_late = jnp.where(row % held < seqs, 0.0, pick.astype(F32)).astype(BF16)
    for piece in range(n_core):
        block = jnp.concatenate(
            [ref[base + piece * part_rows : base + (piece + 1) * part_rows, :] for ref in in_refs], 0
        )
        for late, matrix in enumerate((pick, pick_late)):
            rows = mul(matrix, block).astype(BF16)
            for near in range(n_near):
                parts[late, near, piece * held : (piece + 1) * held, :] = rows[
                    near * held : (near + 1) * held
                ]
    here = near_index(n_near, n_core)
    for k in range(n_near - 1):
        out_refs[k][factor * held :, :] = parts[0, here ^ k]
    out_refs[-1][(n_far - 1) * base :, :] = parts[1, here ^ (n_near - 1)]


def merge_kernel(sizes, factor, seqs, early_ref, late_ref, out_ref):
    n_far, n_near, n_core, _, _ = sizes
    held, part_rows, base = n_far * seqs, seqs * n_near, seqs * factor
    blocks = [(early_ref, 0)] + [(late_ref, far * base) for far in range(n_far - 1)]
    regroup(sizes, factor, seqs, blocks, [out_ref])
    row, col = iotas(n_core * held, n_core * part_rows)
    slot = row // held * part_rows + row % held * n_near + near_index(n_near, n_core)
    pick = ones_where((row % held < seqs) & (col == slot))
    own = mul(pick, early_ref[base:, :])
    out_ref[factor * held :, :] = (own + late_ref[(n_far - 1) * base :, :].astype(F32)).astype(BF16)


def prepare_kernel(factor, *refs):
    n = (len(refs) - 6) // 2
    sources, (pair_t, out_t, tri_t, gate_t, final_t), targets = refs[:n], refs[n : n + 5], refs[n + 5 : -1]
    copies = fetch(refs[-1], list(zip(sources, targets, strict=True)))
    pair_ref, out_w, *tri, gate_w, final_w = targets
    eye = identity(pair_ref.shape[2])
    for copy in copies:
        copy.wait()
    for i in range(pair_ref.shape[0]):
        pair_t[i] = mul_t(eye, pair_ref[i]).astype(BF16)
    shuffle = swap_rows(256 // 16, 16)
    for q in range(0, factor, 16):
        for p in range(0, factor, 256 // 16):
            block = jnp.concatenate(
                [
                    out_w[(p + k) * factor + q : (p + k) * factor + q + 16, :]
                    for k in range(256 // 16)
                ],
                0,
            )
            block = mul(shuffle, block).astype(BF16)
            block = mul_t(eye, block).astype(BF16)
            at = (q // 16 * (factor // 16) + p // 16) * 256
            out_t[:, at : at + 256] = block
    for k, ref in enumerate(tri):
        width = ref.shape[1]
        tri_t[k * width : (k + 1) * width, :] = mul_t(eye, ref[...]).astype(BF16)
    gate_t[...] = mul_t(eye, gate_w[...]).astype(BF16)
    final_t[...] = mul_t(eye, final_w[...]).astype(BF16)


def pair_kernel(sizes, held, scale, *refs):
    n_core, rows, n_dev = sizes[2], sizes[3], sizes[4]
    groups = refs[:-11]
    pair_ref, out_w, tri_w, send_ref, left_ref, mid_ref, norm_ref, outer, both, right_ref, sems = refs[-11:]
    factor = groups[0].shape[0] // held - n_core
    hidden = tri_w.shape[0] // 4
    core = lax.axis_index("seq") % n_core
    at = pl.multiple_of((factor + core) * held, held)
    left = jnp.concatenate([ref[pl.ds(at, held), :] for ref in groups], 0)
    left_t = mul_t(identity(rows * factor), left).astype(BF16)
    for q in range(factor):
        right = jnp.concatenate([ref[q * held : (q + 1) * held, :] for ref in groups], 0)
        block = mul(left_t, right).astype(BF16)
        for i in range(rows):
            for p in range(0, factor, 16):
                at = (q // 16 * (factor // 16) + p // 16) * 256 + q % 16 * 16
                outer[i, at : at + 16, :] = block[i * factor + p : i * factor + p + 16]
    updates = [
        mul(out_w[...], jnp.concatenate([outer[i], outer[i + 1]], 1)) for i in range(0, rows, 2)
    ]
    cols = pair_ref.shape[2]
    for i in range(rows):
        update = updates[i // 2][:, i % 2 * cols : (i % 2 + 1) * cols]
        mid = (pair_ref[i].astype(F32) + update * scale).astype(BF16)
        mid_ref[i] = mid
        normed = normalize(mid.astype(F32), 0).astype(BF16)
        norm_ref[i] = normed
    half = n_dev // 2
    chunk = hidden // half * rows
    some = 256 // rows
    shuffle = swap_rows(rows, some)
    per = some * rows // chunk

    def by_channels(side):
        at = 2 * side * hidden
        for i in range(rows):
            parts = mul(tri_w[at : at + 2 * hidden, :], norm_ref[i])
            both[side, i] = (jax.nn.sigmoid(parts[:hidden]) * parts[hidden:]).astype(BF16)
        blocks = [
            jnp.concatenate([both[side, i, b * some : (b + 1) * some, :] for i in range(rows)], 0)
            for b in range(hidden // some)
        ]
        return [mul(shuffle, block).astype(BF16) for block in blocks]

    copies = []
    for b, block in enumerate(by_channels(1)):
        right_ref[b * per * chunk : (b + 1) * per * chunk, :] = block
        if b % 2 == 1:
            size = 2 * per * chunk
            source = right_ref.at[pl.ds((b - 1) * per * chunk, size)]
            for h in range(2):
                target = send_ref.at[pl.ds((h * half + (b - 1) * per) * chunk, size)]
                copies.append(pltpu.make_async_copy(source, target, sems.at[len(copies)]))
                copies[-1].start()
    for b, block in enumerate(by_channels(0)):
        for d in range(per):
            to = (d % n_core * half + b * per + d) // n_core * chunk
            left_ref[to : to + chunk, :] = block[d * chunk : (d + 1) * chunk]
    for copy in copies:
        copy.wait()


def half_index(sizes):
    n_far, n_near, n_core, _, _ = sizes
    n_y = n_near // 2
    row = lax.axis_index("row") % n_far
    return row * n_y + lax.axis_index("seq") // n_core


def left_kernel(sizes, own_ref, came_ref, *out_refs):
    n_core = sizes[2]
    chunk = own_ref.shape[0] // len(out_refs) // n_core
    core = lax.axis_index("seq") % n_core
    here = half_index(sizes)
    rows = sizes[3]
    per, cols = chunk // rows, own_ref.shape[1]
    for k, ref in enumerate(out_refs):
        at = pl.multiple_of((core * len(out_refs) + (here ^ k)) * chunk, chunk)
        own = own_ref[pl.ds(at, chunk), :].astype(F32).reshape(per, rows, cols)
        came = came_ref[pl.ds(at, chunk), :].astype(F32).reshape(per, rows, cols)
        pair = [jnp.where(core == 0, own, came), jnp.where(core == 0, came, own)]
        ref[...] = jnp.concatenate(pair, 1).reshape(n_core * chunk, cols).astype(BF16)


def product_kernel(sizes, per, recv_ref, *refs):
    n_core, rows, n_dev = sizes[2], sizes[3], sizes[4]
    half, chunk = n_dev // 2, per * rows
    chips = half // n_core
    left_refs, (send_ref, left, right, total) = refs[:chips], refs[chips:]
    here = half_index(sizes)
    for src in range(n_dev):
        block = recv_ref[src * chunk : (src + 1) * chunk, :].astype(F32)
        for c in range(per):
            right[c, src * rows : (src + 1) * rows, :] = block[c * rows : (c + 1) * rows]
    for k, ref in enumerate(left_refs):
        at = pl.multiple_of((here ^ k) * n_core * rows, n_core * rows)
        for c in range(per):
            left[c, pl.ds(at, n_core * rows), :] = ref[c * n_core * rows : (c + 1) * n_core * rows, :]
    for c in range(per):
        prod = mul_t(left[c], right[c].astype(BF16))
        for dst in range(half):
            total[dst, c * rows : (c + 1) * rows, :] = prod[dst * rows : (dst + 1) * rows]
    for dst in range(half):
        send_ref[dst * chunk : (dst + 1) * chunk, :] = total[dst].astype(BF16)


def finish_kernel(sizes, recv_ref, mid_ref, norm_ref, gate_w, out_w, out_ref, apart, done_ref, sems):
    rows = sizes[3]
    _, width, cols = mid_ref.shape
    hidden = out_w.shape[1]
    some = 256 // rows
    blocks = hidden // some
    count = some * rows

    def piece(b):
        return recv_ref[b * count : (b + 1) * count, :].astype(F32).reshape(some, rows, cols)

    mean = sum(jnp.sum(piece(b), 0) for b in range(blocks)) * (1.0 / hidden)
    spread = sum(jnp.sum((piece(b) - mean) ** 2, 0) for b in range(blocks)) * (1.0 / hidden)
    factor = lax.rsqrt(spread + EPS)
    shuffle = swap_rows(some, rows)
    normed = [
        ((piece(b) - mean) * factor).reshape(count, cols).astype(BF16) for b in range(blocks)
    ]
    normed = [mul(shuffle, block).astype(BF16) for block in normed]
    for b in range(blocks):
        for i in range(rows):
            apart[i, b * some : (b + 1) * some, :] = normed[b][i * some : (i + 1) * some]
    eye = identity(cols)
    copies = []
    gates = [mul(gate_w[...], norm_ref[i]) for i in range(rows)]
    updates = [mul(out_w[...], apart[i]) for i in range(rows)]
    dones = [(mid_ref[i].astype(F32) + jax.nn.sigmoid(gates[i]) * updates[i]).astype(BF16) for i in range(rows)]
    for i in range(rows):
        done_ref[i] = mul_t(eye, dones[i]).astype(BF16)
        copies.append(pltpu.make_async_copy(done_ref.at[i], out_ref.at[i], sems.at[i]))
        copies[i].start()
    for copy in copies:
        copy.wait()


def call(kernel, out_shape, scratch, grant, flops, *args, far_in=False, far_out=False):
    if isinstance(far_out, bool):
        far_out = [far_out] * len(out_shape)
    out_specs = [pl.BlockSpec(memory_space=pltpu.HBM if far else pltpu.VMEM) for far in far_out]
    out_shape = [
        (jax.ShapeDtypeStruct if far else pltpu.VMEM)(*(s if isinstance(s[0], tuple) else (s, BF16)))
        for s, far in zip(out_shape, far_out, strict=True)
    ]
    if far_in:
        args = [pltpu.with_memory_space_constraint(a, pltpu.HBM) for a in args]
    moved = sum(math.prod(a.shape) * jnp.dtype(a.dtype).itemsize for a in (*args, *out_shape))
    return pl.pallas_call(
        kernel,
        out_shape=out_shape,
        in_specs=[pl.BlockSpec(memory_space=pltpu.HBM if far_in else pltpu.VMEM)] * len(args),
        out_specs=out_specs,
        scratch_shapes=scratch,
        compiler_params=pltpu.CompilerParams(vmem_limit_bytes=grant * 2**20),
        cost_estimate=pl.CostEstimate(flops=flops, bytes_accessed=moved, transcendentals=0),
    )(*args)


def factors_call(sizes, alignment, opm_left, opm_right):
    n_far, n_near, n_core, rows, _ = sizes
    seqs, cols, width = alignment.shape
    factor = opm_left.shape[1]
    return call(
        functools.partial(factors_kernel, sizes),
        [(seqs * factor + n_core * seqs * n_near, cols)] * n_far,
        [
            pltpu.VMEM((n_far, n_core * seqs * n_near, cols), BF16),
            pltpu.VMEM(alignment.shape, BF16),
            pltpu.VMEM(opm_left.shape[::-1], BF16),
            pltpu.VMEM(opm_right.shape[::-1], BF16),
            pltpu.VMEM((cols, n_core * rows * factor), BF16),
            pltpu.VMEM((seqs, n_far * seqs * n_near, cols), BF16),
            pltpu.SemaphoreType.DMA((2 + seqs,)),
        ],
        8,
        4 * seqs * cols * width * factor,
        alignment,
        opm_left.T,
        opm_right.T,
        far_in=True,
    )


def whole_channels(
    pair,
    alignment,
    opm_left,
    opm_right,
    opm_out,
    tri_left,
    tri_left_gate,
    tri_right,
    tri_right_gate,
    tri_gate,
    tri_out,
):
    rows, cols, width = pair.shape
    seqs = alignment.shape[0]
    factor = opm_left.shape[1]
    hidden = tri_left.shape[1]
    n_row, n_seq = lax.axis_size("row"), lax.axis_size("seq")
    n_dev = n_row * n_seq
    n_core = 2
    n_far, n_near = n_row // 2, 2 * (n_seq // n_core)
    n_y = n_near // 2
    sizes = (n_far, n_near, n_core, rows, n_dev)
    held = n_far * seqs
    half = n_dev // 2
    per = hidden // half
    chips = half // n_core

    def exchange(value, row_bits, seq_bits):
        pairs = [
            (r * n_seq + s, (r ^ row_bits) * n_seq + (s ^ seq_bits))
            for r in range(n_row)
            for s in range(n_seq)
        ]
        return lax.ppermute(value, BOTH, pairs)

    mine = factors_call(sizes, alignment, opm_left, opm_right)
    weights = (
        pair,
        opm_out,
        tri_left_gate,
        tri_left,
        tri_right_gate,
        tri_right,
        tri_gate,
        tri_out,
    )
    mine, weights = lax.optimization_barrier((mine, weights))
    def to_near(value, k):
        return exchange(value, k // n_y, (k % n_y) * n_core)

    far = [exchange(mine[k], 2 * k, 0) for k in range(n_far - 1, 0, -1)]
    early = to_near(mine[0], n_near - 1)
    far = [mine[0], far[0], far[2], far[1]]
    prepared = call(
        functools.partial(prepare_kernel, factor),
        [
            (rows, width, cols),
            (width, factor * factor),
            (4 * hidden, width),
            (width, width),
            (width, hidden),
        ],
        [pltpu.VMEM(w.shape, BF16) for w in weights] + [pltpu.SemaphoreType.DMA((len(weights),))],
        8,
        4 * rows * cols * width * width,
        *weights,
        far_in=True,
    )
    early, far, prepared = lax.optimization_barrier((early, far, prepared))
    pair_t, out_t, tri_t, gate_t, final_t = prepared
    message = ((factor + n_core) * held, cols)
    late = ((n_far - 1) * seqs * factor + n_core * held, cols)
    mine = call(
        functools.partial(regroup_kernel, sizes, factor, seqs),
        [message] * (n_near - 1) + [late],
        [pltpu.VMEM((2, n_near, n_core * held, cols), BF16)],
        8,
        2 * 256 * factor * held * cols,
        *far,
    )
    near = [to_near(mine[k], k) for k in range(n_near - 1, 0, -1)]
    (near[0],) = call(
        functools.partial(merge_kernel, sizes, factor, seqs),
        [message],
        [],
        8,
        2 * 256 * factor * held * cols,
        early,
        near[0],
    )
    near = [mine[0]] + near
    groups = near + [exchange(block, 0, 1) for block in near]
    scale = 1.0 / (held * n_near * n_core)
    send, left, mid, normed = call(
        functools.partial(pair_kernel, sizes, held, scale),
        [
            (2 * hidden * rows, cols),
            (hidden * rows, cols),
            (rows, width, cols),
            (rows, width, cols),
        ],
        [
            pltpu.VMEM((rows, factor * factor, cols), BF16),
            pltpu.VMEM((2, rows, hidden, cols), BF16),
            pltpu.VMEM((hidden * rows, cols), BF16),
            pltpu.SemaphoreType.DMA((hidden * rows // 256,)),
        ],
        16,
        4 * rows * cols * width * (factor * factor + hidden * 2),
        *groups,
        pair_t,
        out_t,
        tri_t,
        far_out=(True, False, False, False),
    )
    recv = lax.all_to_all(send, BOTH, split_axis=0, concat_axis=0, tiled=True)
    mine = call(
        functools.partial(left_kernel, sizes),
        [(n_core * per * rows, cols)] * chips,
        [],
        8,
        0,
        left,
        exchange(left, 0, 1),
    )
    lefts = [mine[0]]
    for k in range(1, chips):
        lefts.append(exchange(mine[k], k // n_y, k % n_y * n_core))
    (send,) = call(
        functools.partial(product_kernel, sizes, per),
        [(hidden * rows, cols)],
        [
            pltpu.VMEM((per, rows * half, cols), BF16),
            pltpu.VMEM((per, rows * n_dev, cols), F32),
            pltpu.VMEM((half, per * rows, cols), F32),
        ],
        16,
        2 * per * cols * cols * cols // 2,
        recv,
        *lefts,
    )
    halves = [list(range(half)), list(range(half, n_dev))]
    recv = lax.all_to_all(
        send, BOTH, split_axis=0, concat_axis=0, tiled=True, axis_index_groups=halves
    )
    (out,) = call(
        functools.partial(finish_kernel, sizes),
        [(rows, cols, width)],
        [
            pltpu.VMEM((rows, hidden, cols), BF16),
            pltpu.VMEM((rows, cols, width), BF16),
            pltpu.SemaphoreType.DMA((rows,)),
        ],
        16,
        4 * rows * cols * width * hidden,
        recv,
        mid,
        normed,
        gate_t,
        final_t,
        far_out=True,
    )
    return out


def power_of_two(n):
    return n & (n - 1) == 0


def on_device(pair, alignment, opm_left, *rest):
    rows, cols, width = pair.shape
    factor, hidden = opm_left.shape[1], rest[2].shape[1]
    n_row, n_col, n_seq = (lax.axis_size(a) for a in ("row", "col", "seq"))
    n_dev = n_row * n_seq
    held = n_row // 2 * alignment.shape[0]
    fits = (
        n_col == 1
        and power_of_two(n_row)
        and power_of_two(n_seq)
        and power_of_two(rows)
        and n_row >= 4
        and n_seq >= 4
        and hidden % n_dev == 0
        and hidden == width
        and factor % 16 == 0
        and rows % 8 == 0
        and (hidden // n_dev * rows) % 16 == 0
        and cols % 256 == 0
        and rows * factor == cols
        and rows * n_dev == cols
        and held % 16 == 0
        and 256 % held == 0
        and factor % (256 // held) == 0
        and hidden % (256 // rows) == 0
        and power_of_two(held * n_seq * 2)
    )
    plan = whole_channels if fits else by_groups
    return plan(pair, alignment, opm_left, *rest)


def solution(mesh):
    return jax.shard_map(
        on_device,
        mesh=mesh,
        in_specs=(
            P(("row", "seq"), "col", None),
            P(("row", "seq"), "col", None),
            P(),
            P(),
            P(),
            P(),
            P(),
            P(),
            P(),
            P(),
            P(),
        ),
        out_specs=P(("row", "seq"), "col", None),
        check_vma=False,
    )
```

```python
import functools
import math

import jax
import jax.numpy as jnp
from jax import lax
from jax.experimental import pallas as pl
from jax.experimental.pallas import tpu as pltpu
from jax.sharding import PartitionSpec as P

EPS = 1e-05
BOTH = ("row", "seq")
BF16 = jnp.bfloat16
F32 = jnp.float32


def spread_2(shard, axis, root):
    mine = lax.axis_index(axis) == root
    return lax.psum(jnp.where(mine, shard, jnp.zeros_like(shard)), axis)


def layer_norm(values, axis):
    values = values.astype(jnp.float32)
    center = values - jnp.mean(values, axis=axis, keepdims=True)
    spread = jnp.mean(center * center, axis=axis, keepdims=True)
    return center * lax.rsqrt(spread + EPS)


def contract(local_rows, piece):
    return jnp.einsum("cik,cjk->cij", local_rows, piece, preferred_element_type=jnp.float32)


def by_groups(
    pair,
    alignment,
    opm_left,
    opm_right,
    opm_out,
    tri_left,
    tri_left_gate,
    tri_right,
    tri_right_gate,
    tri_gate,
    tri_out,
):
    rows_here, cols_here, pair_width = pair.shape
    seq_here = alignment.shape[0]
    model_width = alignment.shape[2]
    factor_width = opm_left.shape[1]
    hidden = tri_left.shape[1]
    n_row = lax.axis_size("row")
    n_col = lax.axis_size("col")
    n_seq = lax.axis_size("seq")
    seq_normed = (
        layer_norm(alignment, 2).astype(jnp.bfloat16).reshape(seq_here * cols_here, model_width)
    )
    left_proj = (
        jnp.dot(seq_normed, opm_left, preferred_element_type=jnp.float32)
        .astype(jnp.bfloat16)
        .reshape(seq_here, cols_here * factor_width)
    )
    right_proj = (
        jnp.dot(seq_normed, opm_right, preferred_element_type=jnp.float32)
        .astype(jnp.bfloat16)
        .reshape(seq_here, cols_here * factor_width)
    )
    per_col = n_row // n_col
    index_row = lax.axis_index("row")
    root_col = index_row // per_col
    right_all = lax.all_gather(right_proj, ("row", "seq"), axis=0, tiled=True)
    left_blocks = left_proj.reshape(seq_here, per_col * n_seq, rows_here * factor_width)
    left_send = jnp.tile(left_blocks, (1, n_col, 1))
    left_recv = lax.all_to_all(left_send, ("row", "seq"), split_axis=1, concat_axis=0, tiled=True)
    row_slice = left_recv.reshape(seq_here * n_row * n_seq, rows_here * factor_width)
    seqs_all = right_all.shape[0]
    row_factors = spread_2(row_slice, "col", root_col)
    right_wide = right_all.reshape(seqs_all, cols_here, factor_width)
    row_stack = jnp.swapaxes(row_factors.reshape(seqs_all, rows_here, factor_width), 0, 1)

    def outer_row(packed):
        row_vals, pair_row = packed
        outer_sum = jnp.einsum(
            "np,njq->jpq", row_vals, right_wide, preferred_element_type=jnp.float32
        )
        mean_outer = (
            (outer_sum * (1.0 / seqs_all))
            .astype(jnp.bfloat16)
            .reshape(cols_here, factor_width * factor_width)
        )
        return (
            pair_row.astype(jnp.float32)
            + jnp.dot(mean_outer, opm_out, preferred_element_type=jnp.float32)
        ).astype(jnp.bfloat16)

    pair_mid = lax.map(outer_row, (row_stack, pair))
    normed_pair = layer_norm(pair_mid, 2).astype(jnp.bfloat16)
    flat_pair = normed_pair.reshape(rows_here * cols_here, pair_width)

    def project(weight):
        return lax.dot_general(
            weight, flat_pair, (((0,), (1,)), ((), ())), preferred_element_type=jnp.float32
        )

    def gated(weight_gate, weight_value):
        gate_part = jax.nn.sigmoid(project(weight_gate))
        return (
            (gate_part * project(weight_value))
            .astype(jnp.bfloat16)
            .reshape(hidden, rows_here, cols_here)
        )

    left_first = gated(tri_left_gate, tri_left)
    right_first = gated(tri_right_gate, tri_right)
    left_local, right_local = (
        lax.all_to_all(
            lax.all_to_all(left_first, "col", split_axis=0, concat_axis=2, tiled=True),
            "seq",
            split_axis=0,
            concat_axis=1,
            tiled=True,
        ),
        lax.all_to_all(
            lax.all_to_all(right_first, "col", split_axis=0, concat_axis=2, tiled=True),
            "seq",
            split_axis=0,
            concat_axis=1,
            tiled=True,
        ),
    )
    product = contract(left_local, lax.all_gather(right_local, "row", axis=1, tiled=True))
    product = product.astype(jnp.bfloat16)
    returned = lax.all_to_all(
        lax.all_to_all(product, "col", split_axis=2, concat_axis=0, tiled=True),
        "seq",
        split_axis=1,
        concat_axis=0,
        tiled=True,
    )
    per_group = hidden // (n_col * n_seq)
    weights_order = (
        tri_out.reshape(n_col, n_seq, per_group, pair_width)
        .transpose(1, 0, 2, 3)
        .reshape(hidden, pair_width)
    )
    normed_product = layer_norm(returned, 0).astype(jnp.bfloat16)
    update = jnp.einsum(
        "cij,cd->ijd", normed_product, weights_order, preferred_element_type=jnp.float32
    )
    gate_part = jax.nn.sigmoid(
        jnp.dot(flat_pair, tri_gate, preferred_element_type=jnp.float32)
    ).reshape(rows_here, cols_here, pair_width)
    return (pair_mid.astype(jnp.float32) + gate_part * update).astype(jnp.bfloat16)


def mul(a, b):
    return jnp.dot(a, b, preferred_element_type=F32)


def mul_t(a, b):
    return lax.dot_general(a, b, (((1,), (1,)), ((), ())), preferred_element_type=F32)


def ones_where(mask):
    return jnp.where(mask, 1.0, 0.0).astype(BF16)


def iotas(rows, cols):
    shape = (rows, cols)
    return lax.broadcasted_iota(jnp.int32, shape, 0), lax.broadcasted_iota(jnp.int32, shape, 1)


def identity(size):
    row, col = iotas(size, size)
    return ones_where(row == col)


def swap_rows(outer, inner):
    row, col = iotas(outer * inner, outer * inner)
    return ones_where(col == (row % outer) * inner + row // outer)


def normalize(values, axis):
    center = values - jnp.mean(values, axis=axis, keepdims=True)
    spread = jnp.mean(center * center, axis=axis, keepdims=True)
    return center * lax.rsqrt(spread + EPS)


def fetch(sems, pairs):
    copies = [
        pltpu.make_async_copy(source, target, sems.at[k]) for k, (source, target) in enumerate(pairs)
    ]
    for copy in copies:
        copy.start()
    return copies


def factors_kernel(sizes, align_in, left_in, right_in, *refs):
    n_far, n_near, n_core, rows, _ = sizes
    out_refs, (parts, align_ref, left_ref, right_ref, own_lane, picks, sems) = refs[:n_far], refs[n_far:]
    pairs = [(left_in, left_ref), (right_in, right_ref)]
    pairs += [(align_in, align_ref)]
    copies = fetch(sems, pairs)
    seqs, cols, width = align_ref.shape
    factor = left_ref.shape[0]
    chip_rows = n_core * rows
    row, col = iotas(chip_rows * factor, factor)
    widen = ones_where(row % factor == col)
    row, col = iotas(cols, chip_rows * factor)
    own_lane[...] = ones_where((row % chip_rows) == (col // factor))
    row, col = iotas(n_far * seqs * n_near, cols)
    chip_of_row = (row // (seqs * n_near)) * n_near + row % n_near
    chip_match = chip_of_row == col // chip_rows
    seq_of_row = (row // n_near) % seqs
    for n in range(seqs):
        picks[n] = ones_where(chip_match & (seq_of_row == n))
    copies[0].wait()
    copies[1].wait()
    left_wide = mul(widen, left_ref[...]).astype(BF16)
    right_rows, left_rows = [], None
    for n in range(seqs):
        if n == 0:
            copies[2].wait()
        normed = normalize(align_ref[n].astype(F32), 1).astype(BF16)
        right_rows.append(mul_t(right_ref[...], normed))
        spread = mul_t(normed, left_wide).astype(BF16) * own_lane[...]
        part = mul(picks[n], spread)
        left_rows = part if left_rows is None else left_rows + part
    right_block = jnp.concatenate(right_rows, 0).astype(BF16)
    part_rows = seqs * n_near
    pieces = n_core
    for far in range(n_far):
        for piece in range(pieces):
            parts[far, piece * part_rows : (piece + 1) * part_rows, :] = left_rows[
                far * part_rows : (far + 1) * part_rows, piece * cols : (piece + 1) * cols
            ].astype(BF16)
    here = lax.axis_index("row") // 2
    for k in range(n_far):
        out_refs[k][: seqs * factor, :] = right_block
        out_refs[k][seqs * factor :, :] = parts[here ^ k]


def near_index(n_near, n_core):
    return (lax.axis_index("row") % 2) * (n_near // 2) + lax.axis_index("seq") // n_core


def regroup(sizes, factor, seqs, blocks, out_refs):
    held = sizes[0] * seqs
    half = 256 // held
    shuffle = swap_rows(held, half)
    for h in range(factor // half):
        block = jnp.concatenate(
            [
                ref[at + n * factor + h * half : at + n * factor + (h + 1) * half, :]
                for ref, at in blocks
                for n in range(seqs)
            ],
            0,
        )
        block = mul(shuffle, block).astype(BF16)
        for ref in out_refs:
            ref[h * half * held : (h + 1) * half * held, :] = block


def regroup_kernel(sizes, factor, seqs, *refs):
    n_far, n_near, n_core, _, _ = sizes
    in_refs, out_refs, parts = refs[:n_far], refs[n_far : n_far + n_near], refs[-1]
    held, part_rows, base = n_far * seqs, seqs * n_near, seqs * factor
    regroup(sizes, factor, seqs, [(ref, 0) for ref in in_refs], out_refs[:-1])
    for far in range(1, n_far):
        out_refs[-1][(far - 1) * base : far * base, :] = in_refs[far][:base, :]
    pick = swap_rows(held, n_near)
    row, _ = iotas(held * n_near, held * n_near)
    pick_late = jnp.where(row % held < seqs, 0.0, pick.astype(F32)).astype(BF16)
    for piece in range(n_core):
        block = jnp.concatenate(
            [ref[base + piece * part_rows : base + (piece + 1) * part_rows, :] for ref in in_refs], 0
        )
        for late, matrix in enumerate((pick, pick_late)):
            rows = mul(matrix, block).astype(BF16)
            for near in range(n_near):
                parts[late, near, piece * held : (piece + 1) * held, :] = rows[
                    near * held : (near + 1) * held
                ]
    here = near_index(n_near, n_core)
    for k in range(n_near - 1):
        out_refs[k][factor * held :, :] = parts[0, here ^ k]
    out_refs[-1][(n_far - 1) * base :, :] = parts[1, here ^ (n_near - 1)]


def merge_kernel(sizes, factor, seqs, early_ref, late_ref, out_ref):
    n_far, n_near, n_core, _, _ = sizes
    held, part_rows, base = n_far * seqs, seqs * n_near, seqs * factor
    blocks = [(early_ref, 0)] + [(late_ref, far * base) for far in range(n_far - 1)]
    regroup(sizes, factor, seqs, blocks, [out_ref])
    row, col = iotas(n_core * held, n_core * part_rows)
    slot = row // held * part_rows + row % held * n_near + near_index(n_near, n_core)
    pick = ones_where((row % held < seqs) & (col == slot))
    own = mul(pick, early_ref[base:, :])
    out_ref[factor * held :, :] = (own + late_ref[(n_far - 1) * base :, :].astype(F32)).astype(BF16)


def prepare_kernel(factor, *refs):
    n = (len(refs) - 6) // 2
    sources, (pair_t, out_t, tri_t, gate_t, final_t), targets = refs[:n], refs[n : n + 5], refs[n + 5 : -1]
    copies = fetch(refs[-1], list(zip(sources, targets, strict=True)))
    pair_ref, out_w, *tri, gate_w, final_w = targets
    eye = identity(pair_ref.shape[2])
    for copy in copies:
        copy.wait()
    for i in range(pair_ref.shape[0]):
        pair_t[i] = mul_t(eye, pair_ref[i]).astype(BF16)
    shuffle = swap_rows(256 // 16, 16)
    for q in range(0, factor, 16):
        for p in range(0, factor, 256 // 16):
            block = jnp.concatenate(
                [
                    out_w[(p + k) * factor + q : (p + k) * factor + q + 16, :]
                    for k in range(256 // 16)
                ],
                0,
            )
            block = mul(shuffle, block).astype(BF16)
            block = mul_t(eye, block).astype(BF16)
            at = (q // 16 * (factor // 16) + p // 16) * 256
            out_t[:, at : at + 256] = block
    for k, ref in enumerate(tri):
        width = ref.shape[1]
        tri_t[k * width : (k + 1) * width, :] = mul_t(eye, ref[...]).astype(BF16)
    gate_t[...] = mul_t(eye, gate_w[...]).astype(BF16)
    final_t[...] = mul_t(eye, final_w[...]).astype(BF16)


def pair_kernel(sizes, held, scale, *refs):
    n_core, rows, n_dev = sizes[2], sizes[3], sizes[4]
    groups = refs[:-11]
    pair_ref, out_w, tri_w, send_ref, left_ref, mid_ref, norm_ref, outer, both, right_ref, sems = refs[-11:]
    factor = groups[0].shape[0] // held - n_core
    hidden = tri_w.shape[0] // 4
    core = lax.axis_index("seq") % n_core
    at = pl.multiple_of((factor + core) * held, held)
    left = jnp.concatenate([ref[pl.ds(at, held), :] for ref in groups], 0)
    left_t = mul_t(identity(rows * factor), left).astype(BF16)
    for q in range(factor):
        right = jnp.concatenate([ref[q * held : (q + 1) * held, :] for ref in groups], 0)
        block = mul(left_t, right).astype(BF16)
        for i in range(rows):
            for p in range(0, factor, 16):
                at = (q // 16 * (factor // 16) + p // 16) * 256 + q % 16 * 16
                outer[i, at : at + 16, :] = block[i * factor + p : i * factor + p + 16]
    updates = [
        mul(out_w[...], jnp.concatenate([outer[i], outer[i + 1]], 1)) for i in range(0, rows, 2)
    ]
    cols = pair_ref.shape[2]
    for i in range(rows):
        update = updates[i // 2][:, i % 2 * cols : (i % 2 + 1) * cols]
        mid = (pair_ref[i].astype(F32) + update * scale).astype(BF16)
        mid_ref[i] = mid
        normed = normalize(mid.astype(F32), 0).astype(BF16)
        norm_ref[i] = normed
    half = n_dev // 2
    chunk = hidden // half * rows
    some = 256 // rows
    shuffle = swap_rows(rows, some)
    per = some * rows // chunk

    def by_channels(side):
        at = 2 * side * hidden
        parts = [mul(tri_w[at : at + 2 * hidden, :], norm_ref[i]) for i in range(rows)]
        for i in range(rows):
            gate = jax.nn.sigmoid(parts[i][:hidden])
            both[side, i] = (gate * parts[i][hidden:]).astype(BF16)
        blocks = [
            jnp.concatenate([both[side, i, b * some : (b + 1) * some, :] for i in range(rows)], 0)
            for b in range(hidden // some)
        ]
        return [mul(shuffle, block).astype(BF16) for block in blocks]

    copies = []
    for b, block in enumerate(by_channels(1)):
        right_ref[b * per * chunk : (b + 1) * per * chunk, :] = block
        if b % 2 == 1:
            size = 2 * per * chunk
            source = right_ref.at[pl.ds((b - 1) * per * chunk, size)]
            for h in range(2):
                target = send_ref.at[pl.ds((h * half + (b - 1) * per) * chunk, size)]
                copies.append(pltpu.make_async_copy(source, target, sems.at[len(copies)]))
                copies[-1].start()
    for b, block in enumerate(by_channels(0)):
        for d in range(per):
            to = (d % n_core * half + b * per + d) // n_core * chunk
            left_ref[to : to + chunk, :] = block[d * chunk : (d + 1) * chunk]
    for copy in copies:
        copy.wait()


def half_index(sizes):
    n_far, n_near, n_core, _, _ = sizes
    n_y = n_near // 2
    row = lax.axis_index("row") % n_far
    return row * n_y + lax.axis_index("seq") // n_core


def left_kernel(sizes, own_ref, came_ref, *out_refs):
    n_core = sizes[2]
    chunk = own_ref.shape[0] // len(out_refs) // n_core
    core = lax.axis_index("seq") % n_core
    here = half_index(sizes)
    rows = sizes[3]
    per, cols = chunk // rows, own_ref.shape[1]
    for k, ref in enumerate(out_refs):
        at = pl.multiple_of((core * len(out_refs) + (here ^ k)) * chunk, chunk)
        own = own_ref[pl.ds(at, chunk), :].astype(F32).reshape(per, rows, cols)
        came = came_ref[pl.ds(at, chunk), :].astype(F32).reshape(per, rows, cols)
        pair = [jnp.where(core == 0, own, came), jnp.where(core == 0, came, own)]
        ref[...] = jnp.concatenate(pair, 1).reshape(n_core * chunk, cols).astype(BF16)


def product_kernel(sizes, per, recv_ref, *refs):
    n_core, rows, n_dev = sizes[2], sizes[3], sizes[4]
    half, chunk = n_dev // 2, per * rows
    chips = half // n_core
    left_refs, (send_ref, left, right, total) = refs[:chips], refs[chips:]
    here = half_index(sizes)
    for src in range(n_dev):
        block = recv_ref[src * chunk : (src + 1) * chunk, :].astype(F32)
        for c in range(per):
            right[c, src * rows : (src + 1) * rows, :] = block[c * rows : (c + 1) * rows]
    for k, ref in enumerate(left_refs):
        at = pl.multiple_of((here ^ k) * n_core * rows, n_core * rows)
        for c in range(per):
            left[c, pl.ds(at, n_core * rows), :] = ref[c * n_core * rows : (c + 1) * n_core * rows, :]
    for c in range(per):
        prod = mul_t(left[c], right[c].astype(BF16))
        for dst in range(half):
            total[dst, c * rows : (c + 1) * rows, :] = prod[dst * rows : (dst + 1) * rows]
    for dst in range(half):
        send_ref[dst * chunk : (dst + 1) * chunk, :] = total[dst].astype(BF16)


def finish_kernel(sizes, recv_ref, mid_ref, norm_ref, gate_w, out_w, out_ref, apart, done_ref, sems):
    rows = sizes[3]
    _, width, cols = mid_ref.shape
    hidden = out_w.shape[1]
    some = 256 // rows
    blocks = hidden // some
    count = some * rows

    def piece(b):
        return recv_ref[b * count : (b + 1) * count, :].astype(F32).reshape(some, rows, cols)

    mean = sum(jnp.sum(piece(b), 0) for b in range(blocks)) * (1.0 / hidden)
    spread = sum(jnp.sum((piece(b) - mean) ** 2, 0) for b in range(blocks)) * (1.0 / hidden)
    factor = lax.rsqrt(spread + EPS)
    shuffle = swap_rows(some, rows)
    normed = [
        ((piece(b) - mean) * factor).reshape(count, cols).astype(BF16) for b in range(blocks)
    ]
    normed = [mul(shuffle, block).astype(BF16) for block in normed]
    for b in range(blocks):
        for i in range(rows):
            apart[i, b * some : (b + 1) * some, :] = normed[b][i * some : (i + 1) * some]
    eye = identity(cols)
    copies = []
    gates = [mul(gate_w[...], norm_ref[i]) for i in range(rows)]
    updates = [mul(out_w[...], apart[i]) for i in range(rows)]
    dones = [(mid_ref[i].astype(F32) + jax.nn.sigmoid(gates[i]) * updates[i]).astype(BF16) for i in range(rows)]
    for i in range(rows):
        done_ref[i] = mul_t(eye, dones[i]).astype(BF16)
        copies.append(pltpu.make_async_copy(done_ref.at[i], out_ref.at[i], sems.at[i]))
        copies[i].start()
    for copy in copies:
        copy.wait()


def call(kernel, out_shape, scratch, grant, flops, *args, far_in=False, far_out=False):
    if isinstance(far_out, bool):
        far_out = [far_out] * len(out_shape)
    out_specs = [pl.BlockSpec(memory_space=pltpu.HBM if far else pltpu.VMEM) for far in far_out]
    out_shape = [
        (jax.ShapeDtypeStruct if far else pltpu.VMEM)(*(s if isinstance(s[0], tuple) else (s, BF16)))
        for s, far in zip(out_shape, far_out, strict=True)
    ]
    if far_in:
        args = [pltpu.with_memory_space_constraint(a, pltpu.HBM) for a in args]
    moved = sum(math.prod(a.shape) * jnp.dtype(a.dtype).itemsize for a in (*args, *out_shape))
    return pl.pallas_call(
        kernel,
        out_shape=out_shape,
        in_specs=[pl.BlockSpec(memory_space=pltpu.HBM if far_in else pltpu.VMEM)] * len(args),
        out_specs=out_specs,
        scratch_shapes=scratch,
        compiler_params=pltpu.CompilerParams(vmem_limit_bytes=grant * 2**20),
        cost_estimate=pl.CostEstimate(flops=flops, bytes_accessed=moved, transcendentals=0),
    )(*args)


def factors_call(sizes, alignment, opm_left, opm_right):
    n_far, n_near, n_core, rows, _ = sizes
    seqs, cols, width = alignment.shape
    factor = opm_left.shape[1]
    return call(
        functools.partial(factors_kernel, sizes),
        [(seqs * factor + n_core * seqs * n_near, cols)] * n_far,
        [
            pltpu.VMEM((n_far, n_core * seqs * n_near, cols), BF16),
            pltpu.VMEM(alignment.shape, BF16),
            pltpu.VMEM(opm_left.shape[::-1], BF16),
            pltpu.VMEM(opm_right.shape[::-1], BF16),
            pltpu.VMEM((cols, n_core * rows * factor), BF16),
            pltpu.VMEM((seqs, n_far * seqs * n_near, cols), BF16),
            pltpu.SemaphoreType.DMA((2 + seqs,)),
        ],
        8,
        4 * seqs * cols * width * factor,
        alignment,
        opm_left.T,
        opm_right.T,
        far_in=True,
    )


def whole_channels(
    pair,
    alignment,
    opm_left,
    opm_right,
    opm_out,
    tri_left,
    tri_left_gate,
    tri_right,
    tri_right_gate,
    tri_gate,
    tri_out,
):
    rows, cols, width = pair.shape
    seqs = alignment.shape[0]
    factor = opm_left.shape[1]
    hidden = tri_left.shape[1]
    n_row, n_seq = lax.axis_size("row"), lax.axis_size("seq")
    n_dev = n_row * n_seq
    n_core = 2
    n_far, n_near = n_row // 2, 2 * (n_seq // n_core)
    n_y = n_near // 2
    sizes = (n_far, n_near, n_core, rows, n_dev)
    held = n_far * seqs
    half = n_dev // 2
    per = hidden // half
    chips = half // n_core

    def exchange(value, row_bits, seq_bits):
        pairs = [
            (r * n_seq + s, (r ^ row_bits) * n_seq + (s ^ seq_bits))
            for r in range(n_row)
            for s in range(n_seq)
        ]
        return lax.ppermute(value, BOTH, pairs)

    mine = factors_call(sizes, alignment, opm_left, opm_right)
    weights = (
        pair,
        opm_out,
        tri_left_gate,
        tri_left,
        tri_right_gate,
        tri_right,
        tri_gate,
        tri_out,
    )
    mine, weights = lax.optimization_barrier((mine, weights))
    def to_near(value, k):
        return exchange(value, k // n_y, (k % n_y) * n_core)

    far = [exchange(mine[k], 2 * k, 0) for k in range(n_far - 1, 0, -1)]
    early = to_near(mine[0], n_near - 1)
    far = [mine[0], far[0], far[2], far[1]]
    prepared = call(
        functools.partial(prepare_kernel, factor),
        [
            (rows, width, cols),
            (width, factor * factor),
            (4 * hidden, width),
            (width, width),
            (width, hidden),
        ],
        [pltpu.VMEM(w.shape, BF16) for w in weights] + [pltpu.SemaphoreType.DMA((len(weights),))],
        8,
        4 * rows * cols * width * width,
        *weights,
        far_in=True,
    )
    early, far, prepared = lax.optimization_barrier((early, far, prepared))
    pair_t, out_t, tri_t, gate_t, final_t = prepared
    message = ((factor + n_core) * held, cols)
    late = ((n_far - 1) * seqs * factor + n_core * held, cols)
    mine = call(
        functools.partial(regroup_kernel, sizes, factor, seqs),
        [message] * (n_near - 1) + [late],
        [pltpu.VMEM((2, n_near, n_core * held, cols), BF16)],
        8,
        2 * 256 * factor * held * cols,
        *far,
    )
    near = [to_near(mine[k], k) for k in range(n_near - 1, 0, -1)]
    (near[0],) = call(
        functools.partial(merge_kernel, sizes, factor, seqs),
        [message],
        [],
        8,
        2 * 256 * factor * held * cols,
        early,
        near[0],
    )
    near = [mine[0]] + near
    groups = near + [exchange(block, 0, 1) for block in near]
    scale = 1.0 / (held * n_near * n_core)
    send, left, mid, normed = call(
        functools.partial(pair_kernel, sizes, held, scale),
        [
            (2 * hidden * rows, cols),
            (hidden * rows, cols),
            (rows, width, cols),
            (rows, width, cols),
        ],
        [
            pltpu.VMEM((rows, factor * factor, cols), BF16),
            pltpu.VMEM((2, rows, hidden, cols), BF16),
            pltpu.VMEM((hidden * rows, cols), BF16),
            pltpu.SemaphoreType.DMA((hidden * rows // 256,)),
        ],
        16,
        4 * rows * cols * width * (factor * factor + hidden * 2),
        *groups,
        pair_t,
        out_t,
        tri_t,
        far_out=(True, False, False, False),
    )
    recv = lax.all_to_all(send, BOTH, split_axis=0, concat_axis=0, tiled=True)
    mine = call(
        functools.partial(left_kernel, sizes),
        [(n_core * per * rows, cols)] * chips,
        [],
        8,
        0,
        left,
        exchange(left, 0, 1),
    )
    lefts = [mine[0]]
    for k in range(1, chips):
        lefts.append(exchange(mine[k], k // n_y, k % n_y * n_core))
    (send,) = call(
        functools.partial(product_kernel, sizes, per),
        [(hidden * rows, cols)],
        [
            pltpu.VMEM((per, rows * half, cols), BF16),
            pltpu.VMEM((per, rows * n_dev, cols), F32),
            pltpu.VMEM((half, per * rows, cols), F32),
        ],
        16,
        2 * per * cols * cols * cols // 2,
        recv,
        *lefts,
    )
    halves = [list(range(half)), list(range(half, n_dev))]
    recv = lax.all_to_all(
        send, BOTH, split_axis=0, concat_axis=0, tiled=True, axis_index_groups=halves
    )
    (out,) = call(
        functools.partial(finish_kernel, sizes),
        [(rows, cols, width)],
        [
            pltpu.VMEM((rows, hidden, cols), BF16),
            pltpu.VMEM((rows, cols, width), BF16),
            pltpu.SemaphoreType.DMA((rows,)),
        ],
        16,
        4 * rows * cols * width * hidden,
        recv,
        mid,
        normed,
        gate_t,
        final_t,
        far_out=True,
    )
    return out


def power_of_two(n):
    return n & (n - 1) == 0


def on_device(pair, alignment, opm_left, *rest):
    rows, cols, width = pair.shape
    factor, hidden = opm_left.shape[1], rest[2].shape[1]
    n_row, n_col, n_seq = (lax.axis_size(a) for a in ("row", "col", "seq"))
    n_dev = n_row * n_seq
    held = n_row // 2 * alignment.shape[0]
    fits = (
        n_col == 1
        and power_of_two(n_row)
        and power_of_two(n_seq)
        and power_of_two(rows)
        and n_row >= 4
        and n_seq >= 4
        and hidden % n_dev == 0
        and hidden == width
        and factor % 16 == 0
        and rows % 8 == 0
        and (hidden // n_dev * rows) % 16 == 0
        and cols % 256 == 0
        and rows * factor == cols
        and rows * n_dev == cols
        and held % 16 == 0
        and 256 % held == 0
        and factor % (256 // held) == 0
        and hidden % (256 // rows) == 0
        and power_of_two(held * n_seq * 2)
    )
    plan = whole_channels if fits else by_groups
    return plan(pair, alignment, opm_left, *rest)


def solution(mesh):
    return jax.shard_map(
        on_device,
        mesh=mesh,
        in_specs=(
            P(("row", "seq"), "col", None),
            P(("row", "seq"), "col", None),
            P(),
            P(),
            P(),
            P(),
            P(),
            P(),
            P(),
            P(),
            P(),
        ),
        out_specs=P(("row", "seq"), "col", None),
        check_vma=False,
    )
```
